256 devices in a mesh: ctx: 16 (over y_lo, x, core), tp: 16 (over z, y_hi).
Axes of the slice: x: 4, y: 4 (y_hi: 2, y_lo: 2; y = y_hi * 2 + y_lo), z: 8, core: 2. Of those that a mesh axis runs over, the one named last changes fastest.
Arguments:
- hidden: bfloat16 [16384, 8192], P('ctx', 'tp'), may hold values from -20 to 20
- norm_gain: bfloat16 [8192], P('tp'), may hold values from 0.5 to 1.5
- router_weight: bfloat16 [8192], P('tp'), may hold values from -0.0625 to 0.0625
- query_weight: bfloat16 [8192, 4096], P('tp'), may hold values from -29 to 29
- key_value_weight: bfloat16 [2, 8192, 512], P(None, 'tp'), may hold values from -1 to 1
- out_weight: bfloat16 [4096, 8192], P(None, 'tp'), may hold values from -0.5 to 0.5
- kept_rows: int32 [16, 512], replicated, may hold values from 0 to 1024, as said below
Outputs:
- block_update: bfloat16 [16384, 8192], P('ctx', 'tp')
The draws below stay inside these ranges and needn't reach their ends.
Inputs may be any that keep to these rules, and one draw needn't show every extreme that they name: `kept_rows`: row c lists, in rising order, the distinct local indices of the kept rows of context shard c, then 1024 in every unused slot. The counts of kept rows over all shards sum to 4096; every shard keeps at least one row and some shard keeps exactly 512.
All inputs are finite; a program needn't handle non-finite values.
Results may differ from the reference program's by a relative error of at most 0.025.
Values may be sent and summed in bfloat16 or wider, within the bound.
No kernel may reach another device: no remote copies, remote signals or barrier semaphores. Data moves between devices by JAX's collectives and lax.ppermute only.
A program may use at most 128 MiB of HBM per device.

```python
import jax
import jax.numpy as jnp
from jax import lax

D = 8192
H = 32
KVH = 4
HD = 128
TOK_DEV = 1024
KEEP_DEV = 256
CAP = 512
TOKENS = 16384
KEPT = 4096
N_CTX = 16


def shared_keys(key, bound):
    base = jax.random.normal(key, (D, KVH * HD), jnp.float32)
    return jnp.clip(base, -bound, bound) * D ** (-0.5)


def draw_hidden(key, part):
    key = jax.random.fold_in(key, 21)
    states = jnp.clip(jax.random.normal(key, (TOKENS, D), jnp.float32), -6.0, 6.0)
    return states.astype(jnp.bfloat16)


def draw_query_weight(key, part):
    key = jax.random.fold_in(key, 31)
    key_free = jax.random.fold_in(key, 0)
    weights = jnp.clip(jax.random.normal(key_free, (D, H * HD), jnp.float32), -4.0, 4.0) * D ** (-0.5)
    return weights.astype(jnp.bfloat16)


def draw_key_value_weight(key, part):
    key_weights = shared_keys(key, 4.0)
    key = jax.random.fold_in(key, 41)
    value_weights = jnp.clip(jax.random.normal(key, (D, KVH * HD), jnp.float32), -4.0, 4.0) * D ** (-0.5)
    return jnp.stack([key_weights, value_weights]).astype(jnp.bfloat16)


def draw_kept_rows(key, part):
    key = jax.random.fold_in(key, 11)
    key_weights, key_full, key_rows = jax.random.split(key, 3)
    shard_ids = jnp.arange(N_CTX, dtype=jnp.int32)
    shares = jax.random.randint(key_weights, (N_CTX,), 2, 5, dtype=jnp.int32)
    full_shard = jax.random.randint(key_full, (), 0, N_CTX, dtype=jnp.int32)
    others = jnp.where(shard_ids == full_shard, 0, shares)
    remaining = KEEP_DEV * N_CTX - CAP
    counts_base = remaining * others // jnp.sum(others)
    shortfall = remaining - jnp.sum(counts_base)
    others_rank = jnp.cumsum((others > 0).astype(jnp.int32)) - 1
    counts_base = counts_base + ((others > 0) & (others_rank < shortfall)).astype(jnp.int32)
    counts = jnp.where(shard_ids == full_shard, CAP, counts_base).astype(jnp.int32)

    def choose_rows(row_key, row_count):
        shuffled = jax.random.permutation(row_key, TOK_DEV).astype(jnp.int32)
        keep_flag = (shuffled < row_count).astype(jnp.int32)
        selected = jnp.argsort(1 - keep_flag, stable=True)[:CAP].astype(jnp.int32)
        return jnp.where(jnp.arange(CAP, dtype=jnp.int32) < row_count, selected, TOK_DEV).astype(jnp.int32)
    return jax.vmap(choose_rows)(jax.random.split(key_rows, N_CTX), counts)


def block_levels(key, shape, cuts, least, high):
    factor_of = 1.0
    for axis_at, blocks in cuts:
        steps = jax.random.uniform(jax.random.fold_in(jax.random.fold_in(key, 6), axis_at), (blocks,), jnp.float32, least / len(cuts), high / len(cuts))
        factor_of = factor_of * jnp.repeat(jnp.exp(steps), shape[axis_at] // blocks).reshape((-1,) + (1,) * (len(shape) - 1 - axis_at))
    return factor_of


def centred(stream_key, dims, width, limit, pieces=(), kind=jnp.bfloat16):
    entries = jax.random.normal(stream_key, dims, jnp.float32) * width
    if len(pieces) > 0:
        entries = block_levels(stream_key, dims, pieces, -0.22, 0.18) * entries
    return jnp.clip(entries, min=-limit, max=limit).astype(kind)


def setup_inputs(seed: int = 0) -> dict:
    seeds = jax.random.split(jax.random.key(seed), 8)
    hidden = draw_hidden(jax.random.fold_in(seeds[7], 71), 0)
    norm_gain = jnp.clip(1.0 + 0.1 * jax.random.normal(seeds[1], (D,), jnp.float32), 0.5, 1.5).astype(jnp.bfloat16)
    router_weight = centred(seeds[2], (D,), D ** -0.5, 0.0625, ((0, 16),))
    query_weight = draw_query_weight(jax.random.fold_in(seeds[7], 71), 0)
    key_value_weight = draw_key_value_weight(jax.random.fold_in(seeds[7], 71), 0)
    out_weight = centred(seeds[5], (H * HD, D), HD ** -0.5, 0.5, ((1, 16),))
    kept_rows = draw_kept_rows(jax.random.fold_in(seeds[7], 71), 0)
    return dict(hidden=hidden, norm_gain=norm_gain, router_weight=router_weight, query_weight=query_weight, key_value_weight=key_value_weight, out_weight=out_weight, kept_rows=kept_rows)


EPSILON = 1e-05
MASKED_SCORE = -1e+30

def reference(hidden, norm_gain, router_weight, query_weight, key_value_weight, out_weight, kept_rows):
    shard_ids = jnp.arange(N_CTX, dtype=jnp.int32)[:, None]
    flat_positions = jnp.where(kept_rows < TOK_DEV, shard_ids * TOK_DEV + kept_rows, TOKENS).reshape(-1)
    positions = jnp.sort(flat_positions)[:KEPT].astype(jnp.int32)
    kept_states = hidden[positions]
    widened = kept_states.astype(jnp.float32)
    square_sum = lax.optimization_barrier(jnp.sum(widened * widened, axis=1))
    router_logit = jnp.dot(kept_states, router_weight, preferred_element_type=jnp.float32)
    normed = (widened * norm_gain.astype(jnp.float32)).astype(jnp.bfloat16)
    inverse_rms = lax.rsqrt(square_sum / D + EPSILON)
    queries = (jnp.dot(normed, query_weight, preferred_element_type=jnp.float32) * inverse_rms[:, None]).astype(jnp.bfloat16)
    keys = (jnp.dot(normed, key_value_weight[0], preferred_element_type=jnp.float32) * inverse_rms[:, None]).astype(jnp.bfloat16)
    values = (jnp.dot(normed, key_value_weight[1], preferred_element_type=jnp.float32) * inverse_rms[:, None]).astype(jnp.bfloat16)
    queries = queries.reshape(KEPT, H, HD)
    keys = keys.reshape(KEPT, KVH, HD)
    values = values.reshape(KEPT, KVH, HD)
    allowed = positions[None, :] <= positions[:, None]
    score_scale = HD ** (-0.5)

    def one_head(head_id):
        group_id = head_id // (H // KVH)
        query_head = lax.dynamic_index_in_dim(queries, head_id, 1, keepdims=False)
        key_head = lax.dynamic_index_in_dim(keys, group_id, 1, keepdims=False)
        value_head = lax.dynamic_index_in_dim(values, group_id, 1, keepdims=False)
        scores = jnp.dot(query_head, key_head.T, preferred_element_type=jnp.float32) * score_scale
        scores = jnp.where(allowed, scores, MASKED_SCORE)
        peak = lax.optimization_barrier(jnp.max(scores, axis=1, keepdims=True))
        weights = jnp.where(allowed, jnp.exp(scores - peak), 0.0)
        total = lax.optimization_barrier(jnp.sum(weights, axis=1))
        mixed = jnp.dot(weights.astype(jnp.bfloat16), value_head, preferred_element_type=jnp.float32)
        return (mixed / total[:, None]).astype(jnp.bfloat16)
    head_output = lax.map(one_head, jnp.arange(H, dtype=jnp.int32))
    head_output = jnp.transpose(head_output, (1, 0, 2)).reshape(KEPT, H * HD)
    projected = jnp.dot(head_output, out_weight, preferred_element_type=jnp.float32)
    row_update = (jax.nn.sigmoid(router_logit)[:, None] * projected).astype(jnp.bfloat16)
    return jnp.zeros_like(hidden).at[positions].set(row_update)
```

```python
import functools

import jax
import jax.numpy as jnp
from jax import lax
from jax.experimental import pallas as pl
from jax.experimental.pallas import tpu as pltpu
from jax.sharding import PartitionSpec as P

D = 8192
H = 32
KVH = 4
HD = 128
ZN = 8
EPSILON = 1e-05
MASKED_SCORE = -1e30
EXP_SCALE = HD ** (-0.5) * 1.4426950408889634
KEY_BLOCK = 256


def z_shift(dz):
    return [(z * 2 + y, ((z + dz) % ZN) * 2 + y) for z in range(ZN) for y in range(2)]


def y_swap():
    return [(t, t ^ 1) for t in range(2 * ZN)]


def core_swap(count):
    return [(c, c ^ 1) for c in range(count)]


def quad_shift(k):
    def target(z):
        return (z // 4) * 4 + (z % 4 + k) % 4

    return [(z * 2 + y, target(z) * 2 + y) for z in range(ZN) for y in range(2)]


def attention_kernel(info_ref, q_ref, kv_ref, o_ref, qt_ref, peak_ref, total_ref, acc_ref):
    shard = pl.program_id(0)
    rows = q_ref.shape[0]
    own = info_ref[pl.num_programs(0)]
    count = info_ref[shard]

    @pl.when(shard == 0)
    def _():
        for head in range(2):
            qt_ref[:, head * rows : (head + 1) * rows] = (
                q_ref[:, head * HD : (head + 1) * HD].astype(jnp.float32).T.astype(jnp.bfloat16)
            )
        peak_ref[...] = jnp.full_like(peak_ref, MASKED_SCORE)
        total_ref[...] = jnp.zeros_like(total_ref)
        acc_ref[...] = jnp.zeros_like(acc_ref)

    for sub in range(rows // KEY_BLOCK):
        start = sub * KEY_BLOCK

        @pl.when((shard <= own) & (start < count))
        def _():
            keys = kv_ref[0, :HD, start : start + KEY_BLOCK]
            values = kv_ref[0, HD:, start : start + KEY_BLOCK]
            scores = lax.dot_general(
                keys, qt_ref[...], (((0,), (0,)), ((), ())), preferred_element_type=jnp.float32
            )
            slot = lax.broadcasted_iota(jnp.int32, (1, 2 * rows), 1) % rows
            limit = jnp.where(shard < own, count, jnp.minimum(count, slot + 1)) - start
            key_slot = lax.broadcasted_iota(jnp.int32, scores.shape, 0)
            scores = jnp.where(key_slot < limit, scores, MASKED_SCORE)
            peak = peak_ref[...]
            new_peak = jnp.maximum(peak, jnp.max(scores, axis=0, keepdims=True))
            weights = jnp.exp2((scores - new_peak) * EXP_SCALE)
            rescale = jnp.exp2((peak - new_peak) * EXP_SCALE)
            total_ref[...] = total_ref[...] * rescale + jnp.sum(weights, axis=0, keepdims=True)
            acc_ref[...] = acc_ref[...] * rescale + jnp.dot(
                values, weights.astype(jnp.bfloat16), preferred_element_type=jnp.float32
            )
            peak_ref[...] = new_peak

    @pl.when(shard == pl.num_programs(0) - 1)
    def _():
        mixed = acc_ref[...] / total_ref[...]
        for head in range(2):
            o_ref[:, head * HD : (head + 1) * HD] = mixed[:, head * rows : (head + 1) * rows].T.astype(
                jnp.bfloat16
            )


def attention(info, queries, kv):
    shards_n, _, rows = kv.shape
    return pl.pallas_call(
        attention_kernel,
        out_shape=jax.ShapeDtypeStruct(queries.shape, jnp.bfloat16),
        grid_spec=pltpu.PrefetchScalarGridSpec(
            num_scalar_prefetch=1,
            grid=(shards_n,),
            in_specs=[
                pl.BlockSpec(queries.shape, lambda s, info: (0, 0)),
                pl.BlockSpec((1, 2 * HD, rows), lambda s, info: (jnp.minimum(s, info[shards_n]), 0, 0)),
            ],
            out_specs=pl.BlockSpec(queries.shape, lambda s, info: (0, 0)),
            scratch_shapes=[
                pltpu.VMEM((HD, 2 * rows), jnp.bfloat16),
                pltpu.VMEM((1, 2 * rows), jnp.float32),
                pltpu.VMEM((1, 2 * rows), jnp.float32),
                pltpu.VMEM((HD, 2 * rows), jnp.float32),
            ],
        ),
        compiler_params=pltpu.CompilerParams(vmem_limit_bytes=32 * 1024 * 1024),
        cost_estimate=pl.CostEstimate(
            flops=4 * 2 * rows * HD * shards_n * rows, bytes_accessed=kv.size * 2, transcendentals=rows * rows * shards_n
        ),
    )(info, queries, kv)


def dot(a, b):
    return jnp.dot(a, b, preferred_element_type=jnp.float32)


def shards(hidden, norm_gain, router_weight, query_weight, key_value_weight, out_weight, kept_rows):
    bf16 = jnp.bfloat16
    shard = lax.axis_index("ctx")
    tp = lax.axis_index("tp")
    shard_n = lax.axis_size("ctx")
    z, y, core = tp // 2, tp % 2, shard % 2
    tokens, width = hidden.shape
    rows = kept_rows.shape[1]
    half_cols = query_weight.shape[1] // 2
    chunk = half_cols // ZN

    def fetch(block, axis):
        got = lax.ppermute(block, "tp", y_swap())
        other = lax.ppermute(got, "ctx", core_swap(shard_n))
        low = jnp.where(core == 0, got, other)
        high = jnp.where(core == 0, other, got)
        return jnp.concatenate([low, high], axis=axis)

    wq_in = fetch(
        lax.dynamic_slice(query_weight, (core * (width // 2), (1 - y) * half_cols), (width // 2, half_cols)), 0
    )
    wo_rows = out_weight.shape[0] // 2
    wo_in = fetch(
        lax.dynamic_slice(out_weight, ((1 - y) * wo_rows + core * (wo_rows // 2), 0), (wo_rows // 2, width)), 0
    )

    own_rows = lax.dynamic_index_in_dim(kept_rows, shard, 0, keepdims=False)
    select = (own_rows[:, None] == jnp.arange(tokens, dtype=jnp.int32)[None, :]).astype(bf16)
    kept = dot(select, hidden)
    square_part = jnp.sum(kept * kept, axis=1)
    router_part = jnp.sum(kept * router_weight.astype(jnp.float32)[None, :], axis=1)
    x_own = (kept * norm_gain.astype(jnp.float32)[None, :]).astype(bf16)
    x_in = lax.ppermute(x_own, "tp", y_swap())

    kv_part = lax.dot_general(
        key_value_weight, x_own, (((1,), (1,)), ((), ())), preferred_element_type=jnp.float32
    ).astype(bf16)
    kv_part = (
        kv_part.reshape(2, 2, 2, 2, HD // 2, rows).transpose(2, 0, 3, 1, 4, 5).reshape(2 * ZN, HD // 2, rows)
    )
    stats = jnp.stack([square_part, router_part])
    stats_high = lax.reduce_precision(stats, 8, 7)
    stats_low = stats - stats_high
    stats_rows = jnp.concatenate([stats_high, stats_low, jnp.zeros((4, rows), jnp.float32)]).astype(bf16)
    sent = jnp.concatenate([kv_part, jnp.broadcast_to(stats_rows[None], (2 * ZN, 8, rows))], axis=1)
    summed = jnp.sum(lax.all_to_all(sent, "tp", 0, 0, tiled=True).astype(jnp.float32), axis=0)
    square_sum = summed[HD // 2] + summed[HD // 2 + 2]
    router_logit = summed[HD // 2 + 1] + summed[HD // 2 + 3]
    inverse_rms = lax.rsqrt(square_sum / D + EPSILON)
    piece = (summed[: HD // 2] * inverse_rms[None, :]).astype(bf16)
    pieces = [lax.ppermute(piece, "tp", quad_shift(k)) for k in (3, 2, 1)] + [piece]
    ordered = jnp.stack(pieces + pieces[:3])
    kv_own = lax.dynamic_slice_in_dim(ordered, (3 - z % 4) % 4, 4, 0).reshape(2 * HD, rows)
    kv_all = lax.all_gather(kv_own, "ctx", axis=0, tiled=False)

    def query_part(offset):
        d = (z + offset) % ZN
        own_w = lax.dynamic_slice(query_weight, (0, y * half_cols + d * chunk), (width, chunk))
        in_w = lax.dynamic_slice(wq_in, (0, d * chunk), (width, chunk))
        return dot(x_own, own_w) + dot(x_in, in_w)

    def right(a):
        return lax.ppermute(a.astype(bf16), "tp", z_shift(1))

    def left(a):
        return lax.ppermute(a.astype(bf16), "tp", z_shift(-1))

    cut = chunk // 2
    far = query_part(4)
    going_right, going_left = right(far[:, :cut]), left(far[:, cut:])
    part = query_part(3)
    going_right = right(jnp.concatenate([part[:, :cut] + going_right, part[:, cut:]], axis=1))
    part = query_part(-3)
    going_left = left(jnp.concatenate([part[:, :cut], part[:, cut:] + going_left], axis=1))
    for step in (2, 1):
        going_right = right(query_part(step) + going_right)
        going_left = left(query_part(-step) + going_left)
    queries = (query_part(0) + going_right + going_left) * inverse_rms[:, None]

    counts = jnp.sum((kept_rows < tokens).astype(jnp.int32), axis=1)
    info = jnp.concatenate([counts, shard[None].astype(jnp.int32)])
    mixed = attention(info, queries.astype(bf16), kv_all)

    def project(piece, offset, low, high):
        start = ((z + offset) % ZN) * chunk + low
        own_w = lax.dynamic_slice(out_weight, (y * wo_rows + start, 0), (high - low, width))
        in_w = lax.dynamic_slice(wo_in, (start, 0), (high - low, width))
        return dot(piece, own_w), dot(piece, in_w)

    terms = [project(mixed, 0, 0, chunk)]
    from_left, from_right = mixed, mixed
    for step in (1, 2, 3):
        from_left, from_right = right(from_left), left(from_right)
        terms.append(project(from_left, -step, 0, chunk))
        terms.append(project(from_right, step, 0, chunk))
    terms.append(project(right(from_left[:, :cut]), 4, 0, cut))
    terms.append(project(left(from_right[:, cut:]), 4, cut, chunk))
    for_partner = functools.reduce(jnp.add, [t[1] for t in terms])
    received = lax.ppermute(for_partner.astype(bf16), "tp", y_swap())
    projected = functools.reduce(jnp.add, [t[0] for t in terms]) + received
    row_update = (jax.nn.sigmoid(router_logit)[:, None] * projected).astype(bf16)
    return lax.dot_general(select, row_update, (((0,), (0,)), ((), ())), preferred_element_type=jnp.float32).astype(
        bf16
    )


def solution(mesh):
    return jax.shard_map(
        shards,
        mesh=mesh,
        in_specs=(
            P("ctx", "tp"),
            P("tp"),
            P("tp"),
            P("tp", None),
            P(None, "tp", None),
            P(None, "tp"),
            P(),
        ),
        out_specs=P("ctx", "tp"),
        check_vma=False,
    )
```

```python
import functools

import jax
import jax.numpy as jnp
from jax import lax
from jax.experimental import pallas as pl
from jax.experimental.pallas import tpu as pltpu
from jax.sharding import PartitionSpec as P

D = 8192
H = 32
KVH = 4
HD = 128
ZN = 8
EPSILON = 1e-05
MASKED_SCORE = -1e30
EXP_SCALE = HD ** (-0.5) * 1.4426950408889634
KEY_BLOCK = 256
ROW_TILE = 128
TILES_AT_ONCE = 2


def z_shift(dz):
    return [(z * 2 + y, ((z + dz) % ZN) * 2 + y) for z in range(ZN) for y in range(2)]


def y_swap():
    return [(t, t ^ 1) for t in range(2 * ZN)]


def core_swap(count):
    return [(c, c ^ 1) for c in range(count)]


def quad_shift(k):
    def target(z):
        return (z // 4) * 4 + (z % 4 + k) % 4

    return [(z * 2 + y, target(z) * 2 + y) for z in range(ZN) for y in range(2)]


def attention_kernel(info_ref, q_ref, kv_ref, o_ref, qt_ref, peak_ref, total_ref, acc_ref):
    shard = pl.program_id(0)
    rows = q_ref.shape[0]
    own = info_ref[pl.num_programs(0)]
    count = info_ref[shard]
    own_count = info_ref[own]
    tiles = rows // ROW_TILE
    lanes = 2 * ROW_TILE

    @pl.when(shard == 0)
    def _():
        for tile in range(tiles):
            for head in range(2):
                block = q_ref[tile * ROW_TILE : (tile + 1) * ROW_TILE, head * HD : (head + 1) * HD]
                qt_ref[tile, :, head * ROW_TILE : (head + 1) * ROW_TILE] = (
                    block.astype(jnp.float32).T.astype(jnp.bfloat16)
                )
        peak_ref[...] = jnp.full_like(peak_ref, MASKED_SCORE)
        total_ref[...] = jnp.zeros_like(total_ref)
        acc_ref[...] = jnp.zeros_like(acc_ref)

    def update(tile, start, masked):
        keys = kv_ref[0, :HD, start : start + KEY_BLOCK]
        values = kv_ref[0, HD:, start : start + KEY_BLOCK]
        scores = lax.dot_general(
            keys, qt_ref[tile], (((0,), (0,)), ((), ())), preferred_element_type=jnp.float32
        )
        if masked:
            slot = tile * ROW_TILE + lax.broadcasted_iota(jnp.int32, (1, lanes), 1) % ROW_TILE
            limit = jnp.where(shard < own, count, jnp.minimum(count, slot + 1)) - start
            key_slot = lax.broadcasted_iota(jnp.int32, scores.shape, 0)
            scores = jnp.where(key_slot < limit, scores, MASKED_SCORE)
        peak = peak_ref[tile]
        new_peak = jnp.maximum(peak, jnp.max(scores, axis=0, keepdims=True))
        weights = jnp.exp2(scores - new_peak)
        rescale = jnp.exp2(peak - new_peak)
        total_ref[tile] = total_ref[tile] * rescale + jnp.sum(weights, axis=0, keepdims=True)
        acc_ref[tile] = acc_ref[tile] * rescale + jnp.dot(
            values, weights.astype(jnp.bfloat16), preferred_element_type=jnp.float32
        )
        peak_ref[tile] = new_peak

    for start in range(0, rows, KEY_BLOCK):
        whole = (shard < own) & (start + KEY_BLOCK <= count)
        some = (shard <= own) & (start < count) & jnp.logical_not(whole)
        for pair in range(tiles // TILES_AT_ONCE):
            first = pair * TILES_AT_ONCE
            used = first * ROW_TILE < own_count
            reached = (shard < own) | ((first + TILES_AT_ONCE) * ROW_TILE > start)

            @pl.when(whole & used)
            def _():
                for tile in range(first, first + TILES_AT_ONCE):
                    update(tile, start, False)

            @pl.when(some & used & reached)
            def _():
                for tile in range(first, first + TILES_AT_ONCE):
                    update(tile, start, True)

    @pl.when(shard == pl.num_programs(0) - 1)
    def _():
        for tile in range(tiles):
            total = total_ref[tile]
            mixed = acc_ref[tile] / jnp.where(total > 0.0, total, 1.0)
            for head in range(2):
                o_ref[tile * ROW_TILE : (tile + 1) * ROW_TILE, head * HD : (head + 1) * HD] = mixed[
                    :, head * ROW_TILE : (head + 1) * ROW_TILE
                ].T.astype(jnp.bfloat16)


def attention(info, queries, kv):
    shards_n, _, rows = kv.shape
    tiles, lanes = rows // ROW_TILE, 2 * ROW_TILE
    return pl.pallas_call(
        attention_kernel,
        out_shape=jax.ShapeDtypeStruct(queries.shape, jnp.bfloat16),
        grid_spec=pltpu.PrefetchScalarGridSpec(
            num_scalar_prefetch=1,
            grid=(shards_n,),
            in_specs=[
                pl.BlockSpec(queries.shape, lambda s, info: (0, 0)),
                pl.BlockSpec((1, 2 * HD, rows), lambda s, info: (jnp.minimum(s, info[shards_n]), 0, 0)),
            ],
            out_specs=pl.BlockSpec(queries.shape, lambda s, info: (0, 0)),
            scratch_shapes=[
                pltpu.VMEM((tiles, HD, lanes), jnp.bfloat16),
                pltpu.VMEM((tiles, 1, lanes), jnp.float32),
                pltpu.VMEM((tiles, 1, lanes), jnp.float32),
                pltpu.VMEM((tiles, HD, lanes), jnp.float32),
            ],
        ),
        compiler_params=pltpu.CompilerParams(vmem_limit_bytes=32 * 1024 * 1024),
        cost_estimate=pl.CostEstimate(
            flops=4 * 2 * rows * HD * shards_n * rows, bytes_accessed=kv.size * 2, transcendentals=rows * rows * shards_n
        ),
    )(info, queries, kv)


def dot(a, b):
    return jnp.dot(a, b, preferred_element_type=jnp.float32)


def shards(hidden, norm_gain, router_weight, query_weight, key_value_weight, out_weight, kept_rows):
    bf16 = jnp.bfloat16
    shard = lax.axis_index("ctx")
    tp = lax.axis_index("tp")
    shard_n = lax.axis_size("ctx")
    z, y, core = tp // 2, tp % 2, shard % 2
    tokens, width = hidden.shape
    rows = kept_rows.shape[1]
    half_cols = query_weight.shape[1] // 2
    chunk = half_cols // ZN

    def merge(got, axis):
        other = lax.ppermute(got, "ctx", core_swap(shard_n))
        low = jnp.where(core == 0, got, other)
        high = jnp.where(core == 0, other, got)
        return jnp.concatenate([low, high], axis=axis)

    wq_got = lax.ppermute(
        lax.dynamic_slice(query_weight, (core * (width // 2), (1 - y) * half_cols), (width // 2, half_cols)),
        "tp",
        y_swap(),
    )

    own_rows = lax.dynamic_index_in_dim(kept_rows, shard, 0, keepdims=False)
    select = (own_rows[:, None] == jnp.arange(tokens, dtype=jnp.int32)[None, :]).astype(bf16)
    kept = dot(select, hidden)
    square_part = jnp.sum(kept * kept, axis=1)
    router_part = jnp.sum(kept * router_weight.astype(jnp.float32)[None, :], axis=1)
    x_own = (kept * norm_gain.astype(jnp.float32)[None, :]).astype(bf16)
    x_in = lax.ppermute(x_own, "tp", y_swap())

    kv_part = lax.dot_general(
        key_value_weight, x_own, (((1,), (1,)), ((), ())), preferred_element_type=jnp.float32
    ).astype(bf16)
    kv_part = (
        kv_part.reshape(2, 2, 2, 2, HD // 2, rows).transpose(2, 0, 3, 1, 4, 5).reshape(2 * ZN, HD // 2, rows)
    )
    stats = jnp.stack([square_part, router_part])
    stats_high = lax.reduce_precision(stats, 8, 7)
    stats_low = stats - stats_high
    stats_rows = jnp.concatenate([stats_high, stats_low, jnp.zeros((4, rows), jnp.float32)]).astype(bf16)
    sent = jnp.concatenate([kv_part, jnp.broadcast_to(stats_rows[None], (2 * ZN, 8, rows))], axis=1)
    summed = jnp.sum(lax.all_to_all(sent, "tp", 0, 0, tiled=True).astype(jnp.float32), axis=0)
    square_sum = summed[HD // 2] + summed[HD // 2 + 2]
    router_logit = summed[HD // 2 + 1] + summed[HD // 2 + 3]
    inverse_rms = lax.rsqrt(square_sum / D + EPSILON)
    piece = (summed[: HD // 2] * inverse_rms[None, :]).astype(bf16)
    piece, wq_got, x_in = lax.optimization_barrier((piece, wq_got, x_in))
    wq_in = merge(wq_got, 0)
    pieces = [lax.ppermute(piece, "tp", quad_shift(k)) for k in (3, 2, 1)] + [piece]
    ordered = jnp.stack(pieces + pieces[:3])
    kv_own = lax.dynamic_slice_in_dim(ordered, (3 - z % 4) % 4, 4, 0).reshape(2 * HD, rows)
    kv_all = lax.all_gather(kv_own, "ctx", axis=0, tiled=False)

    def query_part(offset):
        d = (z + offset) % ZN
        own_w = lax.dynamic_slice(query_weight, (0, y * half_cols + d * chunk), (width, chunk))
        in_w = lax.dynamic_slice(wq_in, (0, d * chunk), (width, chunk))
        return dot(x_own, own_w) + dot(x_in, in_w)

    def right(a):
        return lax.ppermute(a.astype(bf16), "tp", z_shift(1))

    def left(a):
        return lax.ppermute(a.astype(bf16), "tp", z_shift(-1))

    cut = chunk // 2
    far = query_part(4)
    going_right, going_left = right(far[:, :cut]), left(far[:, cut:])
    part = query_part(3)
    going_right = right(jnp.concatenate([part[:, :cut] + going_right, part[:, cut:]], axis=1))
    part = query_part(-3)
    going_left = left(jnp.concatenate([part[:, :cut], part[:, cut:] + going_left], axis=1))
    for step in (2, 1):
        going_right = right(query_part(step) + going_right)
        going_left = left(query_part(-step) + going_left)
    wo_rows = out_weight.shape[0] // 2
    wo_start = (1 - y) * wo_rows + core * (wo_rows // 2)
    going_right, wo_start = lax.optimization_barrier((going_right, wo_start))
    wo_got = lax.ppermute(
        lax.dynamic_slice(out_weight, (wo_start, 0), (wo_rows // 2, width)), "tp", y_swap()
    )
    queries = (query_part(0) + going_right + going_left) * (inverse_rms * EXP_SCALE)[:, None]

    counts = jnp.sum((kept_rows < tokens).astype(jnp.int32), axis=1)
    info = jnp.concatenate([counts, shard[None].astype(jnp.int32)])
    mixed = attention(info, queries.astype(bf16), kv_all)
    mixed, wo_got = lax.optimization_barrier((mixed, wo_got))
    wo_in = merge(wo_got, 0)

    def project(piece, offset, low, high):
        start = ((z + offset) % ZN) * chunk + low
        own_w = lax.dynamic_slice(out_weight, (y * wo_rows + start, 0), (high - low, width))
        in_w = lax.dynamic_slice(wo_in, (start, 0), (high - low, width))
        return dot(piece, own_w), dot(piece, in_w)

    terms = [project(mixed, 0, 0, chunk)]
    from_left, from_right = mixed, mixed
    for step in (1, 2, 3):
        from_left, from_right = right(from_left), left(from_right)
        terms.append(project(from_left, -step, 0, chunk))
        terms.append(project(from_right, step, 0, chunk))
    terms.append(project(right(from_left[:, :cut]), 4, 0, cut))
    terms.append(project(left(from_right[:, cut:]), 4, cut, chunk))
    for_partner = functools.reduce(jnp.add, [t[1] for t in terms])
    received = lax.ppermute(for_partner.astype(bf16), "tp", y_swap())
    projected = functools.reduce(jnp.add, [t[0] for t in terms]) + received
    row_update = (jax.nn.sigmoid(router_logit)[:, None] * projected).astype(bf16)
    return lax.dot_general(select, row_update, (((0,), (0,)), ((), ())), preferred_element_type=jnp.float32).astype(
        bf16
    )


def solution(mesh):
    return jax.shard_map(
        shards,
        mesh=mesh,
        in_specs=(
            P("ctx", "tp"),
            P("tp"),
            P("tp"),
            P("tp", None),
            P(None, "tp", None),
            P(None, "tp"),
            P(),
        ),
        out_specs=P("ctx", "tp"),
        check_vma=False,
    )
```

```python
import functools

import jax
import jax.numpy as jnp
from jax import lax
from jax.experimental import pallas as pl
from jax.experimental.pallas import tpu as pltpu
from jax.sharding import PartitionSpec as P

D = 8192
H = 32
KVH = 4
HD = 128
ZN = 8
EPSILON = 1e-05
MASKED_SCORE = -1e30
EXP_SCALE = HD ** (-0.5) * 1.4426950408889634
KEY_BLOCK = 256
ROW_TILE = 512
TILES_AT_ONCE = 1


def z_shift(dz):
    return [(z * 2 + y, ((z + dz) % ZN) * 2 + y) for z in range(ZN) for y in range(2)]


def y_swap():
    return [(t, t ^ 1) for t in range(2 * ZN)]


def quad_shift(k):
    def target(z):
        return (z // 4) * 4 + (z % 4 + k) % 4

    return [(z * 2 + y, target(z) * 2 + y) for z in range(ZN) for y in range(2)]


def attention_kernel(info_ref, q_ref, kv_ref, o_ref, qt_ref, peak_ref, total_ref, acc_ref):
    shard = pl.program_id(0)
    rows = q_ref.shape[0]
    own = info_ref[pl.num_programs(0)]
    count = info_ref[shard]
    own_count = info_ref[own]
    tiles = rows // ROW_TILE
    lanes = 2 * ROW_TILE

    @pl.when(shard == 0)
    def _():
        for tile in range(tiles):
            for head in range(2):
                block = q_ref[tile * ROW_TILE : (tile + 1) * ROW_TILE, head * HD : (head + 1) * HD]
                qt_ref[tile, :, head * ROW_TILE : (head + 1) * ROW_TILE] = (
                    block.astype(jnp.float32).T.astype(jnp.bfloat16)
                )
        peak_ref[...] = jnp.full_like(peak_ref, MASKED_SCORE)
        total_ref[...] = jnp.zeros_like(total_ref)
        acc_ref[...] = jnp.zeros_like(acc_ref)

    def update(tile, start, masked):
        keys = kv_ref[0, :HD, start : start + KEY_BLOCK]
        values = kv_ref[0, HD:, start : start + KEY_BLOCK]
        scores = lax.dot_general(
            keys, qt_ref[tile], (((0,), (0,)), ((), ())), preferred_element_type=jnp.float32
        )
        if masked:
            slot = tile * ROW_TILE + lax.broadcasted_iota(jnp.int32, (1, lanes), 1) % ROW_TILE
            limit = jnp.where(shard < own, count, jnp.minimum(count, slot + 1)) - start
            key_slot = lax.broadcasted_iota(jnp.int32, scores.shape, 0)
            scores = jnp.where(key_slot < limit, scores, MASKED_SCORE)
        peak = peak_ref[tile]
        new_peak = jnp.maximum(peak, jnp.max(scores, axis=0, keepdims=True))
        weights = jnp.exp2(scores - new_peak)
        rescale = jnp.exp2(peak - new_peak)
        total_ref[tile] = total_ref[tile] * rescale + jnp.sum(weights, axis=0, keepdims=True)
        acc_ref[tile] = acc_ref[tile] * rescale + jnp.dot(
            values, weights.astype(jnp.bfloat16), preferred_element_type=jnp.float32
        )
        peak_ref[tile] = new_peak

    for start in range(0, rows, KEY_BLOCK):
        whole = (shard < own) & (start + KEY_BLOCK <= count)
        some = (shard <= own) & (start < count) & jnp.logical_not(whole)
        for pair in range(tiles // TILES_AT_ONCE):
            first = pair * TILES_AT_ONCE
            used = first * ROW_TILE < own_count
            reached = (shard < own) | ((first + TILES_AT_ONCE) * ROW_TILE > start)

            @pl.when(whole & used)
            def _():
                for tile in range(first, first + TILES_AT_ONCE):
                    update(tile, start, False)

            @pl.when(some & used & reached)
            def _():
                for tile in range(first, first + TILES_AT_ONCE):
                    update(tile, start, True)

    @pl.when(shard == pl.num_programs(0) - 1)
    def _():
        for tile in range(tiles):
            total = total_ref[tile]
            mixed = acc_ref[tile] / jnp.where(total > 0.0, total, 1.0)
            for head in range(2):
                o_ref[tile * ROW_TILE : (tile + 1) * ROW_TILE, head * HD : (head + 1) * HD] = mixed[
                    :, head * ROW_TILE : (head + 1) * ROW_TILE
                ].T.astype(jnp.bfloat16)


def attention(info, queries, kv):
    shards_n, _, rows = kv.shape
    tiles, lanes = rows // ROW_TILE, 2 * ROW_TILE
    return pl.pallas_call(
        attention_kernel,
        out_shape=jax.ShapeDtypeStruct(queries.shape, jnp.bfloat16),
        grid_spec=pltpu.PrefetchScalarGridSpec(
            num_scalar_prefetch=1,
            grid=(shards_n,),
            in_specs=[
                pl.BlockSpec(queries.shape, lambda s, info: (0, 0)),
                pl.BlockSpec((1, 2 * HD, rows), lambda s, info: (jnp.minimum(s, info[shards_n]), 0, 0)),
            ],
            out_specs=pl.BlockSpec(queries.shape, lambda s, info: (0, 0)),
            scratch_shapes=[
                pltpu.VMEM((tiles, HD, lanes), jnp.bfloat16),
                pltpu.VMEM((tiles, 1, lanes), jnp.float32),
                pltpu.VMEM((tiles, 1, lanes), jnp.float32),
                pltpu.VMEM((tiles, HD, lanes), jnp.float32),
            ],
        ),
        compiler_params=pltpu.CompilerParams(vmem_limit_bytes=32 * 1024 * 1024),
        cost_estimate=pl.CostEstimate(
            flops=4 * 2 * rows * HD * shards_n * rows, bytes_accessed=kv.size * 2, transcendentals=rows * rows * shards_n
        ),
    )(info, queries, kv)


def dot(a, b):
    return jnp.dot(a, b, preferred_element_type=jnp.float32)


def shards(hidden, norm_gain, router_weight, query_weight, key_value_weight, out_weight, kept_rows):
    bf16 = jnp.bfloat16
    shard = lax.axis_index("ctx")
    tp = lax.axis_index("tp")
    shard_n = lax.axis_size("ctx")
    z, y = tp // 2, tp % 2
    tokens, width = hidden.shape
    rows = kept_rows.shape[1]
    half_cols = query_weight.shape[1] // 2
    chunk = half_cols // ZN

    group = 2 * ZN // 2
    groups = [list(range(g, g + group)) for g in range(0, shard_n, group)]
    mine = shard % group

    def share(got):
        return lax.all_gather(got, "ctx", axis=0, tiled=False, axis_index_groups=groups)

    wq_sent = lax.dynamic_slice(query_weight, (0, (1 - y) * half_cols + mine * chunk), (width, chunk))
    wq_got = lax.ppermute(wq_sent, "tp", y_swap())

    own_rows = lax.dynamic_index_in_dim(kept_rows, shard, 0, keepdims=False)
    select = (own_rows[:, None] == jnp.arange(tokens, dtype=jnp.int32)[None, :]).astype(bf16)
    kept = dot(select, hidden)
    square_part = jnp.sum(kept * kept, axis=1)
    router_part = jnp.sum(kept * router_weight.astype(jnp.float32)[None, :], axis=1)
    x_own = (kept * norm_gain.astype(jnp.float32)[None, :]).astype(bf16)
    x_in = lax.ppermute(x_own, "tp", y_swap())

    kv_part = lax.dot_general(
        key_value_weight, x_own, (((1,), (1,)), ((), ())), preferred_element_type=jnp.float32
    ).astype(bf16)
    kv_part = (
        kv_part.reshape(2, 2, 2, 2, HD // 2, rows).transpose(2, 0, 3, 1, 4, 5).reshape(2 * ZN, HD // 2, rows)
    )
    stats = jnp.stack([square_part, router_part])
    stats_high = lax.reduce_precision(stats, 8, 7)
    stats_low = stats - stats_high
    stats_rows = jnp.concatenate([stats_high, stats_low, jnp.zeros((4, rows), jnp.float32)]).astype(bf16)
    sent = jnp.concatenate([kv_part, jnp.broadcast_to(stats_rows[None], (2 * ZN, 8, rows))], axis=1)
    sent, wq_got = lax.optimization_barrier((sent, wq_got))
    wq_in = share(wq_got)
    own_weights = lax.dynamic_slice(query_weight, (0, y * half_cols), (width, half_cols))
    query_own = dot(x_own, own_weights)
    summed = jnp.sum(lax.all_to_all(sent, "tp", 0, 0, tiled=True).astype(jnp.float32), axis=0)
    square_sum = summed[HD // 2] + summed[HD // 2 + 2]
    router_logit = summed[HD // 2 + 1] + summed[HD // 2 + 3]
    inverse_rms = lax.rsqrt(square_sum / D + EPSILON)
    piece = (summed[: HD // 2] * inverse_rms[None, :]).astype(bf16)
    piece, wq_in, x_in, query_own = lax.optimization_barrier((piece, wq_in, x_in, query_own))
    pieces = [lax.ppermute(piece, "tp", quad_shift(k)) for k in (3, 2, 1)] + [piece]
    ordered = jnp.stack(pieces + pieces[:3])
    kv_own = lax.dynamic_slice_in_dim(ordered, (3 - z % 4) % 4, 4, 0).reshape(2 * HD, rows)
    kv_all = lax.all_gather(kv_own, "ctx", axis=0, tiled=False)

    def query_part(offset):
        d = (z + offset) % ZN
        own = lax.dynamic_slice(query_own, (0, d * chunk), (rows, chunk))
        return own + dot(x_in, lax.dynamic_index_in_dim(wq_in, d, 0, keepdims=False))

    def right(a):
        return lax.ppermute(a.astype(bf16), "tp", z_shift(1))

    def left(a):
        return lax.ppermute(a.astype(bf16), "tp", z_shift(-1))

    def both(going_right, going_left):
        return lax.optimization_barrier((right(going_right), left(going_left)))

    cut = chunk // 2
    far = query_part(4)
    going_right, going_left = both(far[:, :cut], far[:, cut:])
    part_right, part_left = query_part(3), query_part(-3)
    going_right, going_left = both(
        jnp.concatenate([part_right[:, :cut] + going_right, part_right[:, cut:]], axis=1),
        jnp.concatenate([part_left[:, :cut], part_left[:, cut:] + going_left], axis=1),
    )
    wo_rows = out_weight.shape[0] // 2
    wo_start = (1 - y) * wo_rows + mine * chunk
    going_right, wo_start = lax.optimization_barrier((going_right, wo_start))
    wo_got = lax.ppermute(
        lax.dynamic_slice(out_weight, (wo_start, 0), (chunk, width)), "tp", y_swap()
    )
    for step in (2, 1):
        going_right, going_left = both(query_part(step) + going_right, query_part(-step) + going_left)
    queries = (query_part(0) + going_right + going_left) * (inverse_rms * EXP_SCALE)[:, None]

    queries, wo_got = lax.optimization_barrier((queries.astype(bf16), wo_got))
    wo_in = share(wo_got).reshape(wo_rows, width)

    counts = jnp.sum((kept_rows < tokens).astype(jnp.int32), axis=1)
    info = jnp.concatenate([counts, shard[None].astype(jnp.int32)])
    mixed = attention(info, queries, kv_all)

    def project(piece, offset, low, high):
        start = ((z + offset) % ZN) * chunk + low
        own_w = lax.dynamic_slice(out_weight, (y * wo_rows + start, 0), (high - low, width))
        in_w = lax.dynamic_slice(wo_in, (start, 0), (high - low, width))
        return dot(piece, own_w), dot(piece, in_w)

    terms = [project(mixed, 0, 0, chunk)]
    from_left, from_right = mixed, mixed
    for step in (1, 2, 3):
        from_left, from_right = both(from_left, from_right)
        terms.append(project(from_left, -step, 0, chunk))
        terms.append(project(from_right, step, 0, chunk))
    terms.append(project(right(from_left[:, :cut]), 4, 0, cut))
    terms.append(project(left(from_right[:, cut:]), 4, cut, chunk))
    for_partner = functools.reduce(jnp.add, [t[1] for t in terms])
    received = lax.ppermute(for_partner.astype(bf16), "tp", y_swap())
    projected = functools.reduce(jnp.add, [t[0] for t in terms]) + received
    row_update = (jax.nn.sigmoid(router_logit)[:, None] * projected).astype(bf16)
    return lax.dot_general(select, row_update, (((0,), (0,)), ((), ())), preferred_element_type=jnp.float32).astype(
        bf16
    )


def solution(mesh):
    return jax.shard_map(
        shards,
        mesh=mesh,
        in_specs=(
            P("ctx", "tp"),
            P("tp"),
            P("tp"),
            P("tp", None),
            P(None, "tp", None),
            P(None, "tp"),
            P(),
        ),
        out_specs=P("ctx", "tp"),
        check_vma=False,
    )
```

```python
import functools

import jax
import jax.numpy as jnp
from jax import lax
from jax.experimental import pallas as pl
from jax.experimental.pallas import tpu as pltpu
from jax.sharding import PartitionSpec as P

D = 8192
H = 32
KVH = 4
HD = 128
ZN = 8
EPSILON = 1e-05
MASKED_SCORE = -1e30
EXP_SCALE = HD ** (-0.5) * 1.4426950408889634
KEY_BLOCK = 1024
ROW_TILE = 512
ATTENTION_VMEM = 32 * 1024 * 1024


def z_shift(dz):
    return [(z * 2 + y, ((z + dz) % ZN) * 2 + y) for z in range(ZN) for y in range(2)]


def y_swap():
    return [(t, t ^ 1) for t in range(2 * ZN)]


def quad_shift(k):
    def target(z):
        return (z // 4) * 4 + (z % 4 + k) % 4

    return [(z * 2 + y, target(z) * 2 + y) for z in range(ZN) for y in range(2)]


def attention_kernel(info_ref, q_ref, kv_ref, o_ref, qa_ref, ka_ref, v_ref):
    shards_n, rows, _ = kv_ref.shape
    own = info_ref[shards_n]
    count = info_ref[own]
    first = pl.multiple_of(info_ref[shards_n + 1 + own], 16)

    def pack(step, _):
        start = pl.multiple_of(info_ref[shards_n + 1 + step], 16)
        slot = lax.broadcasted_iota(jnp.int32, (rows, HD), 0)
        ka_ref[pl.ds(start, rows), :HD] = kv_ref[step, :, :HD]
        ka_ref[pl.ds(start, rows), HD:] = jnp.where(slot < info_ref[step], 0.0, MASKED_SCORE).astype(jnp.bfloat16)
        v_ref[pl.ds(start, rows), :] = kv_ref[step, :, HD:]

    lax.fori_loop(0, own + 1, pack, None)
    tail = pl.multiple_of(first + rows, 16)
    ka_ref[pl.ds(tail, KEY_BLOCK), :] = jnp.zeros((KEY_BLOCK, 2 * HD), jnp.bfloat16)
    v_ref[pl.ds(tail, KEY_BLOCK), :] = jnp.zeros((KEY_BLOCK, HD), jnp.bfloat16)
    one = (lax.broadcasted_iota(jnp.int32, (rows, HD), 1) == 0).astype(jnp.bfloat16)
    for head in range(2):
        qa_ref[head, :, :HD] = q_ref[:, head * HD : (head + 1) * HD]
        qa_ref[head, :, HD:] = one
    open_blocks = first // KEY_BLOCK
    blocks = (first + count + KEY_BLOCK - 1) // KEY_BLOCK

    def lane_tiles(array):
        return [array[:, i * HD : (i + 1) * HD] for i in range(KEY_BLOCK // HD)]

    def tile_work(tile):
        base = tile * ROW_TILE

        def scores(block, head, masked):
            start = pl.multiple_of(block * KEY_BLOCK, KEY_BLOCK)
            out = lax.dot_general(
                qa_ref[head, base : base + ROW_TILE, :],
                ka_ref[pl.ds(start, KEY_BLOCK), :],
                (((1,), (1,)), ((), ())),
                preferred_element_type=jnp.float32,
            )
            if masked:
                key = lax.broadcasted_iota(jnp.int32, out.shape, 1)
                query = lax.broadcasted_iota(jnp.int32, out.shape, 0)
                out = jnp.where(key - query <= first + base - start, out, MASKED_SCORE)
            return out

        def body(masked):
            def run(block, state):
                start = pl.multiple_of(block * KEY_BLOCK, KEY_BLOCK)
                new = []
                for head in range(2):
                    peak, total, acc = state[3 * head : 3 * head + 3]
                    score = scores(block, head, masked)
                    lanes = functools.reduce(jnp.maximum, lane_tiles(score))
                    new_peak = jnp.maximum(peak, jnp.max(lanes, axis=1, keepdims=True))
                    weights = jnp.exp2(score - new_peak)
                    rescale = jnp.exp2(peak - new_peak)
                    new.append(new_peak)
                    new.append(functools.reduce(jnp.add, lane_tiles(weights), total * rescale))
                    new.append(
                        acc * rescale
                        + jnp.dot(
                            weights.astype(jnp.bfloat16),
                            v_ref[pl.ds(start, KEY_BLOCK), :],
                            preferred_element_type=jnp.float32,
                        )
                    )
                return tuple(new)

            return run

        zero = jnp.zeros((ROW_TILE, HD), jnp.float32)
        state = (jnp.full((ROW_TILE, 1), MASKED_SCORE, jnp.float32), zero, zero) * 2
        state = lax.fori_loop(0, open_blocks, body(False), state)
        state = lax.fori_loop(open_blocks, blocks, body(True), state)
        for head in range(2):
            total = jnp.sum(state[3 * head + 1], axis=1, keepdims=True)
            o_ref[base : base + ROW_TILE, head * HD : (head + 1) * HD] = (state[3 * head + 2] / total).astype(
                jnp.bfloat16
            )

    for tile in range(rows // ROW_TILE):
        if tile == 0:
            tile_work(tile)
        else:

            @pl.when(tile * ROW_TILE < count)
            def _():
                tile_work(tile)

            @pl.when(tile * ROW_TILE >= count)
            def _():
                o_ref[tile * ROW_TILE : (tile + 1) * ROW_TILE, :] = jnp.zeros((ROW_TILE, 2 * HD), jnp.bfloat16)


def attention(counts, own, queries, kv):
    shards_n, rows, _ = kv.shape
    packed = (counts + 15) // 16 * 16
    first = jnp.cumsum(packed) - packed
    info = jnp.concatenate([counts, own[None], first]).astype(jnp.int32)
    capacity = shards_n * (rows // 2 + 16) + rows + KEY_BLOCK
    return pl.pallas_call(
        attention_kernel,
        out_shape=jax.ShapeDtypeStruct(queries.shape, jnp.bfloat16),
        grid_spec=pltpu.PrefetchScalarGridSpec(
            num_scalar_prefetch=1,
            grid=(),
            in_specs=[pl.BlockSpec(memory_space=pltpu.VMEM)] * 2,
            out_specs=pl.BlockSpec(memory_space=pltpu.VMEM),
            scratch_shapes=[
                pltpu.VMEM((2, rows, 2 * HD), jnp.bfloat16),
                pltpu.VMEM((capacity, 2 * HD), jnp.bfloat16),
                pltpu.VMEM((capacity, HD), jnp.bfloat16),
            ],
        ),
        compiler_params=pltpu.CompilerParams(vmem_limit_bytes=ATTENTION_VMEM),
        cost_estimate=pl.CostEstimate(
            flops=4 * 2 * rows * HD * shards_n * rows, bytes_accessed=kv.size * 2, transcendentals=rows * rows * shards_n
        ),
    )(info, queries, kv)


def dot(a, b):
    return jnp.dot(a, b, preferred_element_type=jnp.float32)


def shards(hidden, norm_gain, router_weight, query_weight, key_value_weight, out_weight, kept_rows):
    bf16 = jnp.bfloat16
    shard = lax.axis_index("ctx")
    tp = lax.axis_index("tp")
    shard_n = lax.axis_size("ctx")
    z, y = tp // 2, tp % 2
    tokens, width = hidden.shape
    rows = kept_rows.shape[1]
    half_cols = query_weight.shape[1] // 2
    chunk = half_cols // ZN

    group = 2 * ZN // 2
    groups = [list(range(g, g + group)) for g in range(0, shard_n, group)]
    mine = shard % group

    def share(got):
        return lax.all_gather(got, "ctx", axis=0, tiled=False, axis_index_groups=groups)

    wq_sent = lax.dynamic_slice(query_weight, (0, (1 - y) * half_cols + mine * chunk), (width, chunk))
    wq_got = lax.ppermute(wq_sent, "tp", y_swap())

    own_rows = lax.dynamic_index_in_dim(kept_rows, shard, 0, keepdims=False)
    select = (own_rows[:, None] == jnp.arange(tokens, dtype=jnp.int32)[None, :]).astype(bf16)
    kept = dot(select, hidden)
    square_part = jnp.sum(kept * kept, axis=1)
    router_part = jnp.sum(kept * router_weight.astype(jnp.float32)[None, :], axis=1)
    x_own = (kept * norm_gain.astype(jnp.float32)[None, :]).astype(bf16)
    x_in = lax.ppermute(x_own, "tp", y_swap())

    kv_part = lax.dot_general(
        key_value_weight, x_own, (((1,), (1,)), ((), ())), preferred_element_type=jnp.float32
    ).astype(bf16)
    kv_part = (
        kv_part.reshape(2, 2, 2, 2, HD // 2, rows).transpose(2, 0, 3, 1, 4, 5).reshape(2 * ZN, HD // 2, rows)
    )
    stats = jnp.stack([square_part, router_part])
    stats_high = lax.reduce_precision(stats, 8, 7)
    stats_low = stats - stats_high
    stats_rows = jnp.concatenate([stats_high, stats_low, jnp.zeros((4, rows), jnp.float32)]).astype(bf16)
    sent = jnp.concatenate([kv_part, jnp.broadcast_to(stats_rows[None], (2 * ZN, 8, rows))], axis=1)
    sent, wq_got = lax.optimization_barrier((sent, wq_got))
    wq_in = share(wq_got)
    own_weights = lax.dynamic_slice(query_weight, (0, y * half_cols), (width, half_cols))
    query_own = dot(x_own, own_weights)
    summed = jnp.sum(lax.all_to_all(sent, "tp", 0, 0, tiled=True).astype(jnp.float32), axis=0)
    square_sum = summed[HD // 2] + summed[HD // 2 + 2]
    router_logit = summed[HD // 2 + 1] + summed[HD // 2 + 3]
    inverse_rms = lax.rsqrt(square_sum / D + EPSILON)
    piece = (summed[: HD // 2] * inverse_rms[None, :]).astype(bf16)
    piece, wq_in, x_in, query_own = lax.optimization_barrier((piece, wq_in, x_in, query_own))
    pieces = [lax.ppermute(piece, "tp", quad_shift(k)) for k in (3, 2, 1)] + [piece]
    ordered = jnp.stack(pieces + pieces[:3])
    kv_own = lax.dynamic_slice_in_dim(ordered, (3 - z % 4) % 4, 4, 0).reshape(2 * HD, rows).T
    kv_all = lax.all_gather(kv_own, "ctx", axis=0, tiled=False)

    def query_part(offset):
        d = (z + offset) % ZN
        own = lax.dynamic_slice(query_own, (0, d * chunk), (rows, chunk))
        return own + dot(x_in, lax.dynamic_index_in_dim(wq_in, d, 0, keepdims=False))

    def right(a):
        return lax.ppermute(a.astype(bf16), "tp", z_shift(1))

    def left(a):
        return lax.ppermute(a.astype(bf16), "tp", z_shift(-1))

    def both(going_right, going_left):
        return lax.optimization_barrier((right(going_right), left(going_left)))

    cut = chunk // 2
    far = query_part(4)
    going_right, going_left = both(far[:, :cut], far[:, cut:])
    part_right, part_left = query_part(3), query_part(-3)
    going_right, going_left = both(
        jnp.concatenate([part_right[:, :cut] + going_right, part_right[:, cut:]], axis=1),
        jnp.concatenate([part_left[:, :cut], part_left[:, cut:] + going_left], axis=1),
    )
    wo_rows = out_weight.shape[0] // 2
    wo_start = (1 - y) * wo_rows + mine * chunk
    going_right, wo_start = lax.optimization_barrier((going_right, wo_start))
    wo_got = lax.ppermute(
        lax.dynamic_slice(out_weight, (wo_start, 0), (chunk, width)), "tp", y_swap()
    )
    for step in (2, 1):
        going_right, going_left = both(query_part(step) + going_right, query_part(-step) + going_left)
    queries = (query_part(0) + going_right + going_left) * (inverse_rms * EXP_SCALE)[:, None]

    queries, wo_got = lax.optimization_barrier((queries.astype(bf16), wo_got))
    wo_in = share(wo_got).reshape(wo_rows, width)

    counts = jnp.sum((kept_rows < tokens).astype(jnp.int32), axis=1)
    mixed = attention(counts, shard, queries, kv_all)

    def project(piece, offset, low, high):
        start = ((z + offset) % ZN) * chunk + low
        own_w = lax.dynamic_slice(out_weight, (y * wo_rows + start, 0), (high - low, width))
        in_w = lax.dynamic_slice(wo_in, (start, 0), (high - low, width))
        return dot(piece, own_w), dot(piece, in_w)

    terms = [project(mixed, 0, 0, chunk)]
    from_left, from_right = mixed, mixed
    for step in (1, 2, 3):
        from_left, from_right = both(from_left, from_right)
        terms.append(project(from_left, -step, 0, chunk))
        terms.append(project(from_right, step, 0, chunk))
    terms.append(project(right(from_left[:, :cut]), 4, 0, cut))
    terms.append(project(left(from_right[:, cut:]), 4, cut, chunk))
    for_partner = functools.reduce(jnp.add, [t[1] for t in terms])
    received = lax.ppermute(for_partner.astype(bf16), "tp", y_swap())
    own_sum, received = lax.optimization_barrier((functools.reduce(jnp.add, [t[0] for t in terms]), received))
    projected = own_sum + received
    row_update = (jax.nn.sigmoid(router_logit)[:, None] * projected).astype(bf16)
    return lax.dot_general(select, row_update, (((0,), (0,)), ((), ())), preferred_element_type=jnp.float32).astype(
        bf16
    )


def solution(mesh):
    return jax.shard_map(
        shards,
        mesh=mesh,
        in_specs=(
            P("ctx", "tp"),
            P("tp"),
            P("tp"),
            P("tp", None),
            P(None, "tp", None),
            P(None, "tp"),
            P(),
        ),
        out_specs=P("ctx", "tp"),
        check_vma=False,
    )
```

```python
import functools

import jax
import jax.numpy as jnp
from jax import lax
from jax.experimental import pallas as pl
from jax.experimental.pallas import tpu as pltpu
from jax.sharding import PartitionSpec as P

D = 8192
H = 32
KVH = 4
HD = 128
ZN = 8
EPSILON = 1e-05
MASKED_SCORE = -1e30
EXP_SCALE = HD ** (-0.5) * 1.4426950408889634
KEY_BLOCK = 1024
ROW_TILE = 512
ATTENTION_VMEM = 32 * 1024 * 1024


def z_shift(dz):
    return [(z * 2 + y, ((z + dz) % ZN) * 2 + y) for z in range(ZN) for y in range(2)]


def y_swap():
    return [(t, t ^ 1) for t in range(2 * ZN)]


def quad_shift(k):
    def target(z):
        return (z // 4) * 4 + (z % 4 + k) % 4

    return [(z * 2 + y, target(z) * 2 + y) for z in range(ZN) for y in range(2)]


def attention_kernel(info_ref, q_ref, kv_ref, o_ref, qa_ref, ka_ref, v_ref):
    shards_n, rows, _ = kv_ref.shape
    own = info_ref[shards_n]
    count = info_ref[own]
    first = pl.multiple_of(info_ref[shards_n + 1 + own], 16)

    def pack(step, _):
        start = pl.multiple_of(info_ref[shards_n + 1 + step], 16)
        slot = lax.broadcasted_iota(jnp.int32, (rows, HD), 0)
        ka_ref[pl.ds(start, rows), :HD] = kv_ref[step, :, :HD]
        ka_ref[pl.ds(start, rows), HD:] = jnp.where(slot < info_ref[step], 0.0, MASKED_SCORE).astype(jnp.bfloat16)
        v_ref[pl.ds(start, rows), :] = kv_ref[step, :, HD:]

    lax.fori_loop(0, own + 1, pack, None)
    tail = pl.multiple_of(first + rows, 16)
    ka_ref[pl.ds(tail, KEY_BLOCK), :] = jnp.zeros((KEY_BLOCK, 2 * HD), jnp.bfloat16)
    v_ref[pl.ds(tail, KEY_BLOCK), :] = jnp.zeros((KEY_BLOCK, HD), jnp.bfloat16)
    one = (lax.broadcasted_iota(jnp.int32, (rows, HD), 1) == 0).astype(jnp.bfloat16)
    for head in range(2):
        qa_ref[head, :, :HD] = q_ref[:, head * HD : (head + 1) * HD]
        qa_ref[head, :, HD:] = one
    open_blocks = first // KEY_BLOCK
    blocks = (first + count + KEY_BLOCK - 1) // KEY_BLOCK

    def lane_tiles(array):
        return [array[:, i * HD : (i + 1) * HD] for i in range(KEY_BLOCK // HD)]

    def tile_work(tile):
        base = tile * ROW_TILE

        def scores(block, head, masked):
            start = pl.multiple_of(block * KEY_BLOCK, KEY_BLOCK)
            out = lax.dot_general(
                qa_ref[head, base : base + ROW_TILE, :],
                ka_ref[pl.ds(start, KEY_BLOCK), :],
                (((1,), (1,)), ((), ())),
                preferred_element_type=jnp.float32,
            )
            if masked:
                key = lax.broadcasted_iota(jnp.int32, out.shape, 1)
                query = lax.broadcasted_iota(jnp.int32, out.shape, 0)
                out = jnp.where(key - query <= first + base - start, out, MASKED_SCORE)
            return out

        def body(masked):
            def run(block, state):
                start = pl.multiple_of(block * KEY_BLOCK, KEY_BLOCK)
                new = []
                for head in range(2):
                    peak, total, acc = state[3 * head : 3 * head + 3]
                    score = scores(block, head, masked)
                    lanes = functools.reduce(jnp.maximum, lane_tiles(score))
                    new_peak = jnp.maximum(peak, jnp.max(lanes, axis=1, keepdims=True))
                    weights = jnp.exp2(score - new_peak)
                    rescale = jnp.exp2(peak - new_peak)
                    new.append(new_peak)
                    new.append(functools.reduce(jnp.add, lane_tiles(weights), total * rescale))
                    new.append(
                        acc * rescale
                        + jnp.dot(
                            weights.astype(jnp.bfloat16),
                            v_ref[pl.ds(start, KEY_BLOCK), :],
                            preferred_element_type=jnp.float32,
                        )
                    )
                return tuple(new)

            return run

        zero = jnp.zeros((ROW_TILE, HD), jnp.float32)
        state = (jnp.full((ROW_TILE, 1), MASKED_SCORE, jnp.float32), zero, zero) * 2
        state = lax.fori_loop(0, open_blocks, body(False), state)
        state = lax.fori_loop(open_blocks, blocks, body(True), state)
        for head in range(2):
            total = jnp.sum(state[3 * head + 1], axis=1, keepdims=True)
            o_ref[base : base + ROW_TILE, head * HD : (head + 1) * HD] = (state[3 * head + 2] / total).astype(
                jnp.bfloat16
            )

    for tile in range(rows // ROW_TILE):
        if tile == 0:
            tile_work(tile)
        else:

            @pl.when(tile * ROW_TILE < count)
            def _():
                tile_work(tile)

            @pl.when(tile * ROW_TILE >= count)
            def _():
                o_ref[tile * ROW_TILE : (tile + 1) * ROW_TILE, :] = jnp.zeros((ROW_TILE, 2 * HD), jnp.bfloat16)


def attention(counts, own, queries, kv):
    shards_n, rows, _ = kv.shape
    packed = (counts + 15) // 16 * 16
    first = jnp.cumsum(packed) - packed
    info = jnp.concatenate([counts, own[None], first]).astype(jnp.int32)
    capacity = shards_n * (rows // 2 + 16) + rows + KEY_BLOCK
    return pl.pallas_call(
        attention_kernel,
        out_shape=jax.ShapeDtypeStruct(queries.shape, jnp.bfloat16),
        grid_spec=pltpu.PrefetchScalarGridSpec(
            num_scalar_prefetch=1,
            grid=(),
            in_specs=[pl.BlockSpec(memory_space=pltpu.VMEM)] * 2,
            out_specs=pl.BlockSpec(memory_space=pltpu.VMEM),
            scratch_shapes=[
                pltpu.VMEM((2, rows, 2 * HD), jnp.bfloat16),
                pltpu.VMEM((capacity, 2 * HD), jnp.bfloat16),
                pltpu.VMEM((capacity, HD), jnp.bfloat16),
            ],
        ),
        compiler_params=pltpu.CompilerParams(vmem_limit_bytes=ATTENTION_VMEM),
        cost_estimate=pl.CostEstimate(
            flops=4 * 2 * rows * HD * shards_n * rows, bytes_accessed=kv.size * 2, transcendentals=rows * rows * shards_n
        ),
    )(info, queries, kv)


def order_kernel(at_ref, *refs):
    pieces, o_ref, scratch_ref = refs[:4], refs[4], refs[5]
    depth = pieces[0].shape[0]
    for k in range(4):
        place = lax.rem(at_ref[0] - k + 4, 4)
        scratch_ref[pl.ds(pl.multiple_of(place * depth, depth), depth), :] = pieces[k][...].astype(jnp.float32)
    o_ref[...] = scratch_ref[...].T.astype(jnp.bfloat16)


def ordered_rows(at, pieces):
    depth, rows = pieces[0].shape
    return pl.pallas_call(
        order_kernel,
        out_shape=jax.ShapeDtypeStruct((rows, 4 * depth), jnp.bfloat16),
        in_specs=[pl.BlockSpec(memory_space=pltpu.SMEM)] + [pl.BlockSpec(memory_space=pltpu.VMEM)] * 4,
        out_specs=pl.BlockSpec(memory_space=pltpu.VMEM),
        scratch_shapes=[pltpu.VMEM((4 * depth, rows), jnp.float32)],
        cost_estimate=pl.CostEstimate(flops=0, bytes_accessed=16 * depth * rows, transcendentals=0),
    )(at[None].astype(jnp.int32), *pieces)


def dot(a, b):
    return jnp.dot(a, b, preferred_element_type=jnp.float32)


def shards(hidden, norm_gain, router_weight, query_weight, key_value_weight, out_weight, kept_rows):
    bf16 = jnp.bfloat16
    shard = lax.axis_index("ctx")
    tp = lax.axis_index("tp")
    shard_n = lax.axis_size("ctx")
    z, y = tp // 2, tp % 2
    tokens, width = hidden.shape
    rows = kept_rows.shape[1]
    half_cols = query_weight.shape[1] // 2
    chunk = half_cols // ZN

    group = 2 * ZN // 2
    groups = [list(range(g, g + group)) for g in range(0, shard_n, group)]
    mine = shard % group

    def share(got):
        return lax.all_gather(got, "ctx", axis=0, tiled=False, axis_index_groups=groups)

    wq_sent = lax.dynamic_slice(query_weight, (0, (1 - y) * half_cols + mine * chunk), (width, chunk))
    wq_got = lax.ppermute(wq_sent, "tp", y_swap())

    own_rows = lax.dynamic_index_in_dim(kept_rows, shard, 0, keepdims=False)
    select = (own_rows[:, None] == jnp.arange(tokens, dtype=jnp.int32)[None, :]).astype(bf16)
    kept = dot(select, hidden)
    square_part = jnp.sum(kept * kept, axis=1)
    router_part = jnp.sum(kept * router_weight.astype(jnp.float32)[None, :], axis=1)
    x_own = (kept * norm_gain.astype(jnp.float32)[None, :]).astype(bf16)
    x_in = lax.ppermute(x_own, "tp", y_swap())

    kv_part = lax.dot_general(
        key_value_weight, x_own, (((1,), (1,)), ((), ())), preferred_element_type=jnp.float32
    ).astype(bf16)
    kv_part = (
        kv_part.reshape(2, 2, 2, 2, HD // 2, rows).transpose(2, 0, 3, 1, 4, 5).reshape(2 * ZN, HD // 2, rows)
    )
    stats = jnp.stack([square_part, router_part])
    stats_high = lax.reduce_precision(stats, 8, 7)
    stats_low = stats - stats_high
    stats_rows = jnp.concatenate([stats_high, stats_low, jnp.zeros((4, rows), jnp.float32)]).astype(bf16)
    sent = jnp.concatenate([kv_part, jnp.broadcast_to(stats_rows[None], (2 * ZN, 8, rows))], axis=1)
    sent, wq_got = lax.optimization_barrier((sent, wq_got))
    wq_in = share(wq_got)
    own_weights = lax.dynamic_slice(query_weight, (0, y * half_cols), (width, half_cols))
    query_own = dot(x_own, own_weights)
    summed = jnp.sum(lax.all_to_all(sent, "tp", 0, 0, tiled=True).astype(jnp.float32), axis=0)
    square_sum = summed[HD // 2] + summed[HD // 2 + 2]
    router_logit = summed[HD // 2 + 1] + summed[HD // 2 + 3]
    inverse_rms = lax.rsqrt(square_sum / D + EPSILON)
    piece = (summed[: HD // 2] * inverse_rms[None, :]).astype(bf16)
    piece, wq_in, x_in, query_own = lax.optimization_barrier((piece, wq_in, x_in, query_own))
    pieces = [lax.ppermute(piece, "tp", quad_shift(k)) for k in (1, 2, 3)]
    pieces = [piece] + pieces
    kv_own = ordered_rows(z % 4, pieces)
    kv_all = lax.all_gather(kv_own, "ctx", axis=0, tiled=False)

    def query_part(offset):
        d = (z + offset) % ZN
        own = lax.dynamic_slice(query_own, (0, d * chunk), (rows, chunk))
        return own + dot(x_in, lax.dynamic_index_in_dim(wq_in, d, 0, keepdims=False))

    def right(a):
        return lax.ppermute(a.astype(bf16), "tp", z_shift(1))

    def left(a):
        return lax.ppermute(a.astype(bf16), "tp", z_shift(-1))

    def both(going_right, going_left):
        return lax.optimization_barrier((right(going_right), left(going_left)))

    cut = chunk // 2
    far = query_part(4)
    going_right, going_left = both(far[:, :cut], far[:, cut:])
    part_right, part_left = query_part(3), query_part(-3)
    going_right, going_left = both(
        jnp.concatenate([part_right[:, :cut] + going_right, part_right[:, cut:]], axis=1),
        jnp.concatenate([part_left[:, :cut], part_left[:, cut:] + going_left], axis=1),
    )
    wo_rows = out_weight.shape[0] // 2
    wo_start = (1 - y) * wo_rows + mine * chunk
    wo_own = lax.dynamic_slice(out_weight, (y * wo_rows, 0), (wo_rows, width))
    going_right, wo_start = lax.optimization_barrier((going_right, wo_start))
    wo_got = lax.ppermute(
        lax.dynamic_slice(out_weight, (wo_start, 0), (chunk, width)), "tp", y_swap()
    )
    for step in (2, 1):
        going_right, going_left = both(query_part(step) + going_right, query_part(-step) + going_left)
    queries = (query_part(0) + going_right + going_left) * (inverse_rms * EXP_SCALE)[:, None]

    queries, wo_got, wo_own = lax.optimization_barrier((queries.astype(bf16), wo_got, wo_own))
    wo_in = share(wo_got).reshape(wo_rows, width)

    counts = jnp.sum((kept_rows < tokens).astype(jnp.int32), axis=1)
    mixed = attention(counts, shard, queries, kv_all)

    halves = [mixed[at : at + rows // 2] for at in (0, rows // 2)]
    arrived = [[(half, half)] for half in halves]
    for step in (1, 2, 3):
        for hops in arrived:
            hops.append(both(*hops[-1]))
        if step == 2:
            arrived[0][-1], wo_in = lax.optimization_barrier((arrived[0][-1], wo_in))

    def weights(array, offset, low, high):
        return lax.dynamic_slice(array, (((z + offset) % ZN) * chunk + low, 0), (high - low, width))

    def project(array, hops, last):
        total = dot(hops[0][0], weights(array, 0, 0, chunk))
        for step in (1, 2, 3):
            total = total + dot(hops[step][0], weights(array, -step, 0, chunk))
            total = total + dot(hops[step][1], weights(array, step, 0, chunk))
        return total + dot(last[0], weights(array, 4, 0, cut)) + dot(last[1], weights(array, 4, cut, chunk))

    projected = []
    for hops in arrived:
        last = right(hops[3][0][:, :cut]), left(hops[3][1][:, cut:])
        received = lax.ppermute(project(wo_in, hops, last).astype(bf16), "tp", y_swap())
        projected.append(lax.optimization_barrier((project(wo_own, hops, last), received)))
    projected = jnp.concatenate([own + received for own, received in projected])
    row_update = (jax.nn.sigmoid(router_logit)[:, None] * projected).astype(bf16)
    return lax.dot_general(select, row_update, (((0,), (0,)), ((), ())), preferred_element_type=jnp.float32).astype(
        bf16
    )


def solution(mesh):
    return jax.shard_map(
        shards,
        mesh=mesh,
        in_specs=(
            P("ctx", "tp"),
            P("tp"),
            P("tp"),
            P("tp", None),
            P(None, "tp", None),
            P(None, "tp"),
            P(),
        ),
        out_specs=P("ctx", "tp"),
        check_vma=False,
    )
```

```python
import functools

import jax
import jax.numpy as jnp
from jax import lax
from jax.experimental import pallas as pl
from jax.experimental.pallas import tpu as pltpu
from jax.sharding import PartitionSpec as P

D = 8192
H = 32
KVH = 4
HD = 128
ZN = 8
EPSILON = 1e-05
MASKED_SCORE = -1e30
EXP_SCALE = HD ** (-0.5) * 1.4426950408889634
KEY_BLOCK = 1024
ROW_TILE = 512
ATTENTION_VMEM = 32 * 1024 * 1024


def z_shift(dz):
    return [(z * 2 + y, ((z + dz) % ZN) * 2 + y) for z in range(ZN) for y in range(2)]


def y_swap():
    return [(t, t ^ 1) for t in range(2 * ZN)]


def quad_shift(k):
    def target(z):
        return (z // 4) * 4 + (z % 4 + k) % 4

    return [(z * 2 + y, target(z) * 2 + y) for z in range(ZN) for y in range(2)]


def attention_kernel(info_ref, q_ref, *refs):
    kv_refs, (o_ref, qa_ref, ka_ref, v_ref) = refs[:-4], refs[-4:]
    blocks_each, rows, _ = kv_refs[0].shape
    order = [(array, place) for array in range(len(kv_refs)) for place in range(blocks_each)]
    order = order[1:] + order[:1]
    count = info_ref[len(order) - 1, 1]
    first = pl.multiple_of(info_ref[len(order) - 1, 2], 16)

    for index, (array, place) in enumerate(order):

        @pl.when(info_ref[index, 0] > 0)
        def _():
            start = pl.multiple_of(info_ref[index, 2], 16)
            slot = lax.broadcasted_iota(jnp.int32, (rows, HD), 0)
            bias = jnp.where(slot < info_ref[index, 1], 0.0, MASKED_SCORE)
            ka_ref[pl.ds(start, rows), :HD] = kv_refs[array][place, :, :HD]
            ka_ref[pl.ds(start, rows), HD:] = bias.astype(jnp.bfloat16)
            v_ref[pl.ds(start, rows), :] = kv_refs[array][place, :, HD:]

    tail = pl.multiple_of(first + rows, 16)
    ka_ref[pl.ds(tail, KEY_BLOCK), :] = jnp.zeros((KEY_BLOCK, 2 * HD), jnp.bfloat16)
    v_ref[pl.ds(tail, KEY_BLOCK), :] = jnp.zeros((KEY_BLOCK, HD), jnp.bfloat16)
    one = (lax.broadcasted_iota(jnp.int32, (rows, HD), 1) == 0).astype(jnp.bfloat16)
    for head in range(2):
        qa_ref[head, :, :HD] = q_ref[:, head * HD : (head + 1) * HD]
        qa_ref[head, :, HD:] = one
    open_blocks = first // KEY_BLOCK
    blocks = (first + count + KEY_BLOCK - 1) // KEY_BLOCK

    def lane_tiles(array):
        return [array[:, i * HD : (i + 1) * HD] for i in range(KEY_BLOCK // HD)]

    def tile_work(tile):
        base = tile * ROW_TILE

        def scores(block, head, masked):
            start = pl.multiple_of(block * KEY_BLOCK, KEY_BLOCK)
            out = lax.dot_general(
                qa_ref[head, base : base + ROW_TILE, :],
                ka_ref[pl.ds(start, KEY_BLOCK), :],
                (((1,), (1,)), ((), ())),
                preferred_element_type=jnp.float32,
            )
            if masked:
                key = lax.broadcasted_iota(jnp.int32, out.shape, 1)
                query = lax.broadcasted_iota(jnp.int32, out.shape, 0)
                out = jnp.where(key - query <= first + base - start, out, MASKED_SCORE)
            return out

        def body(masked):
            def run(block, state):
                start = pl.multiple_of(block * KEY_BLOCK, KEY_BLOCK)
                new = []
                for head in range(2):
                    peak, total, acc = state[3 * head : 3 * head + 3]
                    score = scores(block, head, masked)
                    lanes = functools.reduce(jnp.maximum, lane_tiles(score))
                    new_peak = jnp.maximum(peak, jnp.max(lanes, axis=1, keepdims=True))
                    weights = jnp.exp2(score - new_peak)
                    rescale = jnp.exp2(peak - new_peak)
                    new.append(new_peak)
                    new.append(functools.reduce(jnp.add, lane_tiles(weights), total * rescale))
                    new.append(
                        acc * rescale
                        + jnp.dot(
                            weights.astype(jnp.bfloat16),
                            v_ref[pl.ds(start, KEY_BLOCK), :],
                            preferred_element_type=jnp.float32,
                        )
                    )
                return tuple(new)

            return run

        zero = jnp.zeros((ROW_TILE, HD), jnp.float32)
        state = (jnp.full((ROW_TILE, 1), MASKED_SCORE, jnp.float32), zero, zero) * 2
        state = lax.fori_loop(0, open_blocks, body(False), state)
        state = lax.fori_loop(open_blocks, blocks, body(True), state)
        for head in range(2):
            total = jnp.sum(state[3 * head + 1], axis=1, keepdims=True)
            o_ref[base : base + ROW_TILE, head * HD : (head + 1) * HD] = (state[3 * head + 2] / total).astype(
                jnp.bfloat16
            )

    for tile in range(rows // ROW_TILE):
        if tile == 0:
            tile_work(tile)
        else:

            @pl.when(tile * ROW_TILE < count)
            def _():
                tile_work(tile)

            @pl.when(tile * ROW_TILE >= count)
            def _():
                o_ref[tile * ROW_TILE : (tile + 1) * ROW_TILE, :] = jnp.zeros((ROW_TILE, 2 * HD), jnp.bfloat16)


def attention(counts, own, queries, ids, kv):
    blocks_each, rows, _ = kv[0].shape
    shards_n = blocks_each * len(kv)
    ids = jnp.concatenate([ids[1:], ids[:1]])
    used = ids <= own
    held = jnp.sum(jnp.where(ids[:, None] == jnp.arange(shards_n)[None, :], counts[None, :], 0), axis=1)
    packed = jnp.where(used, (held + 15) // 16 * 16, 0)
    before = jnp.arange(shards_n)[None, :] < jnp.arange(shards_n)[:, None]
    first = jnp.sum(jnp.where(before, packed[None, :], 0), axis=1)
    info = jnp.stack([used.astype(jnp.int32), held, first], axis=1).astype(jnp.int32)
    capacity = shards_n * (rows // 2 + 16) + rows + KEY_BLOCK
    return pl.pallas_call(
        attention_kernel,
        out_shape=jax.ShapeDtypeStruct(queries.shape, jnp.bfloat16),
        in_specs=[pl.BlockSpec(memory_space=pltpu.SMEM)]
        + [pl.BlockSpec(memory_space=pltpu.VMEM)] * (1 + len(kv)),
        out_specs=pl.BlockSpec(memory_space=pltpu.VMEM),
        scratch_shapes=[
            pltpu.VMEM((2, rows, 2 * HD), jnp.bfloat16),
            pltpu.VMEM((capacity, 2 * HD), jnp.bfloat16),
            pltpu.VMEM((capacity, HD), jnp.bfloat16),
        ],
        compiler_params=pltpu.CompilerParams(vmem_limit_bytes=ATTENTION_VMEM),
        cost_estimate=pl.CostEstimate(
            flops=4 * 2 * rows * HD * shards_n * rows,
            bytes_accessed=shards_n * rows * HD * 4,
            transcendentals=rows * rows * shards_n,
        ),
    )(info, queries, *kv)


def query_kernel(y_ref, x_own_ref, x_in_ref, w_own_ref, w_in_ref, o_ref):
    o_ref[0] = (dot(x_own_ref[...], w_own_ref[...]) + dot(x_in_ref[...], w_in_ref[0])).astype(jnp.bfloat16)


def query_parts(y, x_own, x_in, query_weight, wq_in):
    chunks, width, chunk = wq_in.shape
    rows = x_own.shape[0]
    return pl.pallas_call(
        query_kernel,
        out_shape=jax.ShapeDtypeStruct((chunks, rows, chunk), jnp.bfloat16),
        grid_spec=pltpu.PrefetchScalarGridSpec(
            num_scalar_prefetch=1,
            grid=(chunks,),
            in_specs=[
                pl.BlockSpec((rows, width), lambda d, y: (0, 0)),
                pl.BlockSpec((rows, width), lambda d, y: (0, 0)),
                pl.BlockSpec((width, chunk), lambda d, y: (0, y[0] * chunks + d)),
                pl.BlockSpec((1, width, chunk), lambda d, y: (d, 0, 0)),
            ],
            out_specs=pl.BlockSpec((1, rows, chunk), lambda d, y: (d, 0, 0)),
        ),
        compiler_params=pltpu.CompilerParams(vmem_limit_bytes=16 * 1024 * 1024),
        cost_estimate=pl.CostEstimate(
            flops=4 * chunks * rows * width * chunk, bytes_accessed=chunks * chunk * (4 * width + 2 * rows), transcendentals=0
        ),
    )(y[None].astype(jnp.int32), x_own, x_in, query_weight, wq_in)


def order_kernel(at_ref, *refs):
    pieces, o_ref, scratch_ref = refs[:4], refs[4], refs[5]
    depth = pieces[0].shape[0]
    for k in range(4):
        place = lax.rem(at_ref[0] - k + 4, 4)
        scratch_ref[pl.ds(pl.multiple_of(place * depth, depth), depth), :] = pieces[k][...].astype(jnp.float32)
    o_ref[...] = scratch_ref[...].T.astype(jnp.bfloat16)


def ordered_rows(at, pieces):
    depth, rows = pieces[0].shape
    return pl.pallas_call(
        order_kernel,
        out_shape=jax.ShapeDtypeStruct((rows, 4 * depth), jnp.bfloat16),
        in_specs=[pl.BlockSpec(memory_space=pltpu.SMEM)] + [pl.BlockSpec(memory_space=pltpu.VMEM)] * 4,
        out_specs=pl.BlockSpec(memory_space=pltpu.VMEM),
        scratch_shapes=[pltpu.VMEM((4 * depth, rows), jnp.float32)],
        cost_estimate=pl.CostEstimate(flops=0, bytes_accessed=16 * depth * rows, transcendentals=0),
    )(at[None].astype(jnp.int32), *pieces)


def dot(a, b):
    return jnp.dot(a, b, preferred_element_type=jnp.float32)


def shards(hidden, norm_gain, router_weight, query_weight, key_value_weight, out_weight, kept_rows):
    bf16 = jnp.bfloat16
    shard = lax.axis_index("ctx")
    tp = lax.axis_index("tp")
    shard_n = lax.axis_size("ctx")
    z, y = tp // 2, tp % 2
    tokens, width = hidden.shape
    rows = kept_rows.shape[1]
    half_cols = query_weight.shape[1] // 2
    chunk = half_cols // ZN

    group = 2 * ZN // 2
    groups = [list(range(g, g + group)) for g in range(0, shard_n, group)]
    mine = shard % group

    def share(got):
        return lax.all_gather(got, "ctx", axis=0, tiled=False, axis_index_groups=groups)

    wq_sent = lax.dynamic_slice(query_weight, (0, (1 - y) * half_cols + mine * chunk), (width, chunk))
    wq_got = lax.ppermute(wq_sent, "tp", y_swap())

    own_rows = lax.dynamic_index_in_dim(kept_rows, shard, 0, keepdims=False)
    select = (own_rows[:, None] == jnp.arange(tokens, dtype=jnp.int32)[None, :]).astype(bf16)
    kept = dot(select, hidden)
    square_part = jnp.sum(kept * kept, axis=1)
    router_part = jnp.sum(kept * router_weight.astype(jnp.float32)[None, :], axis=1)
    x_own = (kept * norm_gain.astype(jnp.float32)[None, :]).astype(bf16)
    x_in = lax.ppermute(x_own, "tp", y_swap())

    kv_part = lax.dot_general(
        key_value_weight, x_own, (((1,), (1,)), ((), ())), preferred_element_type=jnp.float32
    ).astype(bf16)
    kv_part = (
        kv_part.reshape(2, 2, 2, 2, HD // 2, rows).transpose(2, 0, 3, 1, 4, 5).reshape(2 * ZN, HD // 2, rows)
    )
    stats = jnp.stack([square_part, router_part])
    stats_high = lax.reduce_precision(stats, 8, 7)
    stats_low = stats - stats_high
    stats_rows = jnp.concatenate([stats_high, stats_low, jnp.zeros((4, rows), jnp.float32)]).astype(bf16)
    sent = jnp.concatenate([kv_part, jnp.broadcast_to(stats_rows[None], (2 * ZN, 8, rows))], axis=1)
    sent, wq_got = lax.optimization_barrier((sent, wq_got))
    wq_in = share(wq_got)
    exchanged = lax.all_to_all(sent, "tp", 0, 0, tiled=True)
    part = query_parts(y, x_own, x_in, query_weight, wq_in)
    exchanged, part = lax.optimization_barrier((exchanged, part))
    query_sum = lax.psum_scatter(
        part, "tp", scatter_dimension=0, axis_index_groups=[[2 * k + h for k in range(ZN)] for h in range(2)]
    )
    summed = jnp.sum(exchanged.astype(jnp.float32), axis=0)
    square_sum = summed[HD // 2] + summed[HD // 2 + 2]
    router_logit = summed[HD // 2 + 1] + summed[HD // 2 + 3]
    inverse_rms = lax.rsqrt(square_sum / D + EPSILON)
    piece = (summed[: HD // 2] * inverse_rms[None, :]).astype(bf16)
    pieces = [lax.ppermute(piece, "tp", quad_shift(k)) for k in (1, 2, 3)]
    pieces = [piece] + pieces
    kv_own = ordered_rows(z % 4, pieces)

    x_n = shard_n // 4

    def along(step):
        return [(c, c // (2 * x_n) * (2 * x_n) + (c + 2 * step) % (2 * x_n)) for c in range(shard_n)]

    def x_hop(block, step):
        return lax.ppermute(block, "ctx", along(step))

    middle = rows // 2
    over = lax.ppermute(kv_own, "ctx", [(c, (c + shard_n // 2) % shard_n) for c in range(shard_n)])
    near_left, near_right, over = lax.optimization_barrier((x_hop(kv_own, 1), x_hop(kv_own, -1), over))
    first_half = jnp.stack([kv_own, near_left, near_right, over])
    far = x_hop(near_left[:middle], 1), x_hop(near_right[middle:], -1)
    over_left, over_right = x_hop(over, 1), x_hop(over, -1)
    wo_rows = out_weight.shape[0] // 2
    wo_start = (1 - y) * wo_rows + mine * chunk
    near_left, wo_start = lax.optimization_barrier((near_left, wo_start))
    wo_got = lax.ppermute(lax.dynamic_slice(out_weight, (wo_start, 0), (chunk, width)), "tp", y_swap())
    over_left, over_right, far, wo_got = lax.optimization_barrier((over_left, over_right, far, wo_got))
    wo_in = share(wo_got).reshape(wo_rows, width)
    over_far = x_hop(over_left[:middle], 1), x_hop(over_right[middle:], -1)
    second_half = jnp.stack([over_left, over_right, jnp.concatenate(far), jnp.concatenate(over_far)])

    def core_hop(block):
        return lax.ppermute(block, "ctx", [(c, c ^ 1) for c in range(shard_n)])

    kv_all = [first_half, second_half, core_hop(first_half), core_hop(second_half)]
    at_y, at_x, core = shard // (2 * x_n), shard // 2 % x_n, shard % 2
    offsets = [(0, 0), (-1, 0), (1, 0), (0, 1), (-1, 1), (1, 1), (2, 0), (2, 1)]
    ids = [(at_y + dy) % 2 * (2 * x_n) + (at_x + dx) % x_n * 2 for dx, dy in offsets]
    ids = jnp.stack([i + core for i in ids] + [i + 1 - core for i in ids])

    def right(a):
        return lax.ppermute(a.astype(bf16), "tp", z_shift(1))

    def left(a):
        return lax.ppermute(a.astype(bf16), "tp", z_shift(-1))

    def both(going_right, going_left):
        return lax.optimization_barrier((right(going_right), left(going_left)))

    cut = chunk // 2
    queries = (query_sum.astype(jnp.float32) * (inverse_rms * EXP_SCALE)[:, None]).astype(bf16)

    counts = jnp.sum((kept_rows < tokens).astype(jnp.int32), axis=1)
    mixed = attention(counts, shard, queries, ids, kv_all)

    def project(piece, offset, low, high):
        start = ((z + offset) % ZN) * chunk + low
        own_w = lax.dynamic_slice(out_weight, (y * wo_rows + start, 0), (high - low, width))
        in_w = lax.dynamic_slice(wo_in, (start, 0), (high - low, width))
        return dot(piece, own_w), dot(piece, in_w)

    terms = [project(mixed, 0, 0, chunk)]
    from_left, from_right = mixed, mixed
    for step in (1, 2, 3):
        from_left, from_right = both(from_left, from_right)
        terms.append(project(from_left, -step, 0, chunk))
        terms.append(project(from_right, step, 0, chunk))
    terms.append(project(right(from_left[:, :cut]), 4, 0, cut))
    terms.append(project(left(from_right[:, cut:]), 4, cut, chunk))
    for_partner = functools.reduce(jnp.add, [t[1] for t in terms])
    received = lax.ppermute(for_partner.astype(bf16), "tp", y_swap())
    own_sum, received = lax.optimization_barrier((functools.reduce(jnp.add, [t[0] for t in terms]), received))
    projected = own_sum + received
    row_update = (jax.nn.sigmoid(router_logit)[:, None] * projected).astype(bf16)
    return lax.dot_general(select, row_update, (((0,), (0,)), ((), ())), preferred_element_type=jnp.float32).astype(
        bf16
    )


def solution(mesh):
    return jax.shard_map(
        shards,
        mesh=mesh,
        in_specs=(
            P("ctx", "tp"),
            P("tp"),
            P("tp"),
            P("tp", None),
            P(None, "tp", None),
            P(None, "tp"),
            P(),
        ),
        out_specs=P("ctx", "tp"),
        check_vma=False,
    )
```

```python
import functools

import jax
import jax.numpy as jnp
from jax import lax
from jax.experimental import pallas as pl
from jax.experimental.pallas import tpu as pltpu
from jax.sharding import PartitionSpec as P

D = 8192
H = 32
KVH = 4
HD = 128
ZN = 8
EPSILON = 1e-05
MASKED_SCORE = -1e30
EXP_SCALE = HD ** (-0.5) * 1.4426950408889634
KEY_BLOCK = 1024
ROW_TILE = 512
ATTENTION_VMEM = 32 * 1024 * 1024


def z_shift(dz):
    return [(z * 2 + y, ((z + dz) % ZN) * 2 + y) for z in range(ZN) for y in range(2)]


def y_swap():
    return [(t, t ^ 1) for t in range(2 * ZN)]


def quad_shift(k):
    def target(z):
        return (z // 4) * 4 + (z % 4 + k) % 4

    return [(z * 2 + y, target(z) * 2 + y) for z in range(ZN) for y in range(2)]


def attention_kernel(info_ref, q_ref, *refs):
    kv_refs, (o_ref, qa_ref, ka_ref, v_ref) = refs[:-4], refs[-4:]
    blocks_each, rows, _ = kv_refs[0].shape
    order = [(array, place) for array in range(len(kv_refs)) for place in range(blocks_each)]
    order = order[1:] + order[:1]
    count = info_ref[len(order) - 1, 1]
    first = pl.multiple_of(info_ref[len(order) - 1, 2], 16)

    for index, (array, place) in enumerate(order):

        @pl.when(info_ref[index, 0] > 0)
        def _():
            start = pl.multiple_of(info_ref[index, 2], 16)
            slot = lax.broadcasted_iota(jnp.int32, (rows, HD), 0)
            bias = jnp.where(slot < info_ref[index, 1], 0.0, MASKED_SCORE)
            ka_ref[pl.ds(start, rows), :HD] = kv_refs[array][place, :, :HD]
            ka_ref[pl.ds(start, rows), HD:] = bias.astype(jnp.bfloat16)
            v_ref[pl.ds(start, rows), :] = kv_refs[array][place, :, HD:]

    tail = pl.multiple_of(first + rows, 16)
    ka_ref[pl.ds(tail, KEY_BLOCK), :] = jnp.zeros((KEY_BLOCK, 2 * HD), jnp.bfloat16)
    v_ref[pl.ds(tail, KEY_BLOCK), :] = jnp.zeros((KEY_BLOCK, HD), jnp.bfloat16)
    one = (lax.broadcasted_iota(jnp.int32, (rows, HD), 1) == 0).astype(jnp.bfloat16)
    for head in range(2):
        qa_ref[head, :, :HD] = q_ref[:, head * HD : (head + 1) * HD]
        qa_ref[head, :, HD:] = one
    open_blocks = first // KEY_BLOCK
    blocks = (first + count + KEY_BLOCK - 1) // KEY_BLOCK

    def lane_tiles(array):
        return [array[:, i * HD : (i + 1) * HD] for i in range(KEY_BLOCK // HD)]

    def tile_work(tile):
        base = tile * ROW_TILE

        def scores(block, head, masked):
            start = pl.multiple_of(block * KEY_BLOCK, KEY_BLOCK)
            out = lax.dot_general(
                qa_ref[head, base : base + ROW_TILE, :],
                ka_ref[pl.ds(start, KEY_BLOCK), :],
                (((1,), (1,)), ((), ())),
                preferred_element_type=jnp.float32,
            )
            if masked:
                key = lax.broadcasted_iota(jnp.int32, out.shape, 1)
                query = lax.broadcasted_iota(jnp.int32, out.shape, 0)
                out = jnp.where(key - query <= first + base - start, out, MASKED_SCORE)
            return out

        def body(masked):
            def run(block, state):
                start = pl.multiple_of(block * KEY_BLOCK, KEY_BLOCK)
                new = []
                for head in range(2):
                    peak, total, acc = state[3 * head : 3 * head + 3]
                    score = scores(block, head, masked)
                    lanes = functools.reduce(jnp.maximum, lane_tiles(score))
                    new_peak = jnp.maximum(peak, jnp.max(lanes, axis=1, keepdims=True))
                    weights = jnp.exp2(score - new_peak)
                    rescale = jnp.exp2(peak - new_peak)
                    new.append(new_peak)
                    new.append(functools.reduce(jnp.add, lane_tiles(weights), total * rescale))
                    new.append(
                        acc * rescale
                        + jnp.dot(
                            weights.astype(jnp.bfloat16),
                            v_ref[pl.ds(start, KEY_BLOCK), :],
                            preferred_element_type=jnp.float32,
                        )
                    )
                return tuple(new)

            return run

        zero = jnp.zeros((ROW_TILE, HD), jnp.float32)
        state = (jnp.full((ROW_TILE, 1), MASKED_SCORE, jnp.float32), zero, zero) * 2
        state = lax.fori_loop(0, open_blocks, body(False), state)
        state = lax.fori_loop(open_blocks, blocks, body(True), state)
        for head in range(2):
            total = jnp.sum(state[3 * head + 1], axis=1, keepdims=True)
            o_ref[base : base + ROW_TILE, head * HD : (head + 1) * HD] = (state[3 * head + 2] / total).astype(
                jnp.bfloat16
            )

    for tile in range(rows // ROW_TILE):
        if tile == 0:
            tile_work(tile)
        else:

            @pl.when(tile * ROW_TILE < count)
            def _():
                tile_work(tile)

            @pl.when(tile * ROW_TILE >= count)
            def _():
                o_ref[tile * ROW_TILE : (tile + 1) * ROW_TILE, :] = jnp.zeros((ROW_TILE, 2 * HD), jnp.bfloat16)


def packing(counts, own, ids):
    shards_n = ids.shape[0]
    ids = jnp.concatenate([ids[1:], ids[:1]])
    used = ids <= own
    held = jnp.sum(jnp.where(ids[:, None] == jnp.arange(shards_n)[None, :], counts[None, :], 0), axis=1)
    packed = jnp.where(used, (held + 15) // 16 * 16, 0)
    before = jnp.arange(shards_n)[None, :] < jnp.arange(shards_n)[:, None]
    first = jnp.sum(jnp.where(before, packed[None, :], 0), axis=1)
    return jnp.stack([used.astype(jnp.int32), held, first], axis=1).astype(jnp.int32)


def attention(info, queries, kv):
    blocks_each, rows, _ = kv[0].shape
    shards_n = blocks_each * len(kv)
    capacity = shards_n * (rows // 2 + 16) + rows + KEY_BLOCK
    return pl.pallas_call(
        attention_kernel,
        out_shape=jax.ShapeDtypeStruct(queries.shape, jnp.bfloat16),
        in_specs=[pl.BlockSpec(memory_space=pltpu.SMEM)]
        + [pl.BlockSpec(memory_space=pltpu.VMEM)] * (1 + len(kv)),
        out_specs=pl.BlockSpec(memory_space=pltpu.VMEM),
        scratch_shapes=[
            pltpu.VMEM((2, rows, 2 * HD), jnp.bfloat16),
            pltpu.VMEM((capacity, 2 * HD), jnp.bfloat16),
            pltpu.VMEM((capacity, HD), jnp.bfloat16),
        ],
        compiler_params=pltpu.CompilerParams(vmem_limit_bytes=ATTENTION_VMEM),
        cost_estimate=pl.CostEstimate(
            flops=4 * 2 * rows * HD * shards_n * rows,
            bytes_accessed=shards_n * rows * HD * 4,
            transcendentals=rows * rows * shards_n,
        ),
    )(info, queries, *kv)


def rows_kernel(rows_ref, hidden_ref, gain_ref, router_ref, kv_ref, x_ref, sent_ref):
    tokens, width = hidden_ref.shape
    rows = rows_ref.shape[1]
    token = lax.broadcasted_iota(jnp.int32, (tokens, rows), 0)
    select = jnp.where(token == rows_ref[...], 1.0, 0.0).astype(jnp.bfloat16)
    kept = lax.dot_general(select, hidden_ref[...], (((0,), (0,)), ((), ())), preferred_element_type=jnp.float32)
    normed = kept * gain_ref[...].astype(jnp.float32)
    x_ref[...] = normed.astype(jnp.bfloat16)

    def feature_sum(array):
        tiles = [array[:, i * HD : (i + 1) * HD] for i in range(width // HD)]
        return jnp.sum(functools.reduce(jnp.add, tiles).T, axis=0, keepdims=True)

    stats = jnp.concatenate([feature_sum(kept * kept), feature_sum(kept * router_ref[...].astype(jnp.float32))])
    high = stats.astype(jnp.bfloat16).astype(jnp.float32)
    stats = jnp.concatenate([high, stats - high, jnp.zeros((4, rows), jnp.float32)])
    turned = normed.T.astype(jnp.bfloat16)
    depth = sent_ref.shape[1] - stats.shape[0]
    halves = HD // depth
    for which in range(2):
        sums = lax.dot_general(
            kv_ref[which], turned, (((0,), (0,)), ((), ())), preferred_element_type=jnp.float32
        )
        for group in range(KVH):
            for half in range(halves):
                start = group * HD + half * depth
                place = ((group % 2 * 2 + which) * halves + half) * 2 + group // 2
                sent_ref[place] = jnp.concatenate([sums[start : start + depth], stats]).astype(jnp.bfloat16)


def rows_and_sums(own_rows, hidden, norm_gain, router_weight, key_value_weight):
    rows, (_, width) = own_rows.shape[1], hidden.shape
    return pl.pallas_call(
        rows_kernel,
        out_shape=(
            jax.ShapeDtypeStruct((rows, width), jnp.bfloat16),
            jax.ShapeDtypeStruct((2 * ZN, HD // 2 + 8, rows), jnp.bfloat16),
        ),
        in_specs=[pl.BlockSpec(memory_space=pltpu.VMEM)] * 5,
        out_specs=(pl.BlockSpec(memory_space=pltpu.VMEM),) * 2,
        compiler_params=pltpu.CompilerParams(vmem_limit_bytes=24 * 1024 * 1024),
        cost_estimate=pl.CostEstimate(
            flops=4 * rows * width * hidden.shape[0], bytes_accessed=5 * 1024 * 1024, transcendentals=0
        ),
    )(own_rows, hidden, norm_gain.reshape(1, width), router_weight.reshape(1, width), key_value_weight)


def query_kernel(y_ref, x_own_ref, x_in_ref, w_own_ref, w_in_ref, o_ref):
    o_ref[0] = (dot(x_own_ref[...], w_own_ref[...]) + dot(x_in_ref[...], w_in_ref[0])).astype(jnp.bfloat16)


def query_parts(y, x_own, x_in, query_weight, wq_in):
    chunks, width, chunk = wq_in.shape
    rows = x_own.shape[0]
    return pl.pallas_call(
        query_kernel,
        out_shape=jax.ShapeDtypeStruct((chunks, rows, chunk), jnp.bfloat16),
        grid_spec=pltpu.PrefetchScalarGridSpec(
            num_scalar_prefetch=1,
            grid=(chunks,),
            in_specs=[
                pl.BlockSpec((rows, width), lambda d, y: (0, 0)),
                pl.BlockSpec((rows, width), lambda d, y: (0, 0)),
                pl.BlockSpec((width, chunk), lambda d, y: (0, y[0] * chunks + d)),
                pl.BlockSpec((1, width, chunk), lambda d, y: (d, 0, 0)),
            ],
            out_specs=pl.BlockSpec((1, rows, chunk), lambda d, y: (d, 0, 0)),
        ),
        compiler_params=pltpu.CompilerParams(vmem_limit_bytes=16 * 1024 * 1024),
        cost_estimate=pl.CostEstimate(
            flops=4 * chunks * rows * width * chunk, bytes_accessed=chunks * chunk * (4 * width + 2 * rows), transcendentals=0
        ),
    )(y[None].astype(jnp.int32), x_own, x_in, query_weight, wq_in)


def order_kernel(at_ref, *refs):
    pieces, o_ref, scratch_ref = refs[:4], refs[4], refs[5]
    depth = pieces[0].shape[0]
    for k in range(4):
        place = lax.rem(at_ref[0] - k + 4, 4)
        scratch_ref[pl.ds(pl.multiple_of(place * depth, depth), depth), :] = pieces[k][...].astype(jnp.float32)
    o_ref[...] = scratch_ref[...].T.astype(jnp.bfloat16)


def ordered_rows(at, pieces):
    depth, rows = pieces[0].shape
    return pl.pallas_call(
        order_kernel,
        out_shape=jax.ShapeDtypeStruct((rows, 4 * depth), jnp.bfloat16),
        in_specs=[pl.BlockSpec(memory_space=pltpu.SMEM)] + [pl.BlockSpec(memory_space=pltpu.VMEM)] * 4,
        out_specs=pl.BlockSpec(memory_space=pltpu.VMEM),
        scratch_shapes=[pltpu.VMEM((4 * depth, rows), jnp.float32)],
        cost_estimate=pl.CostEstimate(flops=0, bytes_accessed=16 * depth * rows, transcendentals=0),
    )(at[None].astype(jnp.int32), *pieces)


def dot(a, b):
    return jnp.dot(a, b, preferred_element_type=jnp.float32)


def shards(hidden, norm_gain, router_weight, query_weight, key_value_weight, out_weight, kept_rows):
    bf16 = jnp.bfloat16
    shard = lax.axis_index("ctx")
    tp = lax.axis_index("tp")
    shard_n = lax.axis_size("ctx")
    z, y = tp // 2, tp % 2
    tokens, width = hidden.shape
    rows = kept_rows.shape[1]
    half_cols = query_weight.shape[1] // 2
    chunk = half_cols // ZN

    group = 2 * ZN // 2
    groups = [list(range(g, g + group)) for g in range(0, shard_n, group)]
    mine = shard % group

    def share(got):
        return lax.all_gather(got, "ctx", axis=0, tiled=False, axis_index_groups=groups)

    wq_sent = lax.dynamic_slice(query_weight, (0, (1 - y) * half_cols + mine * chunk), (width, chunk))
    wq_got = lax.ppermute(wq_sent, "tp", y_swap())

    own_rows = lax.dynamic_slice_in_dim(kept_rows, shard, 1, 0)
    x_own, sent = rows_and_sums(own_rows, hidden, norm_gain, router_weight, key_value_weight)
    x_own, sent, wq_got = lax.optimization_barrier((x_own, sent, wq_got))
    x_in = lax.ppermute(x_own, "tp", y_swap())

    sent, x_in = lax.optimization_barrier((sent, x_in))
    wq_in = share(wq_got)
    exchanged = lax.all_to_all(sent, "tp", 0, 0, tiled=True)
    part = query_parts(y, x_own, x_in, query_weight, wq_in)
    x_n = shard_n // 4
    at_y, at_x, core = shard // (2 * x_n), shard // 2 % x_n, shard % 2
    offsets = [(0, 0), (-1, 0), (1, 0), (0, 1), (-1, 1), (1, 1), (2, 0), (2, 1)]
    ids = [(at_y + dy) % 2 * (2 * x_n) + (at_x + dx) % x_n * 2 for dx, dy in offsets]
    ids = jnp.stack([i + core for i in ids] + [i + 1 - core for i in ids])
    counts = jnp.sum((kept_rows < tokens).astype(jnp.int32), axis=1)
    info = packing(counts, shard, ids)
    exchanged, part, info = lax.optimization_barrier((exchanged, part, info))
    query_sum = lax.psum_scatter(
        part, "tp", scatter_dimension=0, axis_index_groups=[[2 * k + h for k in range(ZN)] for h in range(2)]
    )
    summed = jnp.sum(exchanged.astype(jnp.float32), axis=0)
    square_sum = summed[HD // 2] + summed[HD // 2 + 2]
    router_logit = summed[HD // 2 + 1] + summed[HD // 2 + 3]
    inverse_rms = lax.rsqrt(square_sum / D + EPSILON)
    piece = (summed[: HD // 2] * inverse_rms[None, :]).astype(bf16)
    pieces = [lax.ppermute(piece, "tp", quad_shift(k)) for k in (1, 2, 3)]
    pieces = [piece] + pieces
    kv_own = ordered_rows(z % 4, pieces)


    def along(step):
        return [(c, c // (2 * x_n) * (2 * x_n) + (c + 2 * step) % (2 * x_n)) for c in range(shard_n)]

    def x_hop(block, step):
        return lax.ppermute(block, "ctx", along(step))

    middle = rows // 2
    over = lax.ppermute(kv_own, "ctx", [(c, (c + shard_n // 2) % shard_n) for c in range(shard_n)])
    near_left, near_right, over = lax.optimization_barrier((x_hop(kv_own, 1), x_hop(kv_own, -1), over))
    first_half = jnp.stack([kv_own, near_left, near_right, over])
    far = x_hop(near_left[:middle], 1), x_hop(near_right[middle:], -1)
    over_left, over_right = x_hop(over, 1), x_hop(over, -1)
    wo_rows = out_weight.shape[0] // 2
    wo_start = (1 - y) * wo_rows + mine * chunk
    near_left, wo_start = lax.optimization_barrier((near_left, wo_start))
    wo_got = lax.ppermute(lax.dynamic_slice(out_weight, (wo_start, 0), (chunk, width)), "tp", y_swap())
    over_left, over_right, far, wo_got = lax.optimization_barrier((over_left, over_right, far, wo_got))
    wo_in = share(wo_got).reshape(wo_rows, width)
    over_far = x_hop(over_left[:middle], 1), x_hop(over_right[middle:], -1)
    second_half = jnp.stack([over_left, over_right, jnp.concatenate(far), jnp.concatenate(over_far)])

    def core_hop(block):
        return lax.ppermute(block, "ctx", [(c, c ^ 1) for c in range(shard_n)])

    kv_all = [first_half, second_half, core_hop(first_half), core_hop(second_half)]
    def right(a):
        return lax.ppermute(a.astype(bf16), "tp", z_shift(1))

    def left(a):
        return lax.ppermute(a.astype(bf16), "tp", z_shift(-1))

    def both(going_right, going_left):
        return lax.optimization_barrier((right(going_right), left(going_left)))

    cut = chunk // 2
    queries = (query_sum.astype(jnp.float32) * (inverse_rms * EXP_SCALE)[:, None]).astype(bf16)

    mixed = attention(info, queries, kv_all)

    def project(piece, offset, low, high):
        start = ((z + offset) % ZN) * chunk + low
        own_w = lax.dynamic_slice(out_weight, (y * wo_rows + start, 0), (high - low, width))
        in_w = lax.dynamic_slice(wo_in, (start, 0), (high - low, width))
        return dot(piece, own_w), dot(piece, in_w)

    terms = [project(mixed, 0, 0, chunk)]
    from_left, from_right = mixed, mixed
    for step in (1, 2, 3):
        from_left, from_right = both(from_left, from_right)
        terms.append(project(from_left, -step, 0, chunk))
        terms.append(project(from_right, step, 0, chunk))
    for_partner = functools.reduce(jnp.add, [t[1] for t in terms]).astype(bf16)
    far = right(from_left[:, :cut]), left(from_right[:, cut:])
    received = lax.ppermute(for_partner, "tp", y_swap())
    far = jnp.concatenate(far, axis=1)
    far_in = lax.ppermute(far, "tp", y_swap())
    far_start = (z + 4) % ZN * chunk
    far_weights = lax.dynamic_slice(out_weight, (y * wo_rows + far_start, 0), (chunk, width))
    far_in_weights = lax.dynamic_slice(out_weight, ((1 - y) * wo_rows + far_start, 0), (chunk, width))
    own_sum = functools.reduce(jnp.add, [t[0] for t in terms]) + dot(far, far_weights)
    own_sum, received, far_in, far_in_weights = lax.optimization_barrier((own_sum, received, far_in, far_in_weights))
    projected = own_sum + received + dot(far_in, far_in_weights)
    row_update = (jax.nn.sigmoid(router_logit)[:, None] * projected).astype(bf16)
    select = (own_rows.reshape(rows, 1) == jnp.arange(tokens, dtype=jnp.int32)[None, :]).astype(bf16)
    return lax.dot_general(select, row_update, (((0,), (0,)), ((), ())), preferred_element_type=jnp.float32).astype(
        bf16
    )


def solution(mesh):
    return jax.shard_map(
        shards,
        mesh=mesh,
        in_specs=(
            P("ctx", "tp"),
            P("tp"),
            P("tp"),
            P("tp", None),
            P(None, "tp", None),
            P(None, "tp"),
            P(),
        ),
        out_specs=P("ctx", "tp"),
        check_vma=False,
    )
```

```python
import functools

import jax
import jax.numpy as jnp
from jax import lax
from jax.experimental import pallas as pl
from jax.experimental.pallas import tpu as pltpu
from jax.sharding import PartitionSpec as P

D = 8192
H = 32
KVH = 4
HD = 128
ZN = 8
EPSILON = 1e-05
MASKED_SCORE = -1e30
EXP_SCALE = HD ** (-0.5) * 1.4426950408889634
KEY_BLOCK = 1024
ROW_TILE = 512
ATTENTION_VMEM = 32 * 1024 * 1024


def z_shift(dz):
    return [(z * 2 + y, ((z + dz) % ZN) * 2 + y) for z in range(ZN) for y in range(2)]


def y_swap():
    return [(t, t ^ 1) for t in range(2 * ZN)]


def quad_shift(k):
    def target(z):
        return (z // 4) * 4 + (z % 4 + k) % 4

    return [(z * 2 + y, target(z) * 2 + y) for z in range(ZN) for y in range(2)]


def attention_kernel(info_ref, q_ref, *refs):
    kv_refs, (o_ref, qa_ref, ka_ref, v_ref) = refs[:-4], refs[-4:]
    blocks_each, rows, _ = kv_refs[0].shape
    order = [(array, place) for array in range(len(kv_refs)) for place in range(blocks_each)]
    order = order[1:] + order[:1]
    count = info_ref[len(order) - 1, 1]
    first = pl.multiple_of(info_ref[len(order) - 1, 2], 16)

    for index, (array, place) in enumerate(order):

        @pl.when(info_ref[index, 0] > 0)
        def _():
            start = pl.multiple_of(info_ref[index, 2], 16)
            slot = lax.broadcasted_iota(jnp.int32, (rows, HD), 0)
            bias = jnp.where(slot < info_ref[index, 1], 0.0, MASKED_SCORE)
            ka_ref[pl.ds(start, rows), :HD] = kv_refs[array][place, :, :HD]
            ka_ref[pl.ds(start, rows), HD:] = bias.astype(jnp.bfloat16)
            v_ref[pl.ds(start, rows), :] = kv_refs[array][place, :, HD:]

    tail = pl.multiple_of(first + rows, 16)
    ka_ref[pl.ds(tail, KEY_BLOCK), :] = jnp.zeros((KEY_BLOCK, 2 * HD), jnp.bfloat16)
    v_ref[pl.ds(tail, KEY_BLOCK), :] = jnp.zeros((KEY_BLOCK, HD), jnp.bfloat16)
    one = (lax.broadcasted_iota(jnp.int32, (rows, HD), 1) == 0).astype(jnp.bfloat16)
    for head in range(2):
        qa_ref[head, :, :HD] = q_ref[:, head * HD : (head + 1) * HD]
        qa_ref[head, :, HD:] = one
    open_blocks = first // KEY_BLOCK
    blocks = (first + count + KEY_BLOCK - 1) // KEY_BLOCK

    def lane_tiles(array):
        return [array[:, i * HD : (i + 1) * HD] for i in range(KEY_BLOCK // HD)]

    def tile_work(tile):
        base = tile * ROW_TILE

        def scores(block, head, masked):
            start = pl.multiple_of(block * KEY_BLOCK, KEY_BLOCK)
            out = lax.dot_general(
                qa_ref[head, base : base + ROW_TILE, :],
                ka_ref[pl.ds(start, KEY_BLOCK), :],
                (((1,), (1,)), ((), ())),
                preferred_element_type=jnp.float32,
            )
            if masked:
                key = lax.broadcasted_iota(jnp.int32, out.shape, 1)
                query = lax.broadcasted_iota(jnp.int32, out.shape, 0)
                out = jnp.where(key - query <= first + base - start, out, MASKED_SCORE)
            return out

        def body(masked):
            def run(block, state):
                start = pl.multiple_of(block * KEY_BLOCK, KEY_BLOCK)
                new = []
                for head in range(2):
                    peak, total, acc = state[3 * head : 3 * head + 3]
                    score = scores(block, head, masked)
                    lanes = functools.reduce(jnp.maximum, lane_tiles(score))
                    new_peak = jnp.maximum(peak, jnp.max(lanes, axis=1, keepdims=True))
                    weights = jnp.exp2(score - new_peak)
                    rescale = jnp.exp2(peak - new_peak)
                    new.append(new_peak)
                    new.append(functools.reduce(jnp.add, lane_tiles(weights), total * rescale))
                    new.append(
                        acc * rescale
                        + jnp.dot(
                            weights.astype(jnp.bfloat16),
                            v_ref[pl.ds(start, KEY_BLOCK), :],
                            preferred_element_type=jnp.float32,
                        )
                    )
                return tuple(new)

            return run

        zero = jnp.zeros((ROW_TILE, HD), jnp.float32)
        state = (jnp.full((ROW_TILE, 1), MASKED_SCORE, jnp.float32), zero, zero) * 2
        state = lax.fori_loop(0, open_blocks, body(False), state)
        state = lax.fori_loop(open_blocks, blocks, body(True), state)
        for head in range(2):
            total = jnp.sum(state[3 * head + 1], axis=1, keepdims=True)
            o_ref[base : base + ROW_TILE, head * HD : (head + 1) * HD] = (state[3 * head + 2] / total).astype(
                jnp.bfloat16
            )

    for tile in range(rows // ROW_TILE):
        if tile == 0:
            tile_work(tile)
        else:

            @pl.when(tile * ROW_TILE < count)
            def _():
                tile_work(tile)

            @pl.when(tile * ROW_TILE >= count)
            def _():
                o_ref[tile * ROW_TILE : (tile + 1) * ROW_TILE, :] = jnp.zeros((ROW_TILE, 2 * HD), jnp.bfloat16)


def packing(counts, own, ids):
    shards_n = ids.shape[0]
    ids = jnp.concatenate([ids[1:], ids[:1]])
    used = ids <= own
    held = jnp.sum(jnp.where(ids[:, None] == jnp.arange(shards_n)[None, :], counts[None, :], 0), axis=1)
    packed = jnp.where(used, (held + 15) // 16 * 16, 0)
    before = jnp.arange(shards_n)[None, :] < jnp.arange(shards_n)[:, None]
    first = jnp.sum(jnp.where(before, packed[None, :], 0), axis=1)
    return jnp.stack([used.astype(jnp.int32), held, first], axis=1).astype(jnp.int32)


def attention(info, queries, kv):
    blocks_each, rows, _ = kv[0].shape
    shards_n = blocks_each * len(kv)
    capacity = shards_n * (rows // 2 + 16) + rows + KEY_BLOCK
    return pl.pallas_call(
        attention_kernel,
        out_shape=jax.ShapeDtypeStruct(queries.shape, jnp.bfloat16),
        in_specs=[pl.BlockSpec(memory_space=pltpu.SMEM)]
        + [pl.BlockSpec(memory_space=pltpu.VMEM)] * (1 + len(kv)),
        out_specs=pl.BlockSpec(memory_space=pltpu.VMEM),
        scratch_shapes=[
            pltpu.VMEM((2, rows, 2 * HD), jnp.bfloat16),
            pltpu.VMEM((capacity, 2 * HD), jnp.bfloat16),
            pltpu.VMEM((capacity, HD), jnp.bfloat16),
        ],
        compiler_params=pltpu.CompilerParams(vmem_limit_bytes=ATTENTION_VMEM),
        cost_estimate=pl.CostEstimate(
            flops=4 * 2 * rows * HD * shards_n * rows,
            bytes_accessed=shards_n * rows * HD * 4,
            transcendentals=rows * rows * shards_n,
        ),
    )(info, queries, *kv)


def rows_kernel(rows_ref, hidden_ref, gain_ref, router_ref, kv_ref, x_ref, sent_ref):
    tokens, width = hidden_ref.shape
    rows = rows_ref.shape[1]
    token = lax.broadcasted_iota(jnp.int32, (tokens, rows), 0)
    select = jnp.where(token == rows_ref[...], 1.0, 0.0).astype(jnp.bfloat16)
    kept = lax.dot_general(select, hidden_ref[...], (((0,), (0,)), ((), ())), preferred_element_type=jnp.float32)
    normed = kept * gain_ref[...].astype(jnp.float32)
    x_ref[...] = normed.astype(jnp.bfloat16)

    def feature_sum(array):
        tiles = [array[:, i * HD : (i + 1) * HD] for i in range(width // HD)]
        return jnp.sum(functools.reduce(jnp.add, tiles).T, axis=0, keepdims=True)

    stats = jnp.concatenate([feature_sum(kept * kept), feature_sum(kept * router_ref[...].astype(jnp.float32))])
    high = stats.astype(jnp.bfloat16).astype(jnp.float32)
    stats = jnp.concatenate([high, stats - high, jnp.zeros((4, rows), jnp.float32)])
    turned = normed.T.astype(jnp.bfloat16)
    depth = sent_ref.shape[1] - stats.shape[0]
    halves = HD // depth
    for which in range(2):
        sums = lax.dot_general(
            kv_ref[which], turned, (((0,), (0,)), ((), ())), preferred_element_type=jnp.float32
        )
        for group in range(KVH):
            for half in range(halves):
                start = group * HD + half * depth
                place = ((group % 2 * 2 + which) * halves + half) * 2 + group // 2
                sent_ref[place] = jnp.concatenate([sums[start : start + depth], stats]).astype(jnp.bfloat16)


def rows_and_sums(own_rows, hidden, norm_gain, router_weight, key_value_weight):
    rows, (_, width) = own_rows.shape[1], hidden.shape
    return pl.pallas_call(
        rows_kernel,
        out_shape=(
            jax.ShapeDtypeStruct((rows, width), jnp.bfloat16),
            jax.ShapeDtypeStruct((2 * ZN, HD // 2 + 8, rows), jnp.bfloat16),
        ),
        in_specs=[pl.BlockSpec(memory_space=pltpu.VMEM)] * 5,
        out_specs=(pl.BlockSpec(memory_space=pltpu.VMEM),) * 2,
        compiler_params=pltpu.CompilerParams(vmem_limit_bytes=24 * 1024 * 1024),
        cost_estimate=pl.CostEstimate(
            flops=4 * rows * width * hidden.shape[0], bytes_accessed=5 * 1024 * 1024, transcendentals=0
        ),
    )(own_rows, hidden, norm_gain.reshape(1, width), router_weight.reshape(1, width), key_value_weight)


def query_kernel(y_ref, x_own_ref, x_in_ref, w_own_ref, w_in_ref, o_ref):
    o_ref[0] = (dot(x_own_ref[...], w_own_ref[...]) + dot(x_in_ref[...], w_in_ref[0])).astype(jnp.bfloat16)


def query_parts(y, x_own, x_in, query_weight, wq_in):
    chunks, width, chunk = wq_in.shape
    rows = x_own.shape[0]
    return pl.pallas_call(
        query_kernel,
        out_shape=jax.ShapeDtypeStruct((chunks, rows, chunk), jnp.bfloat16),
        grid_spec=pltpu.PrefetchScalarGridSpec(
            num_scalar_prefetch=1,
            grid=(chunks,),
            in_specs=[
                pl.BlockSpec((rows, width), lambda d, y: (0, 0)),
                pl.BlockSpec((rows, width), lambda d, y: (0, 0)),
                pl.BlockSpec((width, chunk), lambda d, y: (0, y[0] * chunks + d)),
                pl.BlockSpec((1, width, chunk), lambda d, y: (d, 0, 0)),
            ],
            out_specs=pl.BlockSpec((1, rows, chunk), lambda d, y: (d, 0, 0)),
        ),
        compiler_params=pltpu.CompilerParams(vmem_limit_bytes=16 * 1024 * 1024),
        cost_estimate=pl.CostEstimate(
            flops=4 * chunks * rows * width * chunk, bytes_accessed=chunks * chunk * (4 * width + 2 * rows), transcendentals=0
        ),
    )(y[None].astype(jnp.int32), x_own, x_in, query_weight, wq_in)


def order_kernel(at_ref, *refs):
    pieces, o_ref, scratch_ref = refs[:4], refs[4], refs[5]
    depth = pieces[0].shape[0]
    for k in range(4):
        place = lax.rem(at_ref[0] - k + 4, 4)
        scratch_ref[pl.ds(pl.multiple_of(place * depth, depth), depth), :] = pieces[k][...].astype(jnp.float32)
    o_ref[...] = scratch_ref[...].T.astype(jnp.bfloat16)


def ordered_rows(at, pieces):
    depth, rows = pieces[0].shape
    return pl.pallas_call(
        order_kernel,
        out_shape=jax.ShapeDtypeStruct((rows, 4 * depth), jnp.bfloat16),
        in_specs=[pl.BlockSpec(memory_space=pltpu.SMEM)] + [pl.BlockSpec(memory_space=pltpu.VMEM)] * 4,
        out_specs=pl.BlockSpec(memory_space=pltpu.VMEM),
        scratch_shapes=[pltpu.VMEM((4 * depth, rows), jnp.float32)],
        cost_estimate=pl.CostEstimate(flops=0, bytes_accessed=16 * depth * rows, transcendentals=0),
    )(at[None].astype(jnp.int32), *pieces)


def dot(a, b):
    return jnp.dot(a, b, preferred_element_type=jnp.float32)


def shards(hidden, norm_gain, router_weight, query_weight, key_value_weight, out_weight, kept_rows):
    bf16 = jnp.bfloat16
    shard = lax.axis_index("ctx")
    tp = lax.axis_index("tp")
    shard_n = lax.axis_size("ctx")
    z, y = tp // 2, tp % 2
    tokens, width = hidden.shape
    rows = kept_rows.shape[1]
    half_cols = query_weight.shape[1] // 2
    chunk = half_cols // ZN

    group = 2 * ZN // 2
    groups = [list(range(g, g + group)) for g in range(0, shard_n, group)]
    mine = shard % group

    def share(got):
        return lax.all_gather(got, "ctx", axis=0, tiled=False, axis_index_groups=groups)

    wq_sent = lax.dynamic_slice(query_weight, (0, (1 - y) * half_cols + mine * chunk), (width, chunk))
    wq_got = lax.ppermute(wq_sent, "tp", y_swap())

    own_rows = lax.dynamic_slice_in_dim(kept_rows, shard, 1, 0)
    x_own, sent = rows_and_sums(own_rows, hidden, norm_gain, router_weight, key_value_weight)
    x_in = lax.ppermute(x_own, "tp", y_swap())

    sent, wq_got = lax.optimization_barrier((sent, wq_got))
    wq_in = share(wq_got)
    exchanged = lax.all_to_all(sent, "tp", 0, 0, tiled=True)
    part = query_parts(y, x_own, x_in, query_weight, wq_in)
    x_n = shard_n // 4
    at_y, at_x, core = shard // (2 * x_n), shard // 2 % x_n, shard % 2
    offsets = [(0, 0), (-1, 0), (1, 0), (0, 1), (-1, 1), (1, 1), (2, 0), (2, 1)]
    ids = [(at_y + dy) % 2 * (2 * x_n) + (at_x + dx) % x_n * 2 for dx, dy in offsets]
    ids = jnp.stack([i + core for i in ids] + [i + 1 - core for i in ids])
    counts = jnp.sum((kept_rows < tokens).astype(jnp.int32), axis=1)
    info = packing(counts, shard, ids)
    wo_rows = out_weight.shape[0] // 2
    wo_sent = lax.dynamic_slice(out_weight, ((1 - y) * wo_rows + mine * chunk, 0), (chunk, width))
    exchanged, info, wo_sent = lax.optimization_barrier((exchanged, info, wo_sent))
    summed = jnp.sum(exchanged.astype(jnp.float32), axis=0)
    square_sum = summed[HD // 2] + summed[HD // 2 + 2]
    router_logit = summed[HD // 2 + 1] + summed[HD // 2 + 3]
    inverse_rms = lax.rsqrt(square_sum / D + EPSILON)
    piece = (summed[: HD // 2] * inverse_rms[None, :]).astype(bf16)
    pieces = [lax.ppermute(piece, "tp", quad_shift(k)) for k in (1, 2, 3)]
    pieces, part = lax.optimization_barrier(([piece] + pieces, part))
    query_sum = lax.psum_scatter(
        part, "tp", scatter_dimension=0, axis_index_groups=[[2 * k + h for k in range(ZN)] for h in range(2)]
    )
    kv_own = ordered_rows(z % 4, pieces)


    def along(step):
        return [(c, c // (2 * x_n) * (2 * x_n) + (c + 2 * step) % (2 * x_n)) for c in range(shard_n)]

    def x_hop(block, step):
        return lax.ppermute(block, "ctx", along(step))

    middle = rows // 2
    over = lax.ppermute(kv_own, "ctx", [(c, (c + shard_n // 2) % shard_n) for c in range(shard_n)])
    kv_own, wo_sent = lax.optimization_barrier((kv_own, wo_sent))
    wo_got = lax.ppermute(wo_sent, "tp", y_swap())
    near_left, near_right, over, wo_got = lax.optimization_barrier((x_hop(kv_own, 1), x_hop(kv_own, -1), over, wo_got))
    wo_in = share(wo_got).reshape(wo_rows, width)
    first_half = jnp.stack([kv_own, near_left, near_right, over])
    far = x_hop(near_left[:middle], 1), x_hop(near_right[middle:], -1)
    over_left, over_right = x_hop(over, 1), x_hop(over, -1)
    over_left, over_right, far = lax.optimization_barrier((over_left, over_right, far))
    over_far = x_hop(over_left[:middle], 1), x_hop(over_right[middle:], -1)
    second_half = jnp.stack([over_left, over_right, jnp.concatenate(far), jnp.concatenate(over_far)])

    def core_hop(block):
        return lax.ppermute(block, "ctx", [(c, c ^ 1) for c in range(shard_n)])

    kv_all = [first_half, second_half, core_hop(first_half), core_hop(second_half)]
    def right(a):
        return lax.ppermute(a.astype(bf16), "tp", z_shift(1))

    def left(a):
        return lax.ppermute(a.astype(bf16), "tp", z_shift(-1))

    def both(going_right, going_left):
        return lax.optimization_barrier((right(going_right), left(going_left)))

    cut = chunk // 2
    queries = (query_sum.astype(jnp.float32) * (inverse_rms * EXP_SCALE)[:, None]).astype(bf16)

    mixed = attention(info, queries, kv_all)

    def project(piece, offset, low, high):
        start = ((z + offset) % ZN) * chunk + low
        own_w = lax.dynamic_slice(out_weight, (y * wo_rows + start, 0), (high - low, width))
        in_w = lax.dynamic_slice(wo_in, (start, 0), (high - low, width))
        return dot(piece, own_w), dot(piece, in_w)

    terms = [project(mixed, 0, 0, chunk)]
    from_left, from_right = mixed, mixed
    for step in (1, 2, 3):
        from_left, from_right = both(from_left, from_right)
        terms.append(project(from_left, -step, 0, chunk))
        terms.append(project(from_right, step, 0, chunk))
    terms.append(project(right(from_left[:, :cut]), 4, 0, cut))
    terms.append(project(left(from_right[:, cut:]), 4, cut, chunk))
    for_partner = functools.reduce(jnp.add, [t[1] for t in terms])
    received = lax.ppermute(for_partner.astype(bf16), "tp", y_swap())
    own_sum, received = lax.optimization_barrier((functools.reduce(jnp.add, [t[0] for t in terms]), received))
    projected = own_sum + received
    row_update = (jax.nn.sigmoid(router_logit)[:, None] * projected).astype(bf16)
    select = (own_rows.reshape(rows, 1) == jnp.arange(tokens, dtype=jnp.int32)[None, :]).astype(bf16)
    return lax.dot_general(select, row_update, (((0,), (0,)), ((), ())), preferred_element_type=jnp.float32).astype(
        bf16
    )


def solution(mesh):
    return jax.shard_map(
        shards,
        mesh=mesh,
        in_specs=(
            P("ctx", "tp"),
            P("tp"),
            P("tp"),
            P("tp", None),
            P(None, "tp", None),
            P(None, "tp"),
            P(),
        ),
        out_specs=P("ctx", "tp"),
        check_vma=False,
    )
```

```python
import functools

import jax
import jax.numpy as jnp
from jax import lax
from jax.experimental import pallas as pl
from jax.experimental.pallas import tpu as pltpu
from jax.sharding import PartitionSpec as P

D = 8192
H = 32
KVH = 4
HD = 128
ZN = 8
EPSILON = 1e-05
MASKED_SCORE = -1e30
EXP_SCALE = HD ** (-0.5) * 1.4426950408889634
KEY_BLOCK = 1024
ROW_TILE = 512
ATTENTION_VMEM = 32 * 1024 * 1024
WHOLE_VMEM = 58 * 1024 * 1024


def z_shift(dz):
    return [(z * 2 + y, ((z + dz) % ZN) * 2 + y) for z in range(ZN) for y in range(2)]


def y_swap():
    return [(t, t ^ 1) for t in range(2 * ZN)]


def quad_shift(k):
    def target(z):
        return (z // 4) * 4 + (z % 4 + k) % 4

    return [(z * 2 + y, target(z) * 2 + y) for z in range(ZN) for y in range(2)]


def attention_kernel(info_ref, q_ref, *refs):
    kv_refs, (o_ref, qa_ref, ka_ref, v_ref) = refs[:-4], refs[-4:]
    blocks_each, rows, _ = kv_refs[0].shape
    order = [(array, place) for array in range(len(kv_refs)) for place in range(blocks_each)]
    order = order[1:] + order[:1]
    count = info_ref[len(order) - 1, 1]
    first = pl.multiple_of(info_ref[len(order) - 1, 2], 16)

    for index, (array, place) in enumerate(order):

        @pl.when(info_ref[index, 0] > 0)
        def _():
            start = pl.multiple_of(info_ref[index, 2], 16)
            slot = lax.broadcasted_iota(jnp.int32, (rows, HD), 0)
            bias = jnp.where(slot < info_ref[index, 1], 0.0, MASKED_SCORE)
            ka_ref[pl.ds(start, rows), :HD] = kv_refs[array][place, :, :HD]
            ka_ref[pl.ds(start, rows), HD:] = bias.astype(jnp.bfloat16)
            v_ref[pl.ds(start, rows), :] = kv_refs[array][place, :, HD:]

    tail = pl.multiple_of(first + rows, 16)
    ka_ref[pl.ds(tail, KEY_BLOCK), :] = jnp.zeros((KEY_BLOCK, 2 * HD), jnp.bfloat16)
    v_ref[pl.ds(tail, KEY_BLOCK), :] = jnp.zeros((KEY_BLOCK, HD), jnp.bfloat16)
    one = (lax.broadcasted_iota(jnp.int32, (rows, HD), 1) == 0).astype(jnp.bfloat16)
    for head in range(2):
        qa_ref[head, :, :HD] = q_ref[:, head * HD : (head + 1) * HD]
        qa_ref[head, :, HD:] = one
    open_blocks = first // KEY_BLOCK
    blocks = (first + count + KEY_BLOCK - 1) // KEY_BLOCK

    def lane_tiles(array):
        return [array[:, i * HD : (i + 1) * HD] for i in range(KEY_BLOCK // HD)]

    def tile_work(tile):
        base = tile * ROW_TILE

        def scores(block, head, masked):
            start = pl.multiple_of(block * KEY_BLOCK, KEY_BLOCK)
            out = lax.dot_general(
                qa_ref[head, base : base + ROW_TILE, :],
                ka_ref[pl.ds(start, KEY_BLOCK), :],
                (((1,), (1,)), ((), ())),
                preferred_element_type=jnp.float32,
            )
            if masked:
                key = lax.broadcasted_iota(jnp.int32, out.shape, 1)
                query = lax.broadcasted_iota(jnp.int32, out.shape, 0)
                out = jnp.where(key - query <= first + base - start, out, MASKED_SCORE)
            return out

        def body(masked):
            def run(block, state):
                start = pl.multiple_of(block * KEY_BLOCK, KEY_BLOCK)
                new = []
                for head in range(2):
                    peak, total, acc = state[3 * head : 3 * head + 3]
                    score = scores(block, head, masked)
                    lanes = functools.reduce(jnp.maximum, lane_tiles(score))
                    new_peak = jnp.maximum(peak, jnp.max(lanes, axis=1, keepdims=True))
                    weights = jnp.exp2(score - new_peak)
                    rescale = jnp.exp2(peak - new_peak)
                    new.append(new_peak)
                    new.append(functools.reduce(jnp.add, lane_tiles(weights), total * rescale))
                    new.append(
                        acc * rescale
                        + jnp.dot(
                            weights.astype(jnp.bfloat16),
                            v_ref[pl.ds(start, KEY_BLOCK), :],
                            preferred_element_type=jnp.float32,
                        )
                    )
                return tuple(new)

            return run

        zero = jnp.zeros((ROW_TILE, HD), jnp.float32)
        state = (jnp.full((ROW_TILE, 1), MASKED_SCORE, jnp.float32), zero, zero) * 2
        state = lax.fori_loop(0, open_blocks, body(False), state)
        state = lax.fori_loop(open_blocks, blocks, body(True), state)
        for head in range(2):
            total = jnp.sum(state[3 * head + 1], axis=1, keepdims=True)
            o_ref[base : base + ROW_TILE, head * HD : (head + 1) * HD] = (state[3 * head + 2] / total).astype(
                jnp.bfloat16
            )

    for tile in range(rows // ROW_TILE):
        if tile == 0:
            tile_work(tile)
        else:

            @pl.when(tile * ROW_TILE < count)
            def _():
                tile_work(tile)

            @pl.when(tile * ROW_TILE >= count)
            def _():
                o_ref[tile * ROW_TILE : (tile + 1) * ROW_TILE, :] = jnp.zeros((ROW_TILE, 2 * HD), jnp.bfloat16)


def packing(counts, own, ids):
    shards_n = ids.shape[0]
    ids = jnp.concatenate([ids[1:], ids[:1]])
    used = ids <= own
    held = jnp.sum(jnp.where(ids[:, None] == jnp.arange(shards_n)[None, :], counts[None, :], 0), axis=1)
    packed = jnp.where(used, (held + 15) // 16 * 16, 0)
    before = jnp.arange(shards_n)[None, :] < jnp.arange(shards_n)[:, None]
    first = jnp.sum(jnp.where(before, packed[None, :], 0), axis=1)
    return jnp.stack([used.astype(jnp.int32), held, first], axis=1).astype(jnp.int32)


def attention(info, queries, kv):
    blocks_each, rows, _ = kv[0].shape
    shards_n = blocks_each * len(kv)
    capacity = shards_n * (rows // 2 + 16) + rows + KEY_BLOCK
    return pl.pallas_call(
        attention_kernel,
        out_shape=jax.ShapeDtypeStruct(queries.shape, jnp.bfloat16),
        in_specs=[pl.BlockSpec(memory_space=pltpu.SMEM)]
        + [pl.BlockSpec(memory_space=pltpu.VMEM)] * (1 + len(kv)),
        out_specs=pl.BlockSpec(memory_space=pltpu.VMEM),
        scratch_shapes=[
            pltpu.VMEM((2, rows, 2 * HD), jnp.bfloat16),
            pltpu.VMEM((capacity, 2 * HD), jnp.bfloat16),
            pltpu.VMEM((capacity, HD), jnp.bfloat16),
        ],
        compiler_params=pltpu.CompilerParams(vmem_limit_bytes=ATTENTION_VMEM),
        cost_estimate=pl.CostEstimate(
            flops=4 * 2 * rows * HD * shards_n * rows,
            bytes_accessed=shards_n * rows * HD * 4,
            transcendentals=rows * rows * shards_n,
        ),
    )(info, queries, *kv)


def rows_kernel(rows_ref, hidden_hbm, gain_ref, router_ref, kv_hbm, x_ref, sent_ref, hidden_ref, kv_ref, sem):
    hidden_copy = pltpu.make_async_copy(hidden_hbm, hidden_ref, sem.at[0])
    kv_copy = pltpu.make_async_copy(kv_hbm, kv_ref, sem.at[1])
    hidden_copy.start()
    kv_copy.start()
    tokens, width = hidden_ref.shape
    rows = rows_ref.shape[1]
    token = lax.broadcasted_iota(jnp.int32, (tokens, rows), 0)
    select = jnp.where(token == rows_ref[...], 1.0, 0.0).astype(jnp.bfloat16)
    hidden_copy.wait()
    kept = lax.dot_general(select, hidden_ref[...], (((0,), (0,)), ((), ())), preferred_element_type=jnp.float32)
    normed = kept * gain_ref[...].astype(jnp.float32)
    x_ref[...] = normed.astype(jnp.bfloat16)

    def feature_sum(array):
        tiles = [array[:, i * HD : (i + 1) * HD] for i in range(width // HD)]
        return jnp.sum(functools.reduce(jnp.add, tiles).T, axis=0, keepdims=True)

    stats = jnp.concatenate([feature_sum(kept * kept), feature_sum(kept * router_ref[...].astype(jnp.float32))])
    high = stats.astype(jnp.bfloat16).astype(jnp.float32)
    stats = jnp.concatenate([high, stats - high, jnp.zeros((4, rows), jnp.float32)])
    turned = normed.T.astype(jnp.bfloat16)
    depth = sent_ref.shape[1] - stats.shape[0]
    halves = HD // depth
    kv_copy.wait()
    for which in range(2):
        sums = lax.dot_general(
            kv_ref[which], turned, (((0,), (0,)), ((), ())), preferred_element_type=jnp.float32
        )
        for group in range(KVH):
            for half in range(halves):
                start = group * HD + half * depth
                place = ((group % 2 * 2 + which) * halves + half) * 2 + group // 2
                sent_ref[place] = jnp.concatenate([sums[start : start + depth], stats]).astype(jnp.bfloat16)


def rows_and_sums(own_rows, hidden, norm_gain, router_weight, key_value_weight):
    rows, (_, width) = own_rows.shape[1], hidden.shape
    return pl.pallas_call(
        rows_kernel,
        out_shape=(
            jax.ShapeDtypeStruct((rows, width), jnp.bfloat16),
            jax.ShapeDtypeStruct((2 * ZN, HD // 2 + 8, rows), jnp.bfloat16),
        ),
        in_specs=[
            pl.BlockSpec(memory_space=pltpu.VMEM),
            pl.BlockSpec(memory_space=pl.ANY),
            pl.BlockSpec(memory_space=pltpu.VMEM),
            pl.BlockSpec(memory_space=pltpu.VMEM),
            pl.BlockSpec(memory_space=pl.ANY),
        ],
        out_specs=(pl.BlockSpec(memory_space=pltpu.VMEM),) * 2,
        scratch_shapes=[
            pltpu.VMEM(hidden.shape, jnp.bfloat16),
            pltpu.VMEM(key_value_weight.shape, jnp.bfloat16),
            pltpu.SemaphoreType.DMA((2,)),
        ],
        compiler_params=pltpu.CompilerParams(vmem_limit_bytes=WHOLE_VMEM),
        cost_estimate=pl.CostEstimate(
            flops=4 * rows * width * hidden.shape[0], bytes_accessed=5 * 1024 * 1024, transcendentals=0
        ),
    )(own_rows, hidden, norm_gain.reshape(1, width), router_weight.reshape(1, width), key_value_weight)


def query_kernel(y_ref, x_own_ref, x_in_ref, w_own_ref, w_in_ref, o_ref):
    o_ref[0] = (dot(x_own_ref[...], w_own_ref[...]) + dot(x_in_ref[...], w_in_ref[0])).astype(jnp.bfloat16)


def query_parts(y, x_own, x_in, query_weight, wq_in):
    chunks, width, chunk = wq_in.shape
    rows = x_own.shape[0]
    return pl.pallas_call(
        query_kernel,
        out_shape=jax.ShapeDtypeStruct((chunks, rows, chunk), jnp.bfloat16),
        grid_spec=pltpu.PrefetchScalarGridSpec(
            num_scalar_prefetch=1,
            grid=(chunks,),
            in_specs=[
                pl.BlockSpec((rows, width), lambda d, y: (0, 0)),
                pl.BlockSpec((rows, width), lambda d, y: (0, 0)),
                pl.BlockSpec((width, chunk), lambda d, y: (0, y[0] * chunks + d)),
                pl.BlockSpec((1, width, chunk), lambda d, y: (d, 0, 0)),
            ],
            out_specs=pl.BlockSpec((1, rows, chunk), lambda d, y: (d, 0, 0)),
        ),
        compiler_params=pltpu.CompilerParams(vmem_limit_bytes=WHOLE_VMEM),
        cost_estimate=pl.CostEstimate(
            flops=4 * chunks * rows * width * chunk, bytes_accessed=chunks * chunk * (4 * width + 2 * rows), transcendentals=0
        ),
    )(y[None].astype(jnp.int32), x_own, x_in, query_weight, wq_in)


def order_kernel(at_ref, *refs):
    pieces, o_ref, scratch_ref = refs[:4], refs[4], refs[5]
    depth = pieces[0].shape[0]
    for k in range(4):
        place = lax.rem(at_ref[0] - k + 4, 4)
        scratch_ref[pl.ds(pl.multiple_of(place * depth, depth), depth), :] = pieces[k][...].astype(jnp.float32)
    o_ref[...] = scratch_ref[...].T.astype(jnp.bfloat16)


def ordered_rows(at, pieces):
    depth, rows = pieces[0].shape
    return pl.pallas_call(
        order_kernel,
        out_shape=jax.ShapeDtypeStruct((rows, 4 * depth), jnp.bfloat16),
        in_specs=[pl.BlockSpec(memory_space=pltpu.SMEM)] + [pl.BlockSpec(memory_space=pltpu.VMEM)] * 4,
        out_specs=pl.BlockSpec(memory_space=pltpu.VMEM),
        scratch_shapes=[pltpu.VMEM((4 * depth, rows), jnp.float32)],
        cost_estimate=pl.CostEstimate(flops=0, bytes_accessed=16 * depth * rows, transcendentals=0),
    )(at[None].astype(jnp.int32), *pieces)


def dot(a, b):
    return jnp.dot(a, b, preferred_element_type=jnp.float32)


def shards(hidden, norm_gain, router_weight, query_weight, key_value_weight, out_weight, kept_rows):
    bf16 = jnp.bfloat16
    shard = lax.axis_index("ctx")
    tp = lax.axis_index("tp")
    shard_n = lax.axis_size("ctx")
    z, y = tp // 2, tp % 2
    tokens, width = hidden.shape
    rows = kept_rows.shape[1]
    half_cols = query_weight.shape[1] // 2
    chunk = half_cols // ZN

    group = 2 * ZN // 2
    groups = [list(range(g, g + group)) for g in range(0, shard_n, group)]
    mine = shard % group

    def share(got):
        return lax.all_gather(got, "ctx", axis=0, tiled=False, axis_index_groups=groups)

    wq_sent = lax.dynamic_slice(query_weight, (0, (1 - y) * half_cols + mine * chunk), (width, chunk))
    wq_got = lax.ppermute(wq_sent, "tp", y_swap())

    own_rows = lax.dynamic_slice_in_dim(kept_rows, shard, 1, 0)
    x_own, sent = rows_and_sums(own_rows, hidden, norm_gain, router_weight, key_value_weight)
    x_in = lax.ppermute(x_own, "tp", y_swap())

    sent, wq_got = lax.optimization_barrier((sent, wq_got))
    wq_in = share(wq_got)
    exchanged = lax.all_to_all(sent, "tp", 0, 0, tiled=True)
    part = query_parts(y, x_own, x_in, query_weight, wq_in)
    x_n = shard_n // 4
    at_y, at_x, core = shard // (2 * x_n), shard // 2 % x_n, shard % 2
    offsets = [(0, 0), (-1, 0), (1, 0), (0, 1), (-1, 1), (1, 1), (2, 0), (2, 1)]
    ids = [(at_y + dy) % 2 * (2 * x_n) + (at_x + dx) % x_n * 2 for dx, dy in offsets]
    ids = jnp.stack([i + core for i in ids] + [i + 1 - core for i in ids])
    counts = jnp.sum((kept_rows < tokens).astype(jnp.int32), axis=1)
    info = packing(counts, shard, ids)
    wo_rows = out_weight.shape[0] // 2
    wo_sent = lax.dynamic_slice(out_weight, ((1 - y) * wo_rows + mine * chunk, 0), (chunk, width))
    exchanged, info, wo_sent = lax.optimization_barrier((exchanged, info, wo_sent))
    summed = jnp.sum(exchanged.astype(jnp.float32), axis=0)
    square_sum = summed[HD // 2] + summed[HD // 2 + 2]
    router_logit = summed[HD // 2 + 1] + summed[HD // 2 + 3]
    inverse_rms = lax.rsqrt(square_sum / D + EPSILON)
    piece = (summed[: HD // 2] * inverse_rms[None, :]).astype(bf16)
    piece, wo_sent = lax.optimization_barrier((piece, wo_sent))
    pieces = [lax.ppermute(piece, "tp", quad_shift(k)) for k in (1, 2, 3)]
    wo_got = lax.ppermute(wo_sent, "tp", y_swap())
    pieces, part, wo_got = lax.optimization_barrier(([piece] + pieces, part, wo_got))
    query_sum = lax.psum_scatter(
        part, "tp", scatter_dimension=0, axis_index_groups=[[2 * k + h for k in range(ZN)] for h in range(2)]
    )
    query_sum, wo_got = lax.optimization_barrier((query_sum, wo_got))
    wo_in = share(wo_got).reshape(wo_rows, width)
    kv_own = ordered_rows(z % 4, pieces)


    def along(step):
        return [(c, c // (2 * x_n) * (2 * x_n) + (c + 2 * step) % (2 * x_n)) for c in range(shard_n)]

    def x_hop(block, step):
        return lax.ppermute(block, "ctx", along(step))

    middle = rows // 2
    over = lax.ppermute(kv_own, "ctx", [(c, (c + shard_n // 2) % shard_n) for c in range(shard_n)])
    near_left, near_right, over = lax.optimization_barrier((x_hop(kv_own, 1), x_hop(kv_own, -1), over))
    first_half = jnp.stack([kv_own, near_left, near_right, over])
    far = x_hop(near_left[:middle], 1), x_hop(near_right[middle:], -1)
    over_left, over_right = x_hop(over, 1), x_hop(over, -1)
    over_left, over_right, far = lax.optimization_barrier((over_left, over_right, far))
    over_far = x_hop(over_left[:middle], 1), x_hop(over_right[middle:], -1)
    second_half = jnp.stack([over_left, over_right, jnp.concatenate(far), jnp.concatenate(over_far)])

    def core_hop(block):
        return lax.ppermute(block, "ctx", [(c, c ^ 1) for c in range(shard_n)])

    kv_all = [first_half, second_half, core_hop(first_half), core_hop(second_half)]
    def right(a):
        return lax.ppermute(a.astype(bf16), "tp", z_shift(1))

    def left(a):
        return lax.ppermute(a.astype(bf16), "tp", z_shift(-1))

    def both(going_right, going_left):
        return lax.optimization_barrier((right(going_right), left(going_left)))

    cut = chunk // 2
    queries = (query_sum.astype(jnp.float32) * (inverse_rms * EXP_SCALE)[:, None]).astype(bf16)

    mixed = attention(info, queries, kv_all)

    def project(piece, offset, low, high):
        start = ((z + offset) % ZN) * chunk + low
        own_w = lax.dynamic_slice(out_weight, (y * wo_rows + start, 0), (high - low, width))
        in_w = lax.dynamic_slice(wo_in, (start, 0), (high - low, width))
        return dot(piece, own_w), dot(piece, in_w)

    terms = [project(mixed, 0, 0, chunk)]
    from_left, from_right = mixed, mixed
    for step in (1, 2, 3):
        from_left, from_right = both(from_left, from_right)
        terms.append(project(from_left, -step, 0, chunk))
        terms.append(project(from_right, step, 0, chunk))
    terms.append(project(right(from_left[:, :cut]), 4, 0, cut))
    terms.append(project(left(from_right[:, cut:]), 4, cut, chunk))
    for_partner = functools.reduce(jnp.add, [t[1] for t in terms])
    received = lax.ppermute(for_partner.astype(bf16), "tp", y_swap())
    own_sum, received = lax.optimization_barrier((functools.reduce(jnp.add, [t[0] for t in terms]), received))
    projected = own_sum + received
    row_update = (jax.nn.sigmoid(router_logit)[:, None] * projected).astype(bf16)
    select = (own_rows.reshape(rows, 1) == jnp.arange(tokens, dtype=jnp.int32)[None, :]).astype(bf16)
    return lax.dot_general(select, row_update, (((0,), (0,)), ((), ())), preferred_element_type=jnp.float32).astype(
        bf16
    )


def solution(mesh):
    return jax.shard_map(
        shards,
        mesh=mesh,
        in_specs=(
            P("ctx", "tp"),
            P("tp"),
            P("tp"),
            P("tp", None),
            P(None, "tp", None),
            P(None, "tp"),
            P(),
        ),
        out_specs=P("ctx", "tp"),
        check_vma=False,
    )
```

```python
import functools

import jax
import jax.numpy as jnp
from jax import lax
from jax.experimental import pallas as pl
from jax.experimental.pallas import tpu as pltpu
from jax.sharding import PartitionSpec as P

D = 8192
H = 32
KVH = 4
HD = 128
ZN = 8
EPSILON = 1e-05
MASKED_SCORE = -1e30
EXP_SCALE = HD ** (-0.5) * 1.4426950408889634
KEY_BLOCK = 1024
ROW_TILE = 512
ATTENTION_VMEM = 32 * 1024 * 1024


def z_shift(dz):
    return [(z * 2 + y, ((z + dz) % ZN) * 2 + y) for z in range(ZN) for y in range(2)]


def y_swap():
    return [(t, t ^ 1) for t in range(2 * ZN)]


def quad_shift(k):
    def target(z):
        return (z // 4) * 4 + (z % 4 + k) % 4

    return [(z * 2 + y, target(z) * 2 + y) for z in range(ZN) for y in range(2)]


def attention_kernel(info_ref, q_ref, *refs):
    kv_refs, (o_ref, qa_ref, ka_ref, v_ref) = refs[:-4], refs[-4:]
    blocks_each, rows, _ = kv_refs[0].shape
    order = [(array, place) for array in range(len(kv_refs)) for place in range(blocks_each)]
    order = order[1:] + order[:1]
    count = info_ref[len(order) - 1, 1]
    first = pl.multiple_of(info_ref[len(order) - 1, 2], 16)

    for index, (array, place) in enumerate(order):

        @pl.when(info_ref[index, 0] > 0)
        def _():
            start = pl.multiple_of(info_ref[index, 2], 16)
            slot = lax.broadcasted_iota(jnp.int32, (rows, HD), 0)
            bias = jnp.where(slot < info_ref[index, 1], 0.0, MASKED_SCORE)
            ka_ref[pl.ds(start, rows), :HD] = kv_refs[array][place, :, :HD]
            ka_ref[pl.ds(start, rows), HD:] = bias.astype(jnp.bfloat16)
            v_ref[pl.ds(start, rows), :] = kv_refs[array][place, :, HD:]

    tail = pl.multiple_of(first + rows, 16)
    ka_ref[pl.ds(tail, KEY_BLOCK), :] = jnp.zeros((KEY_BLOCK, 2 * HD), jnp.bfloat16)
    v_ref[pl.ds(tail, KEY_BLOCK), :] = jnp.zeros((KEY_BLOCK, HD), jnp.bfloat16)
    one = (lax.broadcasted_iota(jnp.int32, (rows, HD), 1) == 0).astype(jnp.bfloat16)
    for head in range(2):
        qa_ref[head, :, :HD] = q_ref[:, head * HD : (head + 1) * HD]
        qa_ref[head, :, HD:] = one
    open_blocks = first // KEY_BLOCK
    blocks = (first + count + KEY_BLOCK - 1) // KEY_BLOCK

    def lane_tiles(array):
        return [array[:, i * HD : (i + 1) * HD] for i in range(KEY_BLOCK // HD)]

    def tile_work(tile):
        base = tile * ROW_TILE

        def scores(block, head, masked):
            start = pl.multiple_of(block * KEY_BLOCK, KEY_BLOCK)
            out = lax.dot_general(
                qa_ref[head, base : base + ROW_TILE, :],
                ka_ref[pl.ds(start, KEY_BLOCK), :],
                (((1,), (1,)), ((), ())),
                preferred_element_type=jnp.float32,
            )
            if masked:
                key = lax.broadcasted_iota(jnp.int32, out.shape, 1)
                query = lax.broadcasted_iota(jnp.int32, out.shape, 0)
                out = jnp.where(key - query <= first + base - start, out, MASKED_SCORE)
            return out

        def body(masked):
            def run(block, state):
                start = pl.multiple_of(block * KEY_BLOCK, KEY_BLOCK)
                new = []
                for head in range(2):
                    peak, total, acc = state[3 * head : 3 * head + 3]
                    score = scores(block, head, masked)
                    lanes = functools.reduce(jnp.maximum, lane_tiles(score))
                    new_peak = jnp.maximum(peak, jnp.max(lanes, axis=1, keepdims=True))
                    weights = jnp.exp2(score - new_peak)
                    rescale = jnp.exp2(peak - new_peak)
                    new.append(new_peak)
                    new.append(functools.reduce(jnp.add, lane_tiles(weights), total * rescale))
                    new.append(
                        acc * rescale
                        + jnp.dot(
                            weights.astype(jnp.bfloat16),
                            v_ref[pl.ds(start, KEY_BLOCK), :],
                            preferred_element_type=jnp.float32,
                        )
                    )
                return tuple(new)

            return run

        zero = jnp.zeros((ROW_TILE, HD), jnp.float32)
        state = (jnp.full((ROW_TILE, 1), MASKED_SCORE, jnp.float32), zero, zero) * 2
        state = lax.fori_loop(0, open_blocks, body(False), state)
        state = lax.fori_loop(open_blocks, blocks, body(True), state)
        for head in range(2):
            total = jnp.sum(state[3 * head + 1], axis=1, keepdims=True)
            o_ref[base : base + ROW_TILE, head * HD : (head + 1) * HD] = (state[3 * head + 2] / total).astype(
                jnp.bfloat16
            )

    for tile in range(rows // ROW_TILE):
        if tile == 0:
            tile_work(tile)
        else:

            @pl.when(tile * ROW_TILE < count)
            def _():
                tile_work(tile)

            @pl.when(tile * ROW_TILE >= count)
            def _():
                o_ref[tile * ROW_TILE : (tile + 1) * ROW_TILE, :] = jnp.zeros((ROW_TILE, 2 * HD), jnp.bfloat16)


def packing(counts, own, ids):
    shards_n = ids.shape[0]
    ids = jnp.concatenate([ids[1:], ids[:1]])
    used = ids <= own
    held = jnp.sum(jnp.where(ids[:, None] == jnp.arange(shards_n)[None, :], counts[None, :], 0), axis=1)
    packed = jnp.where(used, (held + 15) // 16 * 16, 0)
    before = jnp.arange(shards_n)[None, :] < jnp.arange(shards_n)[:, None]
    first = jnp.sum(jnp.where(before, packed[None, :], 0), axis=1)
    return jnp.stack([used.astype(jnp.int32), held, first], axis=1).astype(jnp.int32)


def attention(info, queries, kv):
    blocks_each, rows, _ = kv[0].shape
    shards_n = blocks_each * len(kv)
    capacity = shards_n * (rows // 2 + 16) + rows + KEY_BLOCK
    return pl.pallas_call(
        attention_kernel,
        out_shape=jax.ShapeDtypeStruct(queries.shape, jnp.bfloat16),
        in_specs=[pl.BlockSpec(memory_space=pltpu.SMEM)]
        + [pl.BlockSpec(memory_space=pltpu.VMEM)] * (1 + len(kv)),
        out_specs=pl.BlockSpec(memory_space=pltpu.VMEM),
        scratch_shapes=[
            pltpu.VMEM((2, rows, 2 * HD), jnp.bfloat16),
            pltpu.VMEM((capacity, 2 * HD), jnp.bfloat16),
            pltpu.VMEM((capacity, HD), jnp.bfloat16),
        ],
        compiler_params=pltpu.CompilerParams(vmem_limit_bytes=ATTENTION_VMEM),
        cost_estimate=pl.CostEstimate(
            flops=4 * 2 * rows * HD * shards_n * rows,
            bytes_accessed=shards_n * rows * HD * 4,
            transcendentals=rows * rows * shards_n,
        ),
    )(info, queries, *kv)


def rows_kernel(rows_ref, hidden_ref, gain_ref, router_ref, kv_ref, x_ref, sent_ref):
    tokens, width = hidden_ref.shape
    rows = rows_ref.shape[1]
    token = lax.broadcasted_iota(jnp.int32, (tokens, rows), 0)
    select = jnp.where(token == rows_ref[...], 1.0, 0.0).astype(jnp.bfloat16)
    kept = lax.dot_general(select, hidden_ref[...], (((0,), (0,)), ((), ())), preferred_element_type=jnp.float32)
    normed = kept * gain_ref[...].astype(jnp.float32)
    x_ref[...] = normed.astype(jnp.bfloat16)

    def feature_sum(array):
        tiles = [array[:, i * HD : (i + 1) * HD] for i in range(width // HD)]
        return jnp.sum(functools.reduce(jnp.add, tiles).T, axis=0, keepdims=True)

    stats = jnp.concatenate([feature_sum(kept * kept), feature_sum(kept * router_ref[...].astype(jnp.float32))])
    high = stats.astype(jnp.bfloat16).astype(jnp.float32)
    stats = jnp.concatenate([high, stats - high, jnp.zeros((4, rows), jnp.float32)])
    turned = normed.T.astype(jnp.bfloat16)
    depth = sent_ref.shape[1] - stats.shape[0]
    halves = HD // depth
    for which in range(2):
        sums = lax.dot_general(
            kv_ref[which], turned, (((0,), (0,)), ((), ())), preferred_element_type=jnp.float32
        )
        for group in range(KVH):
            for half in range(halves):
                start = group * HD + half * depth
                place = ((group % 2 * 2 + which) * halves + half) * 2 + group // 2
                sent_ref[place] = jnp.concatenate([sums[start : start + depth], stats]).astype(jnp.bfloat16)


def rows_and_sums(own_rows, hidden, norm_gain, router_weight, key_value_weight):
    rows, (_, width) = own_rows.shape[1], hidden.shape
    return pl.pallas_call(
        rows_kernel,
        out_shape=(
            jax.ShapeDtypeStruct((rows, width), jnp.bfloat16),
            jax.ShapeDtypeStruct((2 * ZN, HD // 2 + 8, rows), jnp.bfloat16),
        ),
        in_specs=[pl.BlockSpec(memory_space=pltpu.VMEM)] * 5,
        out_specs=(pl.BlockSpec(memory_space=pltpu.VMEM),) * 2,
        compiler_params=pltpu.CompilerParams(vmem_limit_bytes=24 * 1024 * 1024),
        cost_estimate=pl.CostEstimate(
            flops=4 * rows * width * hidden.shape[0], bytes_accessed=5 * 1024 * 1024, transcendentals=0
        ),
    )(own_rows, hidden, norm_gain.reshape(1, width), router_weight.reshape(1, width), key_value_weight)


def order_kernel(at_ref, *refs):
    pieces, o_ref, scratch_ref = refs[:4], refs[4], refs[5]
    depth = pieces[0].shape[0]
    for k in range(4):
        place = lax.rem(at_ref[0] - k + 4, 4)
        scratch_ref[pl.ds(pl.multiple_of(place * depth, depth), depth), :] = pieces[k][...].astype(jnp.float32)
    o_ref[...] = scratch_ref[...].T.astype(jnp.bfloat16)


def ordered_rows(at, pieces):
    depth, rows = pieces[0].shape
    return pl.pallas_call(
        order_kernel,
        out_shape=jax.ShapeDtypeStruct((rows, 4 * depth), jnp.bfloat16),
        in_specs=[pl.BlockSpec(memory_space=pltpu.SMEM)] + [pl.BlockSpec(memory_space=pltpu.VMEM)] * 4,
        out_specs=pl.BlockSpec(memory_space=pltpu.VMEM),
        scratch_shapes=[pltpu.VMEM((4 * depth, rows), jnp.float32)],
        cost_estimate=pl.CostEstimate(flops=0, bytes_accessed=16 * depth * rows, transcendentals=0),
    )(at[None].astype(jnp.int32), *pieces)


def dot(a, b):
    return jnp.dot(a, b, preferred_element_type=jnp.float32)


def own_kernel(y_ref, x_ref, w_ref, o_ref):
    o_ref[0] = dot(x_ref[...], w_ref[...]).astype(jnp.bfloat16)


def in_kernel(x_ref, w_ref, own_ref, o_ref):
    o_ref[0] = (dot(x_ref[...], w_ref[0]) + own_ref[0].astype(jnp.float32)).astype(jnp.bfloat16)


def own_parts(y, x_own, query_weight, chunks):
    rows, width = x_own.shape
    chunk = query_weight.shape[1] // 2 // chunks
    return pl.pallas_call(
        own_kernel,
        out_shape=jax.ShapeDtypeStruct((chunks, rows, chunk), jnp.bfloat16),
        grid_spec=pltpu.PrefetchScalarGridSpec(
            num_scalar_prefetch=1,
            grid=(chunks,),
            in_specs=[
                pl.BlockSpec((rows, width), lambda d, y: (0, 0)),
                pl.BlockSpec((width, chunk), lambda d, y: (0, y[0] * chunks + d)),
            ],
            out_specs=pl.BlockSpec((1, rows, chunk), lambda d, y: (d, 0, 0)),
        ),
        compiler_params=pltpu.CompilerParams(vmem_limit_bytes=16 * 1024 * 1024),
        cost_estimate=pl.CostEstimate(
            flops=2 * chunks * rows * width * chunk, bytes_accessed=chunks * chunk * 2 * (width + rows), transcendentals=0
        ),
    )(y[None].astype(jnp.int32), x_own, query_weight)


def all_parts(x_in, wq_in, own):
    chunks, rows, chunk = own.shape
    width = x_in.shape[1]
    return pl.pallas_call(
        in_kernel,
        out_shape=jax.ShapeDtypeStruct(own.shape, jnp.bfloat16),
        grid=(chunks,),
        in_specs=[
            pl.BlockSpec((rows, width), lambda d: (0, 0)),
            pl.BlockSpec((1, width, chunk), lambda d: (d, 0, 0)),
            pl.BlockSpec((1, rows, chunk), lambda d: (d, 0, 0)),
        ],
        out_specs=pl.BlockSpec((1, rows, chunk), lambda d: (d, 0, 0)),
        compiler_params=pltpu.CompilerParams(vmem_limit_bytes=16 * 1024 * 1024),
        cost_estimate=pl.CostEstimate(
            flops=2 * chunks * rows * width * chunk, bytes_accessed=chunks * chunk * 2 * (width + 2 * rows), transcendentals=0
        ),
    )(x_in, wq_in, own)


def shards(hidden, norm_gain, router_weight, query_weight, key_value_weight, out_weight, kept_rows):
    bf16 = jnp.bfloat16
    shard = lax.axis_index("ctx")
    tp = lax.axis_index("tp")
    shard_n = lax.axis_size("ctx")
    z, y = tp // 2, tp % 2
    tokens, width = hidden.shape
    rows = kept_rows.shape[1]
    half_cols = query_weight.shape[1] // 2
    chunk = half_cols // ZN

    group = 2 * ZN // 2
    groups = [list(range(g, g + group)) for g in range(0, shard_n, group)]
    mine = shard % group

    def share(got):
        return lax.all_gather(got, "ctx", axis=0, tiled=False, axis_index_groups=groups)

    wq_sent = lax.dynamic_slice(query_weight, (0, (1 - y) * half_cols + mine * chunk), (width, chunk))
    wq_got = lax.ppermute(wq_sent, "tp", y_swap())

    own_rows = lax.dynamic_slice_in_dim(kept_rows, shard, 1, 0)
    x_own, sent = rows_and_sums(own_rows, hidden, norm_gain, router_weight, key_value_weight)
    x_in = lax.ppermute(x_own, "tp", y_swap())

    sent, wq_got = lax.optimization_barrier((sent, wq_got))
    wq_in = share(wq_got)
    exchanged = lax.all_to_all(sent, "tp", 0, 0, tiled=True)
    part = own_parts(y, x_own, query_weight, ZN)
    x_n = shard_n // 4
    at_y, at_x, core = shard // (2 * x_n), shard // 2 % x_n, shard % 2
    offsets = [(0, 0), (-1, 0), (1, 0), (0, 1), (-1, 1), (1, 1), (2, 0), (2, 1)]
    ids = [(at_y + dy) % 2 * (2 * x_n) + (at_x + dx) % x_n * 2 for dx, dy in offsets]
    ids = jnp.stack([i + core for i in ids] + [i + 1 - core for i in ids])
    counts = jnp.sum((kept_rows < tokens).astype(jnp.int32), axis=1)
    info = packing(counts, shard, ids)
    wo_rows = out_weight.shape[0] // 2
    wo_sent = lax.dynamic_slice(out_weight, ((1 - y) * wo_rows + mine * chunk, 0), (chunk, width))
    exchanged, info, wo_sent, part, wq_in = lax.optimization_barrier((exchanged, info, wo_sent, part, wq_in))
    part = all_parts(x_in, wq_in, part)
    summed = jnp.sum(exchanged.astype(jnp.float32), axis=0)
    square_sum = summed[HD // 2] + summed[HD // 2 + 2]
    router_logit = summed[HD // 2 + 1] + summed[HD // 2 + 3]
    inverse_rms = lax.rsqrt(square_sum / D + EPSILON)
    piece = (summed[: HD // 2] * inverse_rms[None, :]).astype(bf16)
    piece, wo_sent, part = lax.optimization_barrier((piece, wo_sent, part))
    query_sum = lax.psum_scatter(
        part, "tp", scatter_dimension=0, axis_index_groups=[[2 * k + h for k in range(ZN)] for h in range(2)]
    )
    pieces = [lax.ppermute(piece, "tp", quad_shift(k)) for k in (1, 2, 3)]
    wo_got = lax.ppermute(wo_sent, "tp", y_swap())
    pieces, wo_got = lax.optimization_barrier(([piece] + pieces, wo_got))
    query_sum, wo_got = lax.optimization_barrier((query_sum, wo_got))
    wo_in = share(wo_got).reshape(wo_rows, width)
    kv_own = ordered_rows(z % 4, pieces)


    def along(step):
        return [(c, c // (2 * x_n) * (2 * x_n) + (c + 2 * step) % (2 * x_n)) for c in range(shard_n)]

    def x_hop(block, step):
        return lax.ppermute(block, "ctx", along(step))

    middle = rows // 2
    over = lax.ppermute(kv_own, "ctx", [(c, (c + shard_n // 2) % shard_n) for c in range(shard_n)])
    near_left, near_right, over = lax.optimization_barrier((x_hop(kv_own, 1), x_hop(kv_own, -1), over))
    first_half = jnp.stack([kv_own, near_left, near_right, over])
    far = x_hop(near_left[:middle], 1), x_hop(near_right[middle:], -1)
    over_left, over_right = x_hop(over, 1), x_hop(over, -1)
    over_left, over_right, far = lax.optimization_barrier((over_left, over_right, far))
    over_far = x_hop(over_left[:middle], 1), x_hop(over_right[middle:], -1)
    second_half = jnp.stack([over_left, over_right, jnp.concatenate(far), jnp.concatenate(over_far)])

    def core_hop(block):
        return lax.ppermute(block, "ctx", [(c, c ^ 1) for c in range(shard_n)])

    kv_all = [first_half, second_half, core_hop(first_half), core_hop(second_half)]
    def right(a):
        return lax.ppermute(a.astype(bf16), "tp", z_shift(1))

    def left(a):
        return lax.ppermute(a.astype(bf16), "tp", z_shift(-1))

    def both(going_right, going_left):
        return lax.optimization_barrier((right(going_right), left(going_left)))

    cut = chunk // 2
    queries = (query_sum.astype(jnp.float32) * (inverse_rms * EXP_SCALE)[:, None]).astype(bf16)

    mixed = attention(info, queries, kv_all)

    def project(piece, offset, low, high):
        start = ((z + offset) % ZN) * chunk + low
        own_w = lax.dynamic_slice(out_weight, (y * wo_rows + start, 0), (high - low, width))
        in_w = lax.dynamic_slice(wo_in, (start, 0), (high - low, width))
        return dot(piece, own_w), dot(piece, in_w)

    terms = [project(mixed, 0, 0, chunk)]
    from_left, from_right = mixed, mixed
    for step in (1, 2, 3):
        from_left, from_right = both(from_left, from_right)
        terms.append(project(from_left, -step, 0, chunk))
        terms.append(project(from_right, step, 0, chunk))
    terms.append(project(right(from_left[:, :cut]), 4, 0, cut))
    terms.append(project(left(from_right[:, cut:]), 4, cut, chunk))
    for_partner = functools.reduce(jnp.add, [t[1] for t in terms])
    received = lax.ppermute(for_partner.astype(bf16), "tp", y_swap())
    own_sum, received = lax.optimization_barrier((functools.reduce(jnp.add, [t[0] for t in terms]), received))
    projected = own_sum + received
    row_update = (jax.nn.sigmoid(router_logit)[:, None] * projected).astype(bf16)
    select = (own_rows.reshape(rows, 1) == jnp.arange(tokens, dtype=jnp.int32)[None, :]).astype(bf16)
    return lax.dot_general(select, row_update, (((0,), (0,)), ((), ())), preferred_element_type=jnp.float32).astype(
        bf16
    )


def solution(mesh):
    return jax.shard_map(
        shards,
        mesh=mesh,
        in_specs=(
            P("ctx", "tp"),
            P("tp"),
            P("tp"),
            P("tp", None),
            P(None, "tp", None),
            P(None, "tp"),
            P(),
        ),
        out_specs=P("ctx", "tp"),
        check_vma=False,
    )
```

```python
import functools

import jax
import jax.numpy as jnp
from jax import lax
from jax.experimental import pallas as pl
from jax.experimental.pallas import tpu as pltpu
from jax.sharding import PartitionSpec as P

D = 8192
H = 32
KVH = 4
HD = 128
ZN = 8
EPSILON = 1e-05
MASKED_SCORE = -1e30
EXP_SCALE = HD ** (-0.5) * 1.4426950408889634
KEY_BLOCK = 1024
ROW_TILE = 512
ATTENTION_VMEM = 32 * 1024 * 1024


def z_shift(dz):
    return [(z * 2 + y, ((z + dz) % ZN) * 2 + y) for z in range(ZN) for y in range(2)]


def y_swap():
    return [(t, t ^ 1) for t in range(2 * ZN)]


def quad_shift(k):
    def target(z):
        return (z // 4) * 4 + (z % 4 + k) % 4

    return [(z * 2 + y, target(z) * 2 + y) for z in range(ZN) for y in range(2)]


def attention_kernel(info_ref, q_ref, *refs):
    kv_refs, (o_ref, qa_ref, ka_ref, v_ref) = refs[:-4], refs[-4:]
    blocks_each, rows, _ = kv_refs[0].shape
    order = [(array, place) for array in range(len(kv_refs)) for place in range(blocks_each)]
    order = order[1:] + order[:1]
    count = info_ref[len(order) - 1, 1]
    first = pl.multiple_of(info_ref[len(order) - 1, 2], 16)

    for index, (array, place) in enumerate(order):

        @pl.when(info_ref[index, 0] > 0)
        def _():
            start = pl.multiple_of(info_ref[index, 2], 16)
            slot = lax.broadcasted_iota(jnp.int32, (rows, HD), 0)
            bias = jnp.where(slot < info_ref[index, 1], 0.0, MASKED_SCORE)
            ka_ref[pl.ds(start, rows), :HD] = kv_refs[array][place, :, :HD]
            ka_ref[pl.ds(start, rows), HD:] = bias.astype(jnp.bfloat16)
            v_ref[pl.ds(start, rows), :] = kv_refs[array][place, :, HD:]

    tail = pl.multiple_of(first + rows, 16)
    ka_ref[pl.ds(tail, KEY_BLOCK), :] = jnp.zeros((KEY_BLOCK, 2 * HD), jnp.bfloat16)
    v_ref[pl.ds(tail, KEY_BLOCK), :] = jnp.zeros((KEY_BLOCK, HD), jnp.bfloat16)
    one = (lax.broadcasted_iota(jnp.int32, (rows, HD), 1) == 0).astype(jnp.bfloat16)
    for head in range(2):
        qa_ref[head, :, :HD] = q_ref[:, head * HD : (head + 1) * HD]
        qa_ref[head, :, HD:] = one
    open_blocks = first // KEY_BLOCK
    blocks = (first + count + KEY_BLOCK - 1) // KEY_BLOCK

    def lane_tiles(array):
        return [array[:, i * HD : (i + 1) * HD] for i in range(KEY_BLOCK // HD)]

    def tile_work(tile):
        base = tile * ROW_TILE

        def scores(block, head, masked):
            start = pl.multiple_of(block * KEY_BLOCK, KEY_BLOCK)
            out = lax.dot_general(
                qa_ref[head, base : base + ROW_TILE, :],
                ka_ref[pl.ds(start, KEY_BLOCK), :],
                (((1,), (1,)), ((), ())),
                preferred_element_type=jnp.float32,
            )
            if masked:
                key = lax.broadcasted_iota(jnp.int32, out.shape, 1)
                query = lax.broadcasted_iota(jnp.int32, out.shape, 0)
                out = jnp.where(key - query <= first + base - start, out, MASKED_SCORE)
            return out

        def body(masked):
            def run(block, state):
                start = pl.multiple_of(block * KEY_BLOCK, KEY_BLOCK)
                new = []
                for head in range(2):
                    peak, total, acc = state[3 * head : 3 * head + 3]
                    score = scores(block, head, masked)
                    lanes = functools.reduce(jnp.maximum, lane_tiles(score))
                    new_peak = jnp.maximum(peak, jnp.max(lanes, axis=1, keepdims=True))
                    weights = jnp.exp2(score - new_peak)
                    rescale = jnp.exp2(peak - new_peak)
                    new.append(new_peak)
                    new.append(functools.reduce(jnp.add, lane_tiles(weights), total * rescale))
                    new.append(
                        acc * rescale
                        + jnp.dot(
                            weights.astype(jnp.bfloat16),
                            v_ref[pl.ds(start, KEY_BLOCK), :],
                            preferred_element_type=jnp.float32,
                        )
                    )
                return tuple(new)

            return run

        zero = jnp.zeros((ROW_TILE, HD), jnp.float32)
        state = (jnp.full((ROW_TILE, 1), MASKED_SCORE, jnp.float32), zero, zero) * 2
        state = lax.fori_loop(0, open_blocks, body(False), state)
        state = lax.fori_loop(open_blocks, blocks, body(True), state)
        for head in range(2):
            total = jnp.sum(state[3 * head + 1], axis=1, keepdims=True)
            o_ref[base : base + ROW_TILE, head * HD : (head + 1) * HD] = (state[3 * head + 2] / total).astype(
                jnp.bfloat16
            )

    for tile in range(rows // ROW_TILE):
        if tile == 0:
            tile_work(tile)
        else:

            @pl.when(tile * ROW_TILE < count)
            def _():
                tile_work(tile)

            @pl.when(tile * ROW_TILE >= count)
            def _():
                o_ref[tile * ROW_TILE : (tile + 1) * ROW_TILE, :] = jnp.zeros((ROW_TILE, 2 * HD), jnp.bfloat16)


def packing(counts, own, ids):
    shards_n = ids.shape[0]
    ids = jnp.concatenate([ids[1:], ids[:1]])
    used = ids <= own
    held = jnp.sum(jnp.where(ids[:, None] == jnp.arange(shards_n)[None, :], counts[None, :], 0), axis=1)
    packed = jnp.where(used, (held + 15) // 16 * 16, 0)
    before = jnp.arange(shards_n)[None, :] < jnp.arange(shards_n)[:, None]
    first = jnp.sum(jnp.where(before, packed[None, :], 0), axis=1)
    return jnp.stack([used.astype(jnp.int32), held, first], axis=1).astype(jnp.int32)


def attention(info, queries, kv):
    blocks_each, rows, _ = kv[0].shape
    shards_n = blocks_each * len(kv)
    capacity = shards_n * (rows // 2 + 16) + rows + KEY_BLOCK
    return pl.pallas_call(
        attention_kernel,
        out_shape=jax.ShapeDtypeStruct(queries.shape, jnp.bfloat16),
        in_specs=[pl.BlockSpec(memory_space=pltpu.SMEM)]
        + [pl.BlockSpec(memory_space=pltpu.VMEM)] * (1 + len(kv)),
        out_specs=pl.BlockSpec(memory_space=pltpu.VMEM),
        scratch_shapes=[
            pltpu.VMEM((2, rows, 2 * HD), jnp.bfloat16),
            pltpu.VMEM((capacity, 2 * HD), jnp.bfloat16),
            pltpu.VMEM((capacity, HD), jnp.bfloat16),
        ],
        compiler_params=pltpu.CompilerParams(vmem_limit_bytes=ATTENTION_VMEM),
        cost_estimate=pl.CostEstimate(
            flops=4 * 2 * rows * HD * shards_n * rows,
            bytes_accessed=shards_n * rows * HD * 4,
            transcendentals=rows * rows * shards_n,
        ),
    )(info, queries, *kv)


def rows_kernel(rows_ref, hidden_ref, gain_ref, router_ref, kv_ref, x_ref, sent_ref):
    tokens, width = hidden_ref.shape
    rows = rows_ref.shape[1]
    token = lax.broadcasted_iota(jnp.int32, (tokens, rows), 0)
    select = jnp.where(token == rows_ref[...], 1.0, 0.0).astype(jnp.bfloat16)
    kept = lax.dot_general(select, hidden_ref[...], (((0,), (0,)), ((), ())), preferred_element_type=jnp.float32)
    normed = kept * gain_ref[...].astype(jnp.float32)
    x_ref[...] = normed.astype(jnp.bfloat16)

    def feature_sum(array):
        tiles = [array[:, i * HD : (i + 1) * HD] for i in range(width // HD)]
        return jnp.sum(functools.reduce(jnp.add, tiles).T, axis=0, keepdims=True)

    stats = jnp.concatenate([feature_sum(kept * kept), feature_sum(kept * router_ref[...].astype(jnp.float32))])
    high = stats.astype(jnp.bfloat16).astype(jnp.float32)
    stats = jnp.concatenate([high, stats - high, jnp.zeros((4, rows), jnp.float32)])
    turned = normed.T.astype(jnp.bfloat16)
    depth = sent_ref.shape[1] - stats.shape[0]
    halves = HD // depth
    for which in range(2):
        sums = lax.dot_general(
            kv_ref[which], turned, (((0,), (0,)), ((), ())), preferred_element_type=jnp.float32
        )
        for group in range(KVH):
            for half in range(halves):
                start = group * HD + half * depth
                place = ((group % 2 * 2 + which) * halves + half) * 2 + group // 2
                sent_ref[place] = jnp.concatenate([sums[start : start + depth], stats]).astype(jnp.bfloat16)


def rows_and_sums(own_rows, hidden, norm_gain, router_weight, key_value_weight):
    rows, (_, width) = own_rows.shape[1], hidden.shape
    return pl.pallas_call(
        rows_kernel,
        out_shape=(
            jax.ShapeDtypeStruct((rows, width), jnp.bfloat16),
            jax.ShapeDtypeStruct((2 * ZN, HD // 2 + 8, rows), jnp.bfloat16),
        ),
        in_specs=[pl.BlockSpec(memory_space=pltpu.VMEM)] * 5,
        out_specs=(pl.BlockSpec(memory_space=pltpu.VMEM),) * 2,
        compiler_params=pltpu.CompilerParams(vmem_limit_bytes=24 * 1024 * 1024),
        cost_estimate=pl.CostEstimate(
            flops=4 * rows * width * hidden.shape[0], bytes_accessed=5 * 1024 * 1024, transcendentals=0
        ),
    )(own_rows, hidden, norm_gain.reshape(1, width), router_weight.reshape(1, width), key_value_weight)


def order_kernel(at_ref, *refs):
    pieces, o_ref, scratch_ref = refs[:4], refs[4], refs[5]
    depth = pieces[0].shape[0]
    for k in range(4):
        place = lax.rem(at_ref[0] - k + 4, 4)
        scratch_ref[pl.ds(pl.multiple_of(place * depth, depth), depth), :] = pieces[k][...].astype(jnp.float32)
    o_ref[...] = scratch_ref[...].T.astype(jnp.bfloat16)


def ordered_rows(at, pieces):
    depth, rows = pieces[0].shape
    return pl.pallas_call(
        order_kernel,
        out_shape=jax.ShapeDtypeStruct((rows, 4 * depth), jnp.bfloat16),
        in_specs=[pl.BlockSpec(memory_space=pltpu.SMEM)] + [pl.BlockSpec(memory_space=pltpu.VMEM)] * 4,
        out_specs=pl.BlockSpec(memory_space=pltpu.VMEM),
        scratch_shapes=[pltpu.VMEM((4 * depth, rows), jnp.float32)],
        cost_estimate=pl.CostEstimate(flops=0, bytes_accessed=16 * depth * rows, transcendentals=0),
    )(at[None].astype(jnp.int32), *pieces)


def dot(a, b):
    return jnp.dot(a, b, preferred_element_type=jnp.float32)


def own_kernel(y_ref, x_ref, w_ref, o_ref):
    o_ref[0] = dot(x_ref[...], w_ref[...]).astype(jnp.bfloat16)


def in_kernel(x_ref, w_ref, own_ref, o_ref):
    o_ref[0] = (dot(x_ref[...], w_ref[0]) + own_ref[0].astype(jnp.float32)).astype(jnp.bfloat16)


def own_parts(y, x_own, query_weight, chunks):
    rows, width = x_own.shape
    chunk = query_weight.shape[1] // 2 // chunks
    return pl.pallas_call(
        own_kernel,
        out_shape=jax.ShapeDtypeStruct((chunks, rows, chunk), jnp.bfloat16),
        grid_spec=pltpu.PrefetchScalarGridSpec(
            num_scalar_prefetch=1,
            grid=(chunks,),
            in_specs=[
                pl.BlockSpec((rows, width), lambda d, y: (0, 0)),
                pl.BlockSpec((width, chunk), lambda d, y: (0, y[0] * chunks + d)),
            ],
            out_specs=pl.BlockSpec((1, rows, chunk), lambda d, y: (d, 0, 0)),
        ),
        compiler_params=pltpu.CompilerParams(vmem_limit_bytes=16 * 1024 * 1024),
        cost_estimate=pl.CostEstimate(
            flops=2 * chunks * rows * width * chunk, bytes_accessed=chunks * chunk * 2 * (width + rows), transcendentals=0
        ),
    )(y[None].astype(jnp.int32), x_own, query_weight)


def all_parts(x_in, wq_in, own):
    chunks, rows, chunk = own.shape
    width = x_in.shape[1]
    return pl.pallas_call(
        in_kernel,
        out_shape=jax.ShapeDtypeStruct(own.shape, jnp.bfloat16),
        grid=(chunks,),
        in_specs=[
            pl.BlockSpec((rows, width), lambda d: (0, 0)),
            pl.BlockSpec((1, width, chunk), lambda d: (d, 0, 0)),
            pl.BlockSpec((1, rows, chunk), lambda d: (d, 0, 0)),
        ],
        out_specs=pl.BlockSpec((1, rows, chunk), lambda d: (d, 0, 0)),
        compiler_params=pltpu.CompilerParams(vmem_limit_bytes=16 * 1024 * 1024),
        cost_estimate=pl.CostEstimate(
            flops=2 * chunks * rows * width * chunk, bytes_accessed=chunks * chunk * 2 * (width + 2 * rows), transcendentals=0
        ),
    )(x_in, wq_in, own)


def project_kernel(starts_ref, w_hbm, *refs):
    pieces, (o_ref, x_ref, w_ref, sem) = refs[:-4], refs[-4:]
    copies, at = [], 0
    for index, piece in enumerate(pieces):
        depth = piece.shape[1]
        start = pl.multiple_of(starts_ref[index], HD)
        copies.append(
            pltpu.make_async_copy(w_hbm.at[pl.ds(start, depth), :], w_ref.at[pl.ds(at, depth), :], sem.at[index])
        )
        at += depth
    for copy in copies:
        copy.start()
    at = 0
    for piece in pieces:
        depth = piece.shape[1]
        x_ref[:, at : at + depth] = piece[...]
        at += depth
    for copy in copies:
        copy.wait()
    o_ref[...] = dot(x_ref[...], w_ref[...]).astype(o_ref.dtype)


def project(starts, weights, pieces, kind):
    rows = pieces[0].shape[0]
    depth = sum(piece.shape[1] for piece in pieces)
    width = weights.shape[1]
    return pl.pallas_call(
        project_kernel,
        out_shape=jax.ShapeDtypeStruct((rows, width), kind),
        in_specs=[pl.BlockSpec(memory_space=pltpu.SMEM), pl.BlockSpec(memory_space=pl.ANY)]
        + [pl.BlockSpec(memory_space=pltpu.VMEM)] * len(pieces),
        out_specs=pl.BlockSpec(memory_space=pltpu.VMEM),
        scratch_shapes=[
            pltpu.VMEM((rows, depth), jnp.bfloat16),
            pltpu.VMEM((depth, width), jnp.bfloat16),
            pltpu.SemaphoreType.DMA((len(pieces),)),
        ],
        compiler_params=pltpu.CompilerParams(vmem_limit_bytes=24 * 1024 * 1024),
        cost_estimate=pl.CostEstimate(
            flops=2 * rows * depth * width, bytes_accessed=2 * depth * (rows + width) + 4 * rows * width, transcendentals=0
        ),
    )(starts, weights, *pieces)


def shards(hidden, norm_gain, router_weight, query_weight, key_value_weight, out_weight, kept_rows):
    bf16 = jnp.bfloat16
    shard = lax.axis_index("ctx")
    tp = lax.axis_index("tp")
    shard_n = lax.axis_size("ctx")
    z, y = tp // 2, tp % 2
    tokens, width = hidden.shape
    rows = kept_rows.shape[1]
    half_cols = query_weight.shape[1] // 2
    chunk = half_cols // ZN

    group = 2 * ZN // 2
    groups = [list(range(g, g + group)) for g in range(0, shard_n, group)]
    mine = shard % group

    def share(got):
        return lax.all_gather(got, "ctx", axis=0, tiled=False, axis_index_groups=groups)

    wq_sent = lax.dynamic_slice(query_weight, (0, (1 - y) * half_cols + mine * chunk), (width, chunk))
    wq_got = lax.ppermute(wq_sent, "tp", y_swap())

    own_rows = lax.dynamic_slice_in_dim(kept_rows, shard, 1, 0)
    x_own, sent = rows_and_sums(own_rows, hidden, norm_gain, router_weight, key_value_weight)
    x_in = lax.ppermute(x_own, "tp", y_swap())

    sent, wq_got = lax.optimization_barrier((sent, wq_got))
    wq_in = share(wq_got)
    exchanged = lax.all_to_all(sent, "tp", 0, 0, tiled=True)
    part = own_parts(y, x_own, query_weight, ZN)
    x_n = shard_n // 4
    at_y, at_x, core = shard // (2 * x_n), shard // 2 % x_n, shard % 2
    offsets = [(0, 0), (-1, 0), (1, 0), (0, 1), (-1, 1), (1, 1), (2, 0), (2, 1)]
    ids = [(at_y + dy) % 2 * (2 * x_n) + (at_x + dx) % x_n * 2 for dx, dy in offsets]
    ids = jnp.stack([i + core for i in ids] + [i + 1 - core for i in ids])
    counts = jnp.sum((kept_rows < tokens).astype(jnp.int32), axis=1)
    info = packing(counts, shard, ids)
    wo_rows = out_weight.shape[0] // 2
    wo_sent = lax.dynamic_slice(out_weight, ((1 - y) * wo_rows + mine * chunk, 0), (chunk, width))
    exchanged, info, wo_sent, part, wq_in = lax.optimization_barrier((exchanged, info, wo_sent, part, wq_in))
    part = all_parts(x_in, wq_in, part)
    summed = jnp.sum(exchanged.astype(jnp.float32), axis=0)
    square_sum = summed[HD // 2] + summed[HD // 2 + 2]
    router_logit = summed[HD // 2 + 1] + summed[HD // 2 + 3]
    inverse_rms = lax.rsqrt(square_sum / D + EPSILON)
    piece = (summed[: HD // 2] * inverse_rms[None, :]).astype(bf16)
    piece, wo_sent, part = lax.optimization_barrier((piece, wo_sent, part))
    query_sum = lax.psum_scatter(
        part, "tp", scatter_dimension=0, axis_index_groups=[[2 * k + h for k in range(ZN)] for h in range(2)]
    )
    pieces = [lax.ppermute(piece, "tp", quad_shift(k)) for k in (1, 2, 3)]
    wo_got = lax.ppermute(wo_sent, "tp", y_swap())
    pieces, wo_got = lax.optimization_barrier(([piece] + pieces, wo_got))
    query_sum, wo_got = lax.optimization_barrier((query_sum, wo_got))
    wo_in = share(wo_got).reshape(wo_rows, width)
    kv_own = ordered_rows(z % 4, pieces)


    def along(step):
        return [(c, c // (2 * x_n) * (2 * x_n) + (c + 2 * step) % (2 * x_n)) for c in range(shard_n)]

    def x_hop(block, step):
        return lax.ppermute(block, "ctx", along(step))

    middle = rows // 2
    over = lax.ppermute(kv_own, "ctx", [(c, (c + shard_n // 2) % shard_n) for c in range(shard_n)])
    near_left, near_right, over = lax.optimization_barrier((x_hop(kv_own, 1), x_hop(kv_own, -1), over))
    first_half = jnp.stack([kv_own, near_left, near_right, over])
    far = x_hop(near_left[:middle], 1), x_hop(near_right[middle:], -1)
    over_left, over_right = x_hop(over, 1), x_hop(over, -1)
    over_left, over_right, far = lax.optimization_barrier((over_left, over_right, far))
    over_far = x_hop(over_left[:middle], 1), x_hop(over_right[middle:], -1)
    second_half = jnp.stack([over_left, over_right, jnp.concatenate(far), jnp.concatenate(over_far)])

    def core_hop(block):
        return lax.ppermute(block, "ctx", [(c, c ^ 1) for c in range(shard_n)])

    kv_all = [first_half, second_half, core_hop(first_half), core_hop(second_half)]
    def right(a):
        return lax.ppermute(a.astype(bf16), "tp", z_shift(1))

    def left(a):
        return lax.ppermute(a.astype(bf16), "tp", z_shift(-1))

    def both(going_right, going_left):
        return lax.optimization_barrier((right(going_right), left(going_left)))

    cut = chunk // 2
    queries = (query_sum.astype(jnp.float32) * (inverse_rms * EXP_SCALE)[:, None]).astype(bf16)

    mixed = attention(info, queries, kv_all)

    pieces, starts = [mixed], [0]
    from_left, from_right = mixed, mixed
    for step in (1, 2, 3):
        from_left, from_right = both(from_left, from_right)
        if step == 2:
            from_left, from_right, wo_in = lax.optimization_barrier((from_left, from_right, wo_in))
        pieces += [from_left, from_right]
        starts += [-step, step]
    pieces += [right(from_left[:, :cut]), left(from_right[:, cut:])]
    starts = [(z + offset) % ZN * chunk for offset in starts] + [(z + 4) % ZN * chunk + low for low in (0, cut)]
    starts = jnp.stack(starts).astype(jnp.int32)
    for_partner = project(starts, wo_in, pieces, bf16)
    received = lax.ppermute(for_partner, "tp", y_swap())
    pieces, for_partner = lax.optimization_barrier((pieces, for_partner))
    own_sum = project(starts + y * wo_rows, out_weight, pieces, jnp.float32)
    own_sum, received = lax.optimization_barrier((own_sum, received))
    projected = own_sum + received
    row_update = (jax.nn.sigmoid(router_logit)[:, None] * projected).astype(bf16)
    select = (own_rows.reshape(rows, 1) == jnp.arange(tokens, dtype=jnp.int32)[None, :]).astype(bf16)
    return lax.dot_general(select, row_update, (((0,), (0,)), ((), ())), preferred_element_type=jnp.float32).astype(
        bf16
    )


def solution(mesh):
    return jax.shard_map(
        shards,
        mesh=mesh,
        in_specs=(
            P("ctx", "tp"),
            P("tp"),
            P("tp"),
            P("tp", None),
            P(None, "tp", None),
            P(None, "tp"),
            P(),
        ),
        out_specs=P("ctx", "tp"),
        check_vma=False,
    )
```

```python
import functools

import jax
import jax.numpy as jnp
from jax import lax
from jax.experimental import pallas as pl
from jax.experimental.pallas import tpu as pltpu
from jax.sharding import PartitionSpec as P

D = 8192
H = 32
KVH = 4
HD = 128
ZN = 8
EPSILON = 1e-05
MASKED_SCORE = -1e30
EXP_SCALE = HD ** (-0.5) * 1.4426950408889634
KEY_BLOCK = 1024
ROW_TILE = 512
ATTENTION_VMEM = 32 * 1024 * 1024


def z_shift(dz):
    return [(z * 2 + y, ((z + dz) % ZN) * 2 + y) for z in range(ZN) for y in range(2)]


def y_swap():
    return [(t, t ^ 1) for t in range(2 * ZN)]


def quad_shift(k):
    def target(z):
        return (z // 4) * 4 + (z % 4 + k) % 4

    return [(z * 2 + y, target(z) * 2 + y) for z in range(ZN) for y in range(2)]


def attention_kernel(info_ref, q_ref, *refs):
    kv_refs, (o_ref, qa_ref, ka_ref, v_ref) = refs[:-4], refs[-4:]
    blocks_each, rows, _ = kv_refs[0].shape
    order = [(array, place) for array in range(len(kv_refs)) for place in range(blocks_each)]
    order = order[1:] + order[:1]
    count = info_ref[len(order) - 1, 1]
    first = pl.multiple_of(info_ref[len(order) - 1, 2], 16)

    for index, (array, place) in enumerate(order):

        @pl.when(info_ref[index, 0] > 0)
        def _():
            start = pl.multiple_of(info_ref[index, 2], 16)
            slot = lax.broadcasted_iota(jnp.int32, (rows, HD), 0)
            bias = jnp.where(slot < info_ref[index, 1], 0.0, MASKED_SCORE)
            ka_ref[pl.ds(start, rows), :HD] = kv_refs[array][place, :, :HD]
            ka_ref[pl.ds(start, rows), HD:] = bias.astype(jnp.bfloat16)
            v_ref[pl.ds(start, rows), :] = kv_refs[array][place, :, HD:]

    tail = pl.multiple_of(first + rows, 16)
    ka_ref[pl.ds(tail, KEY_BLOCK), :] = jnp.zeros((KEY_BLOCK, 2 * HD), jnp.bfloat16)
    v_ref[pl.ds(tail, KEY_BLOCK), :] = jnp.zeros((KEY_BLOCK, HD), jnp.bfloat16)
    one = (lax.broadcasted_iota(jnp.int32, (rows, HD), 1) == 0).astype(jnp.bfloat16)
    for head in range(2):
        qa_ref[head, :, :HD] = q_ref[:, head * HD : (head + 1) * HD]
        qa_ref[head, :, HD:] = one
    open_blocks = first // KEY_BLOCK
    blocks = (first + count + KEY_BLOCK - 1) // KEY_BLOCK

    def lane_tiles(array):
        return [array[:, i * HD : (i + 1) * HD] for i in range(KEY_BLOCK // HD)]

    def tile_work(tile):
        base = tile * ROW_TILE

        def scores(block, head, masked):
            start = pl.multiple_of(block * KEY_BLOCK, KEY_BLOCK)
            out = lax.dot_general(
                qa_ref[head, base : base + ROW_TILE, :],
                ka_ref[pl.ds(start, KEY_BLOCK), :],
                (((1,), (1,)), ((), ())),
                preferred_element_type=jnp.float32,
            )
            if masked:
                key = lax.broadcasted_iota(jnp.int32, out.shape, 1)
                query = lax.broadcasted_iota(jnp.int32, out.shape, 0)
                out = jnp.where(key - query <= first + base - start, out, MASKED_SCORE)
            return out

        def body(masked):
            def run(block, state):
                start = pl.multiple_of(block * KEY_BLOCK, KEY_BLOCK)
                new = []
                for head in range(2):
                    peak, total, acc = state[3 * head : 3 * head + 3]
                    score = scores(block, head, masked)
                    lanes = functools.reduce(jnp.maximum, lane_tiles(score))
                    new_peak = jnp.maximum(peak, jnp.max(lanes, axis=1, keepdims=True))
                    weights = jnp.exp2(score - new_peak)
                    rescale = jnp.exp2(peak - new_peak)
                    new.append(new_peak)
                    new.append(functools.reduce(jnp.add, lane_tiles(weights), total * rescale))
                    new.append(
                        acc * rescale
                        + jnp.dot(
                            weights.astype(jnp.bfloat16),
                            v_ref[pl.ds(start, KEY_BLOCK), :],
                            preferred_element_type=jnp.float32,
                        )
                    )
                return tuple(new)

            return run

        zero = jnp.zeros((ROW_TILE, HD), jnp.float32)
        state = (jnp.full((ROW_TILE, 1), MASKED_SCORE, jnp.float32), zero, zero) * 2
        state = lax.fori_loop(0, open_blocks, body(False), state)
        state = lax.fori_loop(open_blocks, blocks, body(True), state)
        for head in range(2):
            total = jnp.sum(state[3 * head + 1], axis=1, keepdims=True)
            o_ref[base : base + ROW_TILE, head * HD : (head + 1) * HD] = (state[3 * head + 2] / total).astype(
                jnp.bfloat16
            )

    for tile in range(rows // ROW_TILE):
        if tile == 0:
            tile_work(tile)
        else:

            @pl.when(tile * ROW_TILE < count)
            def _():
                tile_work(tile)

            @pl.when(tile * ROW_TILE >= count)
            def _():
                o_ref[tile * ROW_TILE : (tile + 1) * ROW_TILE, :] = jnp.zeros((ROW_TILE, 2 * HD), jnp.bfloat16)


def packing(counts, own, ids):
    shards_n = ids.shape[0]
    ids = jnp.concatenate([ids[1:], ids[:1]])
    used = ids <= own
    held = jnp.sum(jnp.where(ids[:, None] == jnp.arange(shards_n)[None, :], counts[None, :], 0), axis=1)
    packed = jnp.where(used, (held + 15) // 16 * 16, 0)
    before = jnp.arange(shards_n)[None, :] < jnp.arange(shards_n)[:, None]
    first = jnp.sum(jnp.where(before, packed[None, :], 0), axis=1)
    return jnp.stack([used.astype(jnp.int32), held, first], axis=1).astype(jnp.int32)


def attention(info, queries, kv):
    blocks_each, rows, _ = kv[0].shape
    shards_n = blocks_each * len(kv)
    capacity = shards_n * (rows // 2 + 16) + rows + KEY_BLOCK
    return pl.pallas_call(
        attention_kernel,
        out_shape=jax.ShapeDtypeStruct(queries.shape, jnp.bfloat16),
        in_specs=[pl.BlockSpec(memory_space=pltpu.SMEM)]
        + [pl.BlockSpec(memory_space=pltpu.VMEM)] * (1 + len(kv)),
        out_specs=pl.BlockSpec(memory_space=pltpu.VMEM),
        scratch_shapes=[
            pltpu.VMEM((2, rows, 2 * HD), jnp.bfloat16),
            pltpu.VMEM((capacity, 2 * HD), jnp.bfloat16),
            pltpu.VMEM((capacity, HD), jnp.bfloat16),
        ],
        compiler_params=pltpu.CompilerParams(vmem_limit_bytes=ATTENTION_VMEM),
        cost_estimate=pl.CostEstimate(
            flops=4 * 2 * rows * HD * shards_n * rows,
            bytes_accessed=shards_n * rows * HD * 4,
            transcendentals=rows * rows * shards_n,
        ),
    )(info, queries, *kv)


def rows_kernel(rows_ref, hidden_ref, gain_ref, router_ref, kv_ref, x_ref, sent_ref):
    tokens, width = hidden_ref.shape
    rows = rows_ref.shape[1]
    token = lax.broadcasted_iota(jnp.int32, (tokens, rows), 0)
    select = jnp.where(token == rows_ref[...], 1.0, 0.0).astype(jnp.bfloat16)
    kept = lax.dot_general(select, hidden_ref[...], (((0,), (0,)), ((), ())), preferred_element_type=jnp.float32)
    normed = kept * gain_ref[...].astype(jnp.float32)
    x_ref[...] = normed.astype(jnp.bfloat16)

    def feature_sum(array):
        tiles = [array[:, i * HD : (i + 1) * HD] for i in range(width // HD)]
        return jnp.sum(functools.reduce(jnp.add, tiles).T, axis=0, keepdims=True)

    stats = jnp.concatenate([feature_sum(kept * kept), feature_sum(kept * router_ref[...].astype(jnp.float32))])
    high = stats.astype(jnp.bfloat16).astype(jnp.float32)
    stats = jnp.concatenate([high, stats - high, jnp.zeros((4, rows), jnp.float32)])
    turned = normed.T.astype(jnp.bfloat16)
    depth = sent_ref.shape[1] - stats.shape[0]
    halves = HD // depth
    for which in range(2):
        sums = lax.dot_general(
            kv_ref[which], turned, (((0,), (0,)), ((), ())), preferred_element_type=jnp.float32
        )
        for group in range(KVH):
            for half in range(halves):
                start = group * HD + half * depth
                place = ((group % 2 * 2 + which) * halves + half) * 2 + group // 2
                sent_ref[place] = jnp.concatenate([sums[start : start + depth], stats]).astype(jnp.bfloat16)


def rows_and_sums(own_rows, hidden, norm_gain, router_weight, key_value_weight):
    rows, (_, width) = own_rows.shape[1], hidden.shape
    return pl.pallas_call(
        rows_kernel,
        out_shape=(
            jax.ShapeDtypeStruct((rows, width), jnp.bfloat16),
            jax.ShapeDtypeStruct((2 * ZN, HD // 2 + 8, rows), jnp.bfloat16),
        ),
        in_specs=[pl.BlockSpec(memory_space=pltpu.VMEM)] * 5,
        out_specs=(pl.BlockSpec(memory_space=pltpu.VMEM),) * 2,
        compiler_params=pltpu.CompilerParams(vmem_limit_bytes=24 * 1024 * 1024),
        cost_estimate=pl.CostEstimate(
            flops=4 * rows * width * hidden.shape[0], bytes_accessed=5 * 1024 * 1024, transcendentals=0
        ),
    )(own_rows, hidden, norm_gain.reshape(1, width), router_weight.reshape(1, width), key_value_weight)


def order_kernel(at_ref, *refs):
    pieces, o_ref, scratch_ref = refs[:4], refs[4], refs[5]
    depth = pieces[0].shape[0]
    for k in range(4):
        place = lax.rem(at_ref[0] - k + 4, 4)
        scratch_ref[pl.ds(pl.multiple_of(place * depth, depth), depth), :] = pieces[k][...].astype(jnp.float32)
    o_ref[...] = scratch_ref[...].T.astype(jnp.bfloat16)


def ordered_rows(at, pieces):
    depth, rows = pieces[0].shape
    return pl.pallas_call(
        order_kernel,
        out_shape=jax.ShapeDtypeStruct((rows, 4 * depth), jnp.bfloat16),
        in_specs=[pl.BlockSpec(memory_space=pltpu.SMEM)] + [pl.BlockSpec(memory_space=pltpu.VMEM)] * 4,
        out_specs=pl.BlockSpec(memory_space=pltpu.VMEM),
        scratch_shapes=[pltpu.VMEM((4 * depth, rows), jnp.float32)],
        cost_estimate=pl.CostEstimate(flops=0, bytes_accessed=16 * depth * rows, transcendentals=0),
    )(at[None].astype(jnp.int32), *pieces)


def dot(a, b):
    return jnp.dot(a, b, preferred_element_type=jnp.float32)


def own_kernel(y_ref, x_ref, w_ref, o_ref):
    o_ref[0] = dot(x_ref[...], w_ref[...]).astype(jnp.bfloat16)


def in_kernel(x_ref, w_ref, own_ref, o_ref):
    o_ref[0] = (dot(x_ref[...], w_ref[0]) + own_ref[0].astype(jnp.float32)).astype(jnp.bfloat16)


def own_parts(y, x_own, query_weight, chunks):
    rows, width = x_own.shape
    chunk = query_weight.shape[1] // 2 // chunks
    return pl.pallas_call(
        own_kernel,
        out_shape=jax.ShapeDtypeStruct((chunks, rows, chunk), jnp.bfloat16),
        grid_spec=pltpu.PrefetchScalarGridSpec(
            num_scalar_prefetch=1,
            grid=(chunks,),
            in_specs=[
                pl.BlockSpec((rows, width), lambda d, y: (0, 0)),
                pl.BlockSpec((width, chunk), lambda d, y: (0, y[0] * chunks + d)),
            ],
            out_specs=pl.BlockSpec((1, rows, chunk), lambda d, y: (d, 0, 0)),
        ),
        compiler_params=pltpu.CompilerParams(vmem_limit_bytes=16 * 1024 * 1024),
        cost_estimate=pl.CostEstimate(
            flops=2 * chunks * rows * width * chunk, bytes_accessed=chunks * chunk * 2 * (width + rows), transcendentals=0
        ),
    )(y[None].astype(jnp.int32), x_own, query_weight)


def all_parts(x_in, wq_in, own):
    chunks, rows, chunk = own.shape
    width = x_in.shape[1]
    return pl.pallas_call(
        in_kernel,
        out_shape=jax.ShapeDtypeStruct(own.shape, jnp.bfloat16),
        grid=(chunks,),
        in_specs=[
            pl.BlockSpec((rows, width), lambda d: (0, 0)),
            pl.BlockSpec((1, width, chunk), lambda d: (d, 0, 0)),
            pl.BlockSpec((1, rows, chunk), lambda d: (d, 0, 0)),
        ],
        out_specs=pl.BlockSpec((1, rows, chunk), lambda d: (d, 0, 0)),
        compiler_params=pltpu.CompilerParams(vmem_limit_bytes=16 * 1024 * 1024),
        cost_estimate=pl.CostEstimate(
            flops=2 * chunks * rows * width * chunk, bytes_accessed=chunks * chunk * 2 * (width + 2 * rows), transcendentals=0
        ),
    )(x_in, wq_in, own)


def project_kernel(starts_ref, w_hbm, *refs):
    pieces, (o_ref, x_ref, w_ref, sem) = refs[:-4], refs[-4:]
    copies, at = [], 0
    for index, piece in enumerate(pieces):
        depth = piece.shape[1]
        start = pl.multiple_of(starts_ref[index], HD)
        copies.append(
            pltpu.make_async_copy(w_hbm.at[pl.ds(start, depth), :], w_ref.at[pl.ds(at, depth), :], sem.at[index])
        )
        at += depth
    for copy in copies:
        copy.start()
    at = 0
    for piece in pieces:
        depth = piece.shape[1]
        x_ref[:, at : at + depth] = piece[...]
        at += depth
    for copy in copies:
        copy.wait()
    o_ref[...] = dot(x_ref[...], w_ref[...]).astype(o_ref.dtype)


def project(starts, weights, pieces, kind):
    rows = pieces[0].shape[0]
    depth = sum(piece.shape[1] for piece in pieces)
    width = weights.shape[1]
    return pl.pallas_call(
        project_kernel,
        out_shape=jax.ShapeDtypeStruct((rows, width), kind),
        in_specs=[pl.BlockSpec(memory_space=pltpu.SMEM), pl.BlockSpec(memory_space=pl.ANY)]
        + [pl.BlockSpec(memory_space=pltpu.VMEM)] * len(pieces),
        out_specs=pl.BlockSpec(memory_space=pltpu.VMEM),
        scratch_shapes=[
            pltpu.VMEM((rows, depth), jnp.bfloat16),
            pltpu.VMEM((depth, width), jnp.bfloat16),
            pltpu.SemaphoreType.DMA((len(pieces),)),
        ],
        compiler_params=pltpu.CompilerParams(vmem_limit_bytes=24 * 1024 * 1024),
        cost_estimate=pl.CostEstimate(
            flops=2 * rows * depth * width, bytes_accessed=2 * depth * (rows + width) + 4 * rows * width, transcendentals=0
        ),
    )(starts, weights, *pieces)


def shards(hidden, norm_gain, router_weight, query_weight, key_value_weight, out_weight, kept_rows):
    bf16 = jnp.bfloat16
    shard = lax.axis_index("ctx")
    tp = lax.axis_index("tp")
    shard_n = lax.axis_size("ctx")
    z, y = tp // 2, tp % 2
    tokens, width = hidden.shape
    rows = kept_rows.shape[1]
    half_cols = query_weight.shape[1] // 2
    chunk = half_cols // ZN

    group = 2 * ZN // 2
    groups = [list(range(g, g + group)) for g in range(0, shard_n, group)]
    mine = shard % group

    def share(got):
        return lax.all_gather(got, "ctx", axis=0, tiled=False, axis_index_groups=groups)

    wq_sent = lax.dynamic_slice(query_weight, (0, (1 - y) * half_cols + mine * chunk), (width, chunk))
    wq_got = lax.ppermute(wq_sent, "tp", y_swap())

    own_rows = lax.dynamic_slice_in_dim(kept_rows, shard, 1, 0)
    x_own, sent = rows_and_sums(own_rows, hidden, norm_gain, router_weight, key_value_weight)
    x_in = lax.ppermute(x_own, "tp", y_swap())

    sent, wq_got = lax.optimization_barrier((sent, wq_got))
    wq_in = share(wq_got)
    exchanged = lax.all_to_all(sent, "tp", 0, 0, tiled=True)
    part = own_parts(y, x_own, query_weight, ZN)
    x_n = shard_n // 4
    at_y, at_x, core = shard // (2 * x_n), shard // 2 % x_n, shard % 2
    offsets = [(0, 0), (-1, 0), (1, 0), (0, 1), (-1, 1), (1, 1), (2, 0), (2, 1)]
    ids = [(at_y + dy) % 2 * (2 * x_n) + (at_x + dx) % x_n * 2 for dx, dy in offsets]
    ids = jnp.stack([i + core for i in ids] + [i + 1 - core for i in ids])
    counts = jnp.sum((kept_rows < tokens).astype(jnp.int32), axis=1)
    info = packing(counts, shard, ids)
    wo_rows = out_weight.shape[0] // 2
    wo_sent = lax.dynamic_slice(out_weight, ((1 - y) * wo_rows + mine * chunk, 0), (chunk, width))
    exchanged, info, wo_sent, part, wq_in = lax.optimization_barrier((exchanged, info, wo_sent, part, wq_in))
    part = all_parts(x_in, wq_in, part)
    summed = jnp.sum(exchanged.astype(jnp.float32), axis=0)
    square_sum = summed[HD // 2] + summed[HD // 2 + 2]
    router_logit = summed[HD // 2 + 1] + summed[HD // 2 + 3]
    inverse_rms = lax.rsqrt(square_sum / D + EPSILON)
    piece = (summed[: HD // 2] * inverse_rms[None, :]).astype(bf16)
    piece, wo_sent, part = lax.optimization_barrier((piece, wo_sent, part))
    query_sum = lax.psum_scatter(
        part, "tp", scatter_dimension=0, axis_index_groups=[[2 * k + h for k in range(ZN)] for h in range(2)]
    )
    pieces = [lax.ppermute(piece, "tp", quad_shift(k)) for k in (1, 2, 3)]
    wo_got = lax.ppermute(wo_sent, "tp", y_swap())
    pieces, wo_got = lax.optimization_barrier(([piece] + pieces, wo_got))
    kv_own = ordered_rows(z % 4, pieces)


    def along(step):
        return [(c, c // (2 * x_n) * (2 * x_n) + (c + 2 * step) % (2 * x_n)) for c in range(shard_n)]

    def x_hop(block, step):
        return lax.ppermute(block, "ctx", along(step))

    middle = rows // 2
    over = lax.ppermute(kv_own, "ctx", [(c, (c + shard_n // 2) % shard_n) for c in range(shard_n)])
    near_left, near_right, over, wo_got = lax.optimization_barrier((x_hop(kv_own, 1), x_hop(kv_own, -1), over, wo_got))
    wo_in = share(wo_got).reshape(wo_rows, width)
    first_half = jnp.stack([kv_own, near_left, near_right, over])
    far = x_hop(near_left[:middle], 1), x_hop(near_right[middle:], -1)
    over_left, over_right = x_hop(over, 1), x_hop(over, -1)
    over_left, over_right, far = lax.optimization_barrier((over_left, over_right, far))
    over_far = x_hop(over_left[:middle], 1), x_hop(over_right[middle:], -1)
    second_half = jnp.stack([over_left, over_right, jnp.concatenate(far), jnp.concatenate(over_far)])

    def core_hop(block):
        return lax.ppermute(block, "ctx", [(c, c ^ 1) for c in range(shard_n)])

    kv_all = [first_half, second_half, core_hop(first_half), core_hop(second_half)]
    def right(a):
        return lax.ppermute(a.astype(bf16), "tp", z_shift(1))

    def left(a):
        return lax.ppermute(a.astype(bf16), "tp", z_shift(-1))

    def both(going_right, going_left):
        return lax.optimization_barrier((right(going_right), left(going_left)))

    cut = chunk // 2
    queries = (query_sum.astype(jnp.float32) * (inverse_rms * EXP_SCALE)[:, None]).astype(bf16)

    mixed = attention(info, queries, kv_all)

    pieces, starts = [mixed], [0]
    from_left, from_right = mixed, mixed
    for step in (1, 2, 3):
        from_left, from_right = both(from_left, from_right)
        pieces += [from_left, from_right]
        starts += [-step, step]
    pieces += [right(from_left[:, :cut]), left(from_right[:, cut:])]
    starts = [(z + offset) % ZN * chunk for offset in starts] + [(z + 4) % ZN * chunk + low for low in (0, cut)]
    for_partner = functools.reduce(
        jnp.add,
        [
            dot(piece, lax.dynamic_slice(wo_in, (start, 0), (piece.shape[1], width)))
            for piece, start in zip(pieces, starts)
        ],
    ).astype(bf16)
    received = lax.ppermute(for_partner, "tp", y_swap())
    pieces, for_partner = lax.optimization_barrier((pieces, for_partner))
    own_sum = project(jnp.stack(starts).astype(jnp.int32) + y * wo_rows, out_weight, pieces, jnp.float32)
    own_sum, received = lax.optimization_barrier((own_sum, received))
    projected = own_sum + received
    row_update = (jax.nn.sigmoid(router_logit)[:, None] * projected).astype(bf16)
    select = (own_rows.reshape(rows, 1) == jnp.arange(tokens, dtype=jnp.int32)[None, :]).astype(bf16)
    return lax.dot_general(select, row_update, (((0,), (0,)), ((), ())), preferred_element_type=jnp.float32).astype(
        bf16
    )


def solution(mesh):
    return jax.shard_map(
        shards,
        mesh=mesh,
        in_specs=(
            P("ctx", "tp"),
            P("tp"),
            P("tp"),
            P("tp", None),
            P(None, "tp", None),
            P(None, "tp"),
            P(),
        ),
        out_specs=P("ctx", "tp"),
        check_vma=False,
    )
```

```python
import functools

import jax
import jax.numpy as jnp
from jax import lax
from jax.experimental import pallas as pl
from jax.experimental.pallas import tpu as pltpu
from jax.sharding import PartitionSpec as P

D = 8192
H = 32
KVH = 4
HD = 128
ZN = 8
EPSILON = 1e-05
MASKED_SCORE = -1e30
EXP_SCALE = HD ** (-0.5) * 1.4426950408889634
KEY_BLOCK = 1024
ROW_TILE = 512
ATTENTION_VMEM = 32 * 1024 * 1024


def z_shift(dz):
    return [(z * 2 + y, ((z + dz) % ZN) * 2 + y) for z in range(ZN) for y in range(2)]


def y_swap():
    return [(t, t ^ 1) for t in range(2 * ZN)]


def quad_shift(k):
    def target(z):
        return (z // 4) * 4 + (z % 4 + k) % 4

    return [(z * 2 + y, target(z) * 2 + y) for z in range(ZN) for y in range(2)]


def attention_kernel(info_ref, q_ref, *refs):
    kv_refs, (o_ref, qa_ref, ka_ref, v_ref) = refs[:-4], refs[-4:]
    blocks_each, rows, _ = kv_refs[0].shape
    order = [(array, place) for array in range(len(kv_refs)) for place in range(blocks_each)]
    order = order[1:] + order[:1]
    count = info_ref[len(order) - 1, 1]
    first = pl.multiple_of(info_ref[len(order) - 1, 2], 16)

    for index, (array, place) in enumerate(order):

        @pl.when(info_ref[index, 0] > 0)
        def _():
            start = pl.multiple_of(info_ref[index, 2], 16)
            slot = lax.broadcasted_iota(jnp.int32, (rows, HD), 0)
            bias = jnp.where(slot < info_ref[index, 1], 0.0, MASKED_SCORE)
            ka_ref[pl.ds(start, rows), :HD] = kv_refs[array][place, :, :HD]
            ka_ref[pl.ds(start, rows), HD:] = bias.astype(jnp.bfloat16)
            v_ref[pl.ds(start, rows), :] = kv_refs[array][place, :, HD:]

    tail = pl.multiple_of(first + rows, 16)
    ka_ref[pl.ds(tail, KEY_BLOCK), :] = jnp.zeros((KEY_BLOCK, 2 * HD), jnp.bfloat16)
    v_ref[pl.ds(tail, KEY_BLOCK), :] = jnp.zeros((KEY_BLOCK, HD), jnp.bfloat16)
    one = (lax.broadcasted_iota(jnp.int32, (rows, HD), 1) == 0).astype(jnp.bfloat16)
    for head in range(2):
        qa_ref[head, :, :HD] = q_ref[:, head * HD : (head + 1) * HD]
        qa_ref[head, :, HD:] = one
    open_blocks = first // KEY_BLOCK
    blocks = (first + count + KEY_BLOCK - 1) // KEY_BLOCK

    def lane_tiles(array):
        return [array[:, i * HD : (i + 1) * HD] for i in range(KEY_BLOCK // HD)]

    def tile_work(tile):
        base = tile * ROW_TILE

        def scores(block, head, masked):
            start = pl.multiple_of(block * KEY_BLOCK, KEY_BLOCK)
            out = lax.dot_general(
                qa_ref[head, base : base + ROW_TILE, :],
                ka_ref[pl.ds(start, KEY_BLOCK), :],
                (((1,), (1,)), ((), ())),
                preferred_element_type=jnp.float32,
            )
            if masked:
                key = lax.broadcasted_iota(jnp.int32, out.shape, 1)
                query = lax.broadcasted_iota(jnp.int32, out.shape, 0)
                out = jnp.where(key - query <= first + base - start, out, MASKED_SCORE)
            return out

        def body(masked):
            def run(block, state):
                start = pl.multiple_of(block * KEY_BLOCK, KEY_BLOCK)
                new = []
                for head in range(2):
                    peak, total, acc = state[3 * head : 3 * head + 3]
                    score = scores(block, head, masked)
                    lanes = functools.reduce(jnp.maximum, lane_tiles(score))
                    new_peak = jnp.maximum(peak, jnp.max(lanes, axis=1, keepdims=True))
                    weights = jnp.exp2(score - new_peak)
                    rescale = jnp.exp2(peak - new_peak)
                    new.append(new_peak)
                    new.append(functools.reduce(jnp.add, lane_tiles(weights), total * rescale))
                    new.append(
                        acc * rescale
                        + jnp.dot(
                            weights.astype(jnp.bfloat16),
                            v_ref[pl.ds(start, KEY_BLOCK), :],
                            preferred_element_type=jnp.float32,
                        )
                    )
                return tuple(new)

            return run

        zero = jnp.zeros((ROW_TILE, HD), jnp.float32)
        state = (jnp.full((ROW_TILE, 1), MASKED_SCORE, jnp.float32), zero, zero) * 2
        state = lax.fori_loop(0, open_blocks, body(False), state)
        state = lax.fori_loop(open_blocks, blocks, body(True), state)
        for head in range(2):
            total = jnp.sum(state[3 * head + 1], axis=1, keepdims=True)
            o_ref[base : base + ROW_TILE, head * HD : (head + 1) * HD] = (state[3 * head + 2] / total).astype(
                jnp.bfloat16
            )

    for tile in range(rows // ROW_TILE):
        if tile == 0:
            tile_work(tile)
        else:

            @pl.when(tile * ROW_TILE < count)
            def _():
                tile_work(tile)

            @pl.when(tile * ROW_TILE >= count)
            def _():
                o_ref[tile * ROW_TILE : (tile + 1) * ROW_TILE, :] = jnp.zeros((ROW_TILE, 2 * HD), jnp.bfloat16)


def packing(counts, own, ids):
    shards_n = ids.shape[0]
    ids = jnp.concatenate([ids[1:], ids[:1]])
    used = ids <= own
    held = jnp.sum(jnp.where(ids[:, None] == jnp.arange(shards_n)[None, :], counts[None, :], 0), axis=1)
    packed = jnp.where(used, (held + 15) // 16 * 16, 0)
    before = jnp.arange(shards_n)[None, :] < jnp.arange(shards_n)[:, None]
    first = jnp.sum(jnp.where(before, packed[None, :], 0), axis=1)
    return jnp.stack([used.astype(jnp.int32), held, first], axis=1).astype(jnp.int32)


def attention(info, queries, kv):
    blocks_each, rows, _ = kv[0].shape
    shards_n = blocks_each * len(kv)
    capacity = shards_n * (rows // 2 + 16) + rows + KEY_BLOCK
    return pl.pallas_call(
        attention_kernel,
        out_shape=jax.ShapeDtypeStruct(queries.shape, jnp.bfloat16),
        in_specs=[pl.BlockSpec(memory_space=pltpu.SMEM)]
        + [pl.BlockSpec(memory_space=pltpu.VMEM)] * (1 + len(kv)),
        out_specs=pl.BlockSpec(memory_space=pltpu.VMEM),
        scratch_shapes=[
            pltpu.VMEM((2, rows, 2 * HD), jnp.bfloat16),
            pltpu.VMEM((capacity, 2 * HD), jnp.bfloat16),
            pltpu.VMEM((capacity, HD), jnp.bfloat16),
        ],
        compiler_params=pltpu.CompilerParams(vmem_limit_bytes=ATTENTION_VMEM),
        cost_estimate=pl.CostEstimate(
            flops=4 * 2 * rows * HD * shards_n * rows,
            bytes_accessed=shards_n * rows * HD * 4,
            transcendentals=rows * rows * shards_n,
        ),
    )(info, queries, *kv)


def rows_kernel(rows_ref, hidden_ref, gain_ref, router_ref, kv_ref, x_ref, sent_ref):
    tokens, width = hidden_ref.shape
    rows = rows_ref.shape[1]
    token = lax.broadcasted_iota(jnp.int32, (tokens, rows), 0)
    select = jnp.where(token == rows_ref[...], 1.0, 0.0).astype(jnp.bfloat16)
    kept = lax.dot_general(select, hidden_ref[...], (((0,), (0,)), ((), ())), preferred_element_type=jnp.float32)
    normed = kept * gain_ref[...].astype(jnp.float32)
    x_ref[...] = normed.astype(jnp.bfloat16)

    def feature_sum(array):
        tiles = [array[:, i * HD : (i + 1) * HD] for i in range(width // HD)]
        return jnp.sum(functools.reduce(jnp.add, tiles).T, axis=0, keepdims=True)

    stats = jnp.concatenate([feature_sum(kept * kept), feature_sum(kept * router_ref[...].astype(jnp.float32))])
    high = stats.astype(jnp.bfloat16).astype(jnp.float32)
    stats = jnp.concatenate([high, stats - high, jnp.zeros((4, rows), jnp.float32)])
    turned = normed.T.astype(jnp.bfloat16)
    depth = sent_ref.shape[1] - stats.shape[0]
    halves = HD // depth
    for which in range(2):
        sums = lax.dot_general(
            kv_ref[which], turned, (((0,), (0,)), ((), ())), preferred_element_type=jnp.float32
        )
        for group in range(KVH):
            for half in range(halves):
                start = group * HD + half * depth
                place = ((group % 2 * 2 + which) * halves + half) * 2 + group // 2
                sent_ref[place] = jnp.concatenate([sums[start : start + depth], stats]).astype(jnp.bfloat16)


def rows_and_sums(own_rows, hidden, norm_gain, router_weight, key_value_weight):
    rows, (_, width) = own_rows.shape[1], hidden.shape
    return pl.pallas_call(
        rows_kernel,
        out_shape=(
            jax.ShapeDtypeStruct((rows, width), jnp.bfloat16),
            jax.ShapeDtypeStruct((2 * ZN, HD // 2 + 8, rows), jnp.bfloat16),
        ),
        in_specs=[pl.BlockSpec(memory_space=pltpu.VMEM)] * 5,
        out_specs=(pl.BlockSpec(memory_space=pltpu.VMEM),) * 2,
        compiler_params=pltpu.CompilerParams(vmem_limit_bytes=24 * 1024 * 1024),
        cost_estimate=pl.CostEstimate(
            flops=4 * rows * width * hidden.shape[0], bytes_accessed=5 * 1024 * 1024, transcendentals=0
        ),
    )(own_rows, hidden, norm_gain.reshape(1, width), router_weight.reshape(1, width), key_value_weight)


def order_kernel(at_ref, *refs):
    pieces, o_ref, scratch_ref = refs[:4], refs[4], refs[5]
    depth = pieces[0].shape[0]
    for k in range(4):
        place = lax.rem(at_ref[0] - k + 4, 4)
        scratch_ref[pl.ds(pl.multiple_of(place * depth, depth), depth), :] = pieces[k][...].astype(jnp.float32)
    o_ref[...] = scratch_ref[...].T.astype(jnp.bfloat16)


def ordered_rows(at, pieces):
    depth, rows = pieces[0].shape
    return pl.pallas_call(
        order_kernel,
        out_shape=jax.ShapeDtypeStruct((rows, 4 * depth), jnp.bfloat16),
        in_specs=[pl.BlockSpec(memory_space=pltpu.SMEM)] + [pl.BlockSpec(memory_space=pltpu.VMEM)] * 4,
        out_specs=pl.BlockSpec(memory_space=pltpu.VMEM),
        scratch_shapes=[pltpu.VMEM((4 * depth, rows), jnp.float32)],
        cost_estimate=pl.CostEstimate(flops=0, bytes_accessed=16 * depth * rows, transcendentals=0),
    )(at[None].astype(jnp.int32), *pieces)


def dot(a, b):
    return jnp.dot(a, b, preferred_element_type=jnp.float32)


def own_kernel(y_ref, x_ref, w_ref, o_ref):
    o_ref[0] = dot(x_ref[...], w_ref[...]).astype(jnp.bfloat16)


def in_kernel(x_ref, w_ref, own_ref, o_ref):
    o_ref[0] = (dot(x_ref[...], w_ref[0]) + own_ref[0].astype(jnp.float32)).astype(jnp.bfloat16)


def own_parts(y, x_own, query_weight, chunks):
    rows, width = x_own.shape
    chunk = query_weight.shape[1] // 2 // chunks
    return pl.pallas_call(
        own_kernel,
        out_shape=jax.ShapeDtypeStruct((chunks, rows, chunk), jnp.bfloat16),
        grid_spec=pltpu.PrefetchScalarGridSpec(
            num_scalar_prefetch=1,
            grid=(chunks,),
            in_specs=[
                pl.BlockSpec((rows, width), lambda d, y: (0, 0)),
                pl.BlockSpec((width, chunk), lambda d, y: (0, y[0] * chunks + d)),
            ],
            out_specs=pl.BlockSpec((1, rows, chunk), lambda d, y: (d, 0, 0)),
        ),
        compiler_params=pltpu.CompilerParams(vmem_limit_bytes=16 * 1024 * 1024),
        cost_estimate=pl.CostEstimate(
            flops=2 * chunks * rows * width * chunk, bytes_accessed=chunks * chunk * 2 * (width + rows), transcendentals=0
        ),
    )(y[None].astype(jnp.int32), x_own, query_weight)


def all_parts(x_in, wq_in, own):
    chunks, rows, chunk = own.shape
    width = x_in.shape[1]
    return pl.pallas_call(
        in_kernel,
        out_shape=jax.ShapeDtypeStruct(own.shape, jnp.bfloat16),
        grid=(chunks,),
        in_specs=[
            pl.BlockSpec((rows, width), lambda d: (0, 0)),
            pl.BlockSpec((1, width, chunk), lambda d: (d, 0, 0)),
            pl.BlockSpec((1, rows, chunk), lambda d: (d, 0, 0)),
        ],
        out_specs=pl.BlockSpec((1, rows, chunk), lambda d: (d, 0, 0)),
        compiler_params=pltpu.CompilerParams(vmem_limit_bytes=16 * 1024 * 1024),
        cost_estimate=pl.CostEstimate(
            flops=2 * chunks * rows * width * chunk, bytes_accessed=chunks * chunk * 2 * (width + 2 * rows), transcendentals=0
        ),
    )(x_in, wq_in, own)


def project_kernel(starts_ref, w_hbm, *refs):
    pieces, (o_ref, x_ref, w_ref, sem) = refs[:-4], refs[-4:]
    copies, at = [], 0
    for index, piece in enumerate(pieces):
        depth = piece.shape[1]
        start = pl.multiple_of(starts_ref[index], HD)
        copies.append(
            pltpu.make_async_copy(w_hbm.at[pl.ds(start, depth), :], w_ref.at[pl.ds(at, depth), :], sem.at[index])
        )
        at += depth
    for copy in copies:
        copy.start()
    at = 0
    for piece in pieces:
        depth = piece.shape[1]
        x_ref[:, at : at + depth] = piece[...]
        at += depth
    for copy in copies:
        copy.wait()
    o_ref[...] = dot(x_ref[...], w_ref[...]).astype(o_ref.dtype)


def project(starts, weights, pieces, kind):
    rows = pieces[0].shape[0]
    depth = sum(piece.shape[1] for piece in pieces)
    width = weights.shape[1]
    return pl.pallas_call(
        project_kernel,
        out_shape=jax.ShapeDtypeStruct((rows, width), kind),
        in_specs=[pl.BlockSpec(memory_space=pltpu.SMEM), pl.BlockSpec(memory_space=pl.ANY)]
        + [pl.BlockSpec(memory_space=pltpu.VMEM)] * len(pieces),
        out_specs=pl.BlockSpec(memory_space=pltpu.VMEM),
        scratch_shapes=[
            pltpu.VMEM((rows, depth), jnp.bfloat16),
            pltpu.VMEM((depth, width), jnp.bfloat16),
            pltpu.SemaphoreType.DMA((len(pieces),)),
        ],
        compiler_params=pltpu.CompilerParams(vmem_limit_bytes=24 * 1024 * 1024),
        cost_estimate=pl.CostEstimate(
            flops=2 * rows * depth * width, bytes_accessed=2 * depth * (rows + width) + 4 * rows * width, transcendentals=0
        ),
    )(starts, weights, *pieces)


def shards(hidden, norm_gain, router_weight, query_weight, key_value_weight, out_weight, kept_rows):
    bf16 = jnp.bfloat16
    shard = lax.axis_index("ctx")
    tp = lax.axis_index("tp")
    shard_n = lax.axis_size("ctx")
    z, y = tp // 2, tp % 2
    tokens, width = hidden.shape
    rows = kept_rows.shape[1]
    half_cols = query_weight.shape[1] // 2
    chunk = half_cols // ZN

    group = 2 * ZN // 2
    groups = [list(range(g, g + group)) for g in range(0, shard_n, group)]
    mine = shard % group

    def share(got):
        return lax.all_gather(got, "ctx", axis=0, tiled=False, axis_index_groups=groups)

    wq_sent = lax.dynamic_slice(query_weight, (0, (1 - y) * half_cols + mine * chunk), (width, chunk))
    wq_got = lax.ppermute(wq_sent, "tp", y_swap())

    own_rows = lax.dynamic_slice_in_dim(kept_rows, shard, 1, 0)
    x_own, sent = rows_and_sums(own_rows, hidden, norm_gain, router_weight, key_value_weight)
    x_in = lax.ppermute(x_own, "tp", y_swap())

    sent, wq_got = lax.optimization_barrier((sent, wq_got))
    wq_in = share(wq_got)
    exchanged = lax.all_to_all(sent, "tp", 0, 0, tiled=True)
    part = own_parts(y, x_own, query_weight, ZN)
    x_n = shard_n // 4
    at_y, at_x, core = shard // (2 * x_n), shard // 2 % x_n, shard % 2
    offsets = [(0, 0), (-1, 0), (1, 0), (0, 1), (-1, 1), (1, 1), (2, 0), (2, 1)]
    ids = [(at_y + dy) % 2 * (2 * x_n) + (at_x + dx) % x_n * 2 for dx, dy in offsets]
    ids = jnp.stack([i + core for i in ids] + [i + 1 - core for i in ids])
    counts = jnp.sum((kept_rows < tokens).astype(jnp.int32), axis=1)
    info = packing(counts, shard, ids)
    wo_rows = out_weight.shape[0] // 2
    wo_sent = lax.dynamic_slice(out_weight, ((1 - y) * wo_rows + mine * chunk, 0), (chunk, width))
    exchanged, info, wo_sent, part, wq_in = lax.optimization_barrier((exchanged, info, wo_sent, part, wq_in))
    part = all_parts(x_in, wq_in, part)
    summed = jnp.sum(exchanged.astype(jnp.float32), axis=0)
    square_sum = summed[HD // 2] + summed[HD // 2 + 2]
    router_logit = summed[HD // 2 + 1] + summed[HD // 2 + 3]
    inverse_rms = lax.rsqrt(square_sum / D + EPSILON)
    piece = (summed[: HD // 2] * inverse_rms[None, :]).astype(bf16)
    piece, wo_sent, part = lax.optimization_barrier((piece, wo_sent, part))
    query_sum = lax.psum_scatter(
        part, "tp", scatter_dimension=0, axis_index_groups=[[2 * k + h for k in range(ZN)] for h in range(2)]
    )
    pieces = [lax.ppermute(piece, "tp", quad_shift(k)) for k in (1, 2, 3)]
    wo_got = lax.ppermute(wo_sent, "tp", y_swap())
    pieces, wo_got = lax.optimization_barrier(([piece] + pieces, wo_got))
    kv_own = ordered_rows(z % 4, pieces)


    def along(step):
        return [(c, c // (2 * x_n) * (2 * x_n) + (c + 2 * step) % (2 * x_n)) for c in range(shard_n)]

    def x_hop(block, step):
        return lax.ppermute(block, "ctx", along(step))

    middle = rows // 2
    over = lax.ppermute(kv_own, "ctx", [(c, (c + shard_n // 2) % shard_n) for c in range(shard_n)])
    near_left, near_right, over, wo_got = lax.optimization_barrier((x_hop(kv_own, 1), x_hop(kv_own, -1), over, wo_got))
    wo_in = share(wo_got).reshape(wo_rows, width)
    first_half = jnp.stack([kv_own, near_left, near_right, over])
    far = x_hop(near_left[:middle], 1), x_hop(near_right[middle:], -1)
    over_left, over_right = x_hop(over, 1), x_hop(over, -1)
    over_left, over_right, far = lax.optimization_barrier((over_left, over_right, far))
    over_far = x_hop(over_left[:middle], 1), x_hop(over_right[middle:], -1)
    second_half = jnp.stack([over_left, over_right, jnp.concatenate(far), jnp.concatenate(over_far)])

    def core_hop(block):
        return lax.ppermute(block, "ctx", [(c, c ^ 1) for c in range(shard_n)])

    kv_all = [first_half, second_half, core_hop(first_half), core_hop(second_half)]
    def right(a):
        return lax.ppermute(a.astype(bf16), "tp", z_shift(1))

    def left(a):
        return lax.ppermute(a.astype(bf16), "tp", z_shift(-1))

    def both(going_right, going_left):
        return lax.optimization_barrier((right(going_right), left(going_left)))

    cut = chunk // 2
    queries = (query_sum.astype(jnp.float32) * (inverse_rms * EXP_SCALE)[:, None]).astype(bf16)

    mixed = attention(info, queries, kv_all)

    pieces, starts = [mixed], [0]
    from_left, from_right = mixed, mixed
    for step in (1, 2, 3):
        from_left, from_right = both(from_left, from_right)
        if step == 2:
            from_left, from_right, wo_in = lax.optimization_barrier((from_left, from_right, wo_in))
        pieces += [from_left, from_right]
        starts += [-step, step]
    pieces += [right(from_left[:, :cut]), left(from_right[:, cut:])]
    starts = [(z + offset) % ZN * chunk for offset in starts] + [(z + 4) % ZN * chunk + low for low in (0, cut)]
    for_partner = functools.reduce(
        jnp.add,
        [
            dot(piece, lax.dynamic_slice(wo_in, (start, 0), (piece.shape[1], width)))
            for piece, start in zip(pieces, starts)
        ],
    ).astype(bf16)
    received = lax.ppermute(for_partner, "tp", y_swap())
    pieces, for_partner = lax.optimization_barrier((pieces, for_partner))
    own_sum = project(jnp.stack(starts).astype(jnp.int32) + y * wo_rows, out_weight, pieces, jnp.float32)
    own_sum, received = lax.optimization_barrier((own_sum, received))
    projected = own_sum + received
    row_update = (jax.nn.sigmoid(router_logit)[:, None] * projected).astype(bf16)
    select = (own_rows.reshape(rows, 1) == jnp.arange(tokens, dtype=jnp.int32)[None, :]).astype(bf16)
    return lax.dot_general(select, row_update, (((0,), (0,)), ((), ())), preferred_element_type=jnp.float32).astype(
        bf16
    )


def solution(mesh):
    return jax.shard_map(
        shards,
        mesh=mesh,
        in_specs=(
            P("ctx", "tp"),
            P("tp"),
            P("tp"),
            P("tp", None),
            P(None, "tp", None),
            P(None, "tp"),
            P(),
        ),
        out_specs=P("ctx", "tp"),
        check_vma=False,
    )
```
